256 devices in a mesh: bx: 4 (over x_hi, core), by: 32 (over y, z), ka: 2 (over x_lo).
Axes of the slice: x: 4 (x_hi: 2, x_lo: 2; x = x_hi * 2 + x_lo), y: 4, z: 8, core: 2. Of those that a mesh axis runs over, the one named last changes fastest.
Arguments:
- positions: float32 [3, 32768], P(None, ('bx', 'by', 'ka')), may hold values from 0 to 1024, as said below
- species: int32 [32768], P(('bx', 'by', 'ka')), may hold values from 0 to 5
- send_x: int32 [2, 8192], P(None, ('bx', 'by', 'ka')), may hold values from 0 to 127, as said below
- send_y: int32 [2, 12288], P(None, ('bx', 'by', 'ka')), may hold values from 0 to 191, as said below
- neighbours: int32 [24, 32768], P(None, ('bx', 'by', 'ka')), may hold values from 0 to 287, as said below
- live_slots: int32 [24, 32768], P(None, ('bx', 'by', 'ka')), may hold values from 0 to 1, as said below
- embedding: bfloat16 [128, 6], replicated, may hold values from -6 to 6
- radial_in: bfloat16 [2, 64, 8], replicated, may hold values from -2 to 2
- radial_mid: bfloat16 [2, 64, 64], replicated, may hold values from -0.75 to 0.75
- radial_out: bfloat16 [2, 384, 64], replicated, may hold values from -0.75 to 0.75
- mixing: bfloat16 [2, 128, 384], replicated, may hold values from -0.3125 to 0.3125
- read_first: float32 [128], replicated, may hold values from -0.5 to 0.5
- read_hidden: bfloat16 [16, 128], replicated, may hold values from -0.5 to 0.5
- read_last: float32 [16], replicated, may hold values from -1.5 to 1.5
- w_charge: bfloat16 [64, 128], replicated, may hold values from -0.5 to 0.5
- spectral: float32 [64, 1024], replicated, may hold values from 0.3 to 3
- wave_ids: int32 [3, 1024], replicated, may hold values from -7 to 8, as said below
Outputs:
- energies: float32 [32768], P(('bx', 'by', 'ka'))
- forces: float32 [3, 32768], P(None, ('bx', 'by', 'ka'))
The draws below stay inside these ranges and needn't reach their ends.
Inputs may be any that keep to these rules, and one draw needn't show every extreme that they name: `positions`: the atoms of device (bx, by, ka) lie in x from 16 bx to 16 bx + 16, y from 16 (by 2 + ka) to that plus 16, z from 0 to 16. `send_x`: row 0 lists every own atom within 4 of the device's lower face along x, row 1 every own atom within 4 of its upper face. `send_y`: indices into the device's own atoms followed by those received from the lower and then the upper device along bx; row 0 lists every such entry within 4 of the device's lower face along y, row 1 every one within 4 of its upper face. `neighbours`: indices into the device's atom table: own atoms, then those from the lower and upper device along bx, then those from the lower and upper device along by+ka; a live slot names a table atom within the cutoff of 4, never the atom itself, each at most once; live slots come first in each atom's list. `live_slots`: the share of live slots differs from device to device. The 1024 columns are distinct k-vectors of one half-space: wave_ids[2] runs from 1 to 8 and the other two rows from -7 to 7, so no two columns are equal or opposite.
All inputs are finite; a program needn't handle non-finite values.
Results may differ from the reference program's by a relative error of at most 0.006.
Values sent between devices are 32-bit elements; how exact they have to be, the bound alone decides.
No kernel may reach another device: no remote copies, remote signals or barrier semaphores. Data moves between devices by JAX's collectives and lax.ppermute only.
A program may use at most 128 MiB of HBM per device.

```python
import math
import jax
import jax.numpy as jnp
import numpy as np
from jax import lax

C = 128
RH = 64
NBASIS = 8
SPECIES = 6
READH = 16
KC = 64
K = 1024
NB = 24
LAYERS = 2
ATOM_DEV = 128
ATOMS = 32768
N_BX = 4
N_BY = 32
N_KA = 2


def lattice_layout(key):
    device_count = N_BX * N_BY * N_KA
    count_y = N_BY * N_KA
    per_col = ATOM_DEV // 16
    layer_key, site_key, order_key = jax.random.split(jax.random.fold_in(key, 101), 3)
    layers = jax.random.randint(layer_key, (device_count,), 8, 17)
    site_keys = jax.random.split(site_key, device_count * 16)
    site_scores = jax.vmap(lambda one_key: jax.random.permutation(one_key, 256))(site_keys)
    site_scores = site_scores.reshape(device_count, 16, 256).astype(jnp.int32)
    depth_of = jnp.arange(256, dtype=jnp.int32) // 16
    valid = (depth_of[None, None, :] < layers[:, None, None]).astype(jnp.int32)
    _, chosen = lax.top_k(site_scores + 256 * valid, per_col)
    chosen = chosen.astype(jnp.int32)
    column = jnp.arange(16, dtype=jnp.int32)[None, :, None]
    site_x = (4 * (column // 4) + chosen % 4).reshape(device_count, ATOM_DEV)
    site_y = (4 * (column % 4) + chosen // 4 % 4).reshape(device_count, ATOM_DEV)
    site_z = (chosen // 16).reshape(device_count, ATOM_DEV)
    order_keys = jax.random.split(order_key, device_count)
    order = jax.vmap(lambda one_key: jax.random.permutation(one_key, ATOM_DEV))(order_keys).astype(jnp.int32)
    counting = jnp.arange(ATOM_DEV, dtype=jnp.int32)
    inverse = jax.vmap(lambda row: jnp.zeros((ATOM_DEV,), jnp.int32).at[row].set(counting))(order)
    device_ids = jnp.arange(device_count, dtype=jnp.int32)
    cell_x = (device_ids // count_y)[:, None]
    cell_y = (device_ids % count_y)[:, None]
    glob_x = cell_x * 16 + jnp.take_along_axis(site_x, order, axis=1)
    glob_y = cell_y * 16 + jnp.take_along_axis(site_y, order, axis=1)
    glob_z = jnp.take_along_axis(site_z, order, axis=1)
    return (inverse, jnp.stack([glob_x, glob_y, glob_z]))


def send_lists(inverse):
    device_count = inverse.shape[0]
    per_col = ATOM_DEV // 16
    quarter = ATOM_DEV // 4
    send_x = jnp.stack([inverse[:, :quarter], inverse[:, ATOM_DEV - quarter:]])
    values = np.arange(ATOM_DEV)
    own_band = values // per_col % 4
    ghost_ids = np.arange(quarter)
    ghost_band = ghost_ids // per_col % 4
    rows = []
    for band in (0, 3):
        own_part = inverse[:, values[own_band == band]]
        picked = ghost_ids[ghost_band == band]
        extra = np.concatenate([ATOM_DEV + picked, ATOM_DEV + quarter + picked]).astype(np.int32)
        extra_rows = jnp.broadcast_to(jnp.asarray(extra)[None], (device_count, extra.shape[0]))
        rows.append(jnp.concatenate([own_part, extra_rows], 1))
    return (send_x, jnp.stack(rows))


def neighbour_lists(key):
    inverse, glob = lattice_layout(key)
    send_x, send_y = send_lists(inverse)
    count_y = N_BY * N_KA
    device_count = N_BX * count_y
    grid_x = send_x.reshape(2, N_BX, count_y, -1)
    grid_y = send_y.reshape(2, N_BX, count_y, -1)

    def pick_rows(local_rows, index_rows):
        widened = jnp.broadcast_to(index_rows[None], (local_rows.shape[0],) + index_rows.shape)
        return jnp.take_along_axis(local_rows, widened, axis=3)
    local_rows = glob.reshape(3, N_BX, count_y, ATOM_DEV)
    extended = jnp.concatenate([local_rows, jnp.roll(pick_rows(local_rows, grid_x[1]), 1, axis=1), jnp.roll(pick_rows(local_rows, grid_x[0]), -1, axis=1)], axis=3)
    widened = jnp.concatenate([extended, jnp.roll(pick_rows(extended, grid_y[1]), 1, axis=2), jnp.roll(pick_rows(extended, grid_y[0]), -1, axis=2)], axis=3)
    tables = jnp.moveaxis(widened.reshape(3, device_count, -1), 1, 0)
    table_count = tables.shape[2]
    owns = jnp.moveaxis(glob, 1, 0)
    box_x = 16 * N_BX
    box_y = 16 * count_y
    tie_keys = jax.random.split(jax.random.fold_in(key, 202), device_count)
    table_ids = jnp.arange(table_count, dtype=jnp.int32)
    atom_ids = jnp.arange(ATOM_DEV, dtype=jnp.int32)
    top_base = 1025 * table_count

    def per_device(item):
        own_rows, table_rows, tie_key = item
        step_x = (table_rows[0][None, :] - own_rows[0][:, None] + box_x // 2) % box_x - box_x // 2
        step_y = (table_rows[1][None, :] - own_rows[1][:, None] + box_y // 2) % box_y - box_y // 2
        step_z = table_rows[2][None, :] - own_rows[2][:, None]
        square = step_x * step_x + step_y * step_y + step_z * step_z
        near = (square <= 9) & (table_ids[None, :] != atom_ids[:, None])
        ties = jax.random.randint(tie_key, (ATOM_DEV, table_count), 0, 1024)
        score = ties * table_count + table_ids[None, :] + near.astype(jnp.int32) * top_base
        best, picked = lax.top_k(score, NB)
        return (picked.astype(jnp.int32), (best >= top_base).astype(jnp.int32))
    picked, live = lax.map(per_device, (owns, tables, tie_keys))
    picked = jnp.moveaxis(picked, 2, 0).reshape(NB, device_count * ATOM_DEV)
    live = jnp.moveaxis(live, 2, 0).reshape(NB, device_count * ATOM_DEV)
    return (picked, live)


def draw_positions(key, part):
    inverse, glob = lattice_layout(key)
    key = jax.random.fold_in(key, 11)
    jitter = 0.5 * jax.random.uniform(key, (3, ATOMS), jnp.float32)
    return (glob.reshape(3, ATOMS).astype(jnp.float32) + jitter).astype(jnp.float32)


def draw_send_x(key, part):
    inverse, glob = lattice_layout(key)
    send_x, send_y = send_lists(inverse)
    return send_x.reshape(2, -1)


def draw_send_y(key, part):
    inverse, glob = lattice_layout(key)
    send_x, send_y = send_lists(inverse)
    return send_y.reshape(2, -1)


def draw_neighbours(key, part):
    picked, live = neighbour_lists(key)
    return picked


def draw_live_slots(key, part):
    picked, live = neighbour_lists(key)
    return live


def draw_wave_ids(key, part):
    key = jax.random.fold_in(key, 29)
    score_key, shuffle_key = jax.random.split(key)
    candidates = 15 * 15 * 8
    cand_scores = jax.random.permutation(score_key, candidates).astype(jnp.int32)
    cand_ids = jnp.arange(candidates, dtype=jnp.int32)
    corner = ((cand_ids == 14) | (cand_ids == 1785)).astype(jnp.int32)
    _, picked = lax.top_k(cand_scores + candidates * corner, K)
    picked = picked.astype(jnp.int32)
    shuffle = jax.random.permutation(shuffle_key, K).astype(jnp.int32)
    picked = jnp.take(picked, shuffle)
    return jnp.stack([picked % 15 - 7, picked // 15 % 15 - 7, picked // 225 + 1]).astype(jnp.int32)


def place_ends(entries, key, low, top_value):
    longest = entries.shape.index(max(entries.shape))
    spots = []
    for shift in (0, 1):
        where = [jax.random.randint(jax.random.fold_in(key, axis), (), 0, length) for axis, length in enumerate(entries.shape)]
        where[longest] = (where[longest] + shift) % entries.shape[longest]
        spots.append(tuple(where))
    return entries.at[spots[0]].set(low).at[spots[1]].set(top_value)


def scatter_about(stream_key, dims, scale, limit, held_as=jnp.bfloat16):
    values = jax.random.normal(stream_key, dims, jnp.float32) * scale
    return jnp.minimum(jnp.maximum(values, -limit), limit).astype(held_as)


def setup_inputs(seed: int = 0) -> dict:
    key_list = jax.random.split(jax.random.key(seed), 18)
    positions = draw_positions(jax.random.fold_in(key_list[17], 71), 0)
    species = place_ends(jax.random.randint(key_list[1], (ATOMS,), 0, SPECIES), jax.random.fold_in(key_list[1], 1), 0, SPECIES - 1).astype(jnp.int32)
    send_x = draw_send_x(jax.random.fold_in(key_list[17], 71), 0)
    send_y = draw_send_y(jax.random.fold_in(key_list[17], 71), 0)
    neighbours = draw_neighbours(jax.random.fold_in(key_list[17], 71), 0)
    live_slots = draw_live_slots(jax.random.fold_in(key_list[17], 71), 0)
    embedding = scatter_about(key_list[6], (C, SPECIES), 1.0, 6.0)
    radial_in = scatter_about(key_list[7], (LAYERS, RH, NBASIS), NBASIS ** -0.5, 2.0)
    radial_mid = scatter_about(key_list[8], (LAYERS, RH, RH), RH ** -0.5, 0.75)
    radial_out = scatter_about(key_list[9], (LAYERS, 3 * C, RH), RH ** -0.5, 0.75)
    mixing = scatter_about(key_list[10], (LAYERS, C, 3 * C), (3 * C) ** -0.5, 0.3125)
    read_first = scatter_about(key_list[11], (C,), C ** -0.5, 0.5, jnp.float32)
    read_hidden = scatter_about(key_list[12], (READH, C), C ** -0.5, 0.5)
    read_last = scatter_about(key_list[13], (READH,), READH ** -0.5, 1.5, jnp.float32)
    w_charge = scatter_about(key_list[14], (KC, C), C ** -0.5, 0.5)
    spectral = jnp.clip(jnp.exp(jax.random.uniform(key_list[15], (KC, K), jnp.float32, math.log(0.3), math.log(3.0))), 0.3, 3.0)
    wave_ids = draw_wave_ids(jax.random.fold_in(key_list[17], 71), 0)
    return {"positions": positions, "species": species, "send_x": send_x, "send_y": send_y, "neighbours": neighbours, "live_slots": live_slots, "embedding": embedding, "radial_in": radial_in, "radial_mid": radial_mid, "radial_out": radial_out, "mixing": mixing, "read_first": read_first, "read_hidden": read_hidden, "read_last": read_last, "w_charge": w_charge, "spectral": spectral, "wave_ids": wave_ids}


CUTOFF = 4.0
SOFTEN = 0.25
WIDTH_X = 16.0
WIDTH_Y = 16.0
DEPTH_Z = 16.0
ACT_GAIN = 1.679
ROOT_THREE = math.sqrt(3.0)
HIGHEST_PRECISION = lax.Precision.HIGHEST

def activate(inputs):
    return ACT_GAIN * jax.nn.silu(inputs)

def edge_geometry(pos_table, neighbours, live_slots, box_x, box_y):
    atom_count = neighbours.shape[1]
    centre = pos_table[:, :atom_count]
    others = jnp.take(pos_table, neighbours, axis=1)
    offsets = others - centre[:, None, :]
    step_x = offsets[0] - box_x * jnp.floor(offsets[0] / box_x + 0.5)
    step_y = offsets[1] - box_y * jnp.floor(offsets[1] / box_y + 0.5)
    step_z = offsets[2]
    square = step_x * step_x + step_y * step_y + step_z * step_z
    distance = jnp.sqrt(square + SOFTEN)
    envelope = jnp.square(jnp.maximum(1.0 - square / (CUTOFF * CUTOFF), 0.0)) * live_slots.astype(jnp.float32)
    unit_x = step_x / CUTOFF
    unit_y = step_y / CUTOFF
    unit_z = step_z / CUTOFF
    harmonics = jnp.stack([jnp.ones_like(unit_x), unit_x, unit_y, unit_z, unit_x * unit_y, unit_y * unit_z, unit_z * unit_x, unit_x * unit_x - unit_y * unit_y, (2.0 * unit_z * unit_z - unit_x * unit_x - unit_y * unit_y) / ROOT_THREE])
    return (distance, envelope, harmonics)

def interaction(radial_in, radial_mid, radial_out, mixing, pos_table, feat_table, neighbours, live_slots, box_x, box_y):
    slot_count, atom_count = neighbours.shape
    distance, envelope, harmonics = edge_geometry(pos_table, neighbours, live_slots, box_x, box_y)
    basis_count = radial_in.shape[1]
    spacing = CUTOFF / (basis_count - 1)
    centres = jnp.arange(basis_count, dtype=jnp.float32) * spacing
    basis_rows = jnp.exp(-jnp.square((distance[None] - centres[:, None, None]) / spacing))
    basis_rows = basis_rows.reshape(basis_count, slot_count * atom_count).astype(jnp.bfloat16)
    first_hidden = activate(jnp.dot(radial_in, basis_rows, preferred_element_type=jnp.float32)).astype(jnp.bfloat16)
    second_hidden = activate(jnp.dot(radial_mid, first_hidden, preferred_element_type=jnp.float32)).astype(jnp.bfloat16)
    radial = jnp.dot(radial_out, second_hidden, preferred_element_type=jnp.float32)
    channels = mixing.shape[0]
    radial = radial.reshape(3, channels, slot_count, atom_count) * envelope[None, None]
    source = jnp.take(feat_table, neighbours, axis=1)
    scalar = jnp.einsum('cni,cni,ni->ci', radial[0], source, harmonics[0], precision=HIGHEST_PRECISION)
    vector = jnp.einsum('cni,cni,mni->mci', radial[1], source, harmonics[1:4], precision=HIGHEST_PRECISION)
    tensor = jnp.einsum('cni,cni,mni->mci', radial[2], source, harmonics[4:9], precision=HIGHEST_PRECISION)
    invariants = jnp.concatenate([scalar, lax.optimization_barrier(jnp.sum(vector * vector, 0)), lax.optimization_barrier(jnp.sum(tensor * tensor, 0))], 0).astype(jnp.bfloat16)
    return feat_table[:, :atom_count] + jnp.dot(mixing, invariants, preferred_element_type=jnp.float32)

def readout(h_one, h_two, read_first, read_hidden, read_last, w_charge):
    rounded = h_two.astype(jnp.bfloat16)
    hidden = activate(jnp.dot(read_hidden, rounded, preferred_element_type=jnp.float32))
    site_local = lax.optimization_barrier(jnp.sum(read_first[:, None] * h_one, 0)) + lax.optimization_barrier(jnp.sum(read_last[:, None] * hidden, 0))
    charge = jnp.dot(w_charge, rounded, preferred_element_type=jnp.float32)
    return (site_local, charge)

def structure(positions, charge, wave_ids, box_x, box_y):
    wave = wave_ids.astype(jnp.float32) * (2.0 * math.pi)
    phase = wave[0][:, None] * (positions[0] / box_x)[None] + wave[1][:, None] * (positions[1] / box_y)[None] + wave[2][:, None] * (positions[2] / DEPTH_Z)[None]
    cosine_sum = jnp.einsum('cm,km->ck', charge, jnp.cos(phase), precision=HIGHEST_PRECISION)
    sine_sum = jnp.einsum('cm,km->ck', charge, jnp.sin(phase), precision=HIGHEST_PRECISION)
    return (cosine_sum, sine_sum)

def reference(positions, species, send_x, send_y, neighbours, live_slots, embedding, radial_in, radial_mid, radial_out, mixing, read_first, read_hidden, read_last, w_charge, spectral, wave_ids):
    count_y = N_BY * N_KA
    device_count = N_BX * count_y
    box_x = N_BX * WIDTH_X
    box_y = count_y * WIDTH_Y
    grid_x = send_x.reshape(2, N_BX, count_y, -1)
    grid_y = send_y.reshape(2, N_BX, count_y, -1)

    def pick_rows(local_rows, index_rows):
        widened = jnp.broadcast_to(index_rows[None], (local_rows.shape[0],) + index_rows.shape)
        return jnp.take_along_axis(local_rows, widened, axis=3)

    def table_of(values):
        local_rows = values.reshape(values.shape[0], N_BX, count_y, ATOM_DEV)
        extended = jnp.concatenate([local_rows, jnp.roll(pick_rows(local_rows, grid_x[1]), 1, axis=1), jnp.roll(pick_rows(local_rows, grid_x[0]), -1, axis=1)], axis=3)
        widened = jnp.concatenate([extended, jnp.roll(pick_rows(extended, grid_y[1]), 1, axis=2), jnp.roll(pick_rows(extended, grid_y[0]), -1, axis=2)], axis=3)
        return jnp.moveaxis(widened.reshape(values.shape[0], device_count, -1), 1, 0)
    neighbour_rows = jnp.moveaxis(neighbours.reshape(NB, device_count, ATOM_DEV), 1, 0)
    slot_rows = jnp.moveaxis(live_slots.reshape(NB, device_count, ATOM_DEV), 1, 0)
    h_zero = jnp.take(embedding, species, axis=1).astype(jnp.float32)

    def layer(layer_index, pos_tables, feat_tables):

        def per_device(device_item):
            pos_rows, feat_rows, index_rows, mask_rows = device_item
            return interaction(radial_in[layer_index], radial_mid[layer_index], radial_out[layer_index], mixing[layer_index], pos_rows, feat_rows, index_rows, mask_rows, box_x, box_y)
        result = lax.map(jax.checkpoint(per_device), (pos_tables, feat_tables, neighbour_rows, slot_rows))
        return jnp.moveaxis(result, 0, 1).reshape(result.shape[1], ATOMS)

    def model_parts(coords):
        pos_tables = table_of(coords)
        h_one = layer(0, pos_tables, table_of(h_zero))
        h_two = layer(1, pos_tables, table_of(h_one))
        return readout(h_one, h_two, read_first, read_hidden, read_last, w_charge)
    spectral_scale = 1.0 / math.sqrt(K * ATOMS)
    block_size = math.gcd(K, 64)

    def ewald(coords, charge):
        wave_blocks = jnp.moveaxis(wave_ids.reshape(3, K // block_size, block_size), 1, 0)
        filter_blocks = jnp.moveaxis(spectral.reshape(KC, K // block_size, block_size), 1, 0)

        def per_block(block_item):
            wave_rows, filter_rows = block_item
            cosine_sum, sine_sum = structure(coords, charge, wave_rows, box_x, box_y)
            return jnp.sum(filter_rows * (cosine_sum * cosine_sum + sine_sum * sine_sum))
        return 0.5 * spectral_scale * jnp.sum(lax.map(jax.checkpoint(per_block), (wave_blocks, filter_blocks)))

    def total_energy(coords):
        site_local, charge = model_parts(coords)
        return jnp.sum(site_local) + ewald(coords, charge)
    gradient = jax.grad(total_energy)(positions)
    site_local, charge = model_parts(positions)
    potential = jax.grad(ewald, argnums=1)(positions, charge)
    energies = site_local + 0.5 * lax.optimization_barrier(jnp.sum(charge * potential, 0))
    return (energies, -gradient)
```

```python
import functools
import math

import jax
import jax.numpy as jnp
from jax import lax
from jax.experimental import pallas as pl
from jax.experimental.pallas import tpu as pltpu
from jax.sharding import Mesh, PartitionSpec as P

CUTOFF = 4.0
SOFTEN = 0.25
WIDTH_X = 16.0
WIDTH_Y = 16.0
DEPTH_Z = 16.0
ACT_GAIN = 1.679
ROOT_THREE = math.sqrt(3.0)
HIGHEST = lax.Precision.HIGHEST
F32 = jnp.float32
BF16 = jnp.bfloat16

C = 128
NB = 24
ATOMS = 128
EDGES = NB * ATOMS
TABLE = 384
NBASIS = 8
K = 1024
KC = 64
TILES = 2 * K // 128
AXES = ("xh", "co", "y", "z", "xl")
WIDE = ("xh", "co", "y", "xl")
NWIDE = 32

NN = (((1,), (0,)), ((), ()))
NT = (((1,), (1,)), ((), ()))
TN = (((0,), (0,)), ((), ()))


def dot(a, b, dims=NN, precision=None):
    return lax.dot_general(a, b, dims, precision=precision, preferred_element_type=F32)


def split(a):
    high = a.astype(BF16)
    return high, (a - high.astype(F32)).astype(BF16)


def dot3(a, b, dims=NN):
    a_hi, a_lo = split(a)
    b_hi, b_lo = split(b)
    return dot(a_hi, b_hi, dims) + (dot(a_lo, b_hi, dims) + dot(a_hi, b_lo, dims))


def gate(v):
    s = 0.5 + 0.5 * jnp.tanh(0.5 * v)
    return s, (ACT_GAIN * v) * s


def gate_slope(v, s):
    return ACT_GAIN * s * (1.0 + v * (1.0 - s))


def onehot_columns(index_row, count, dtype):
    rows = lax.broadcasted_iota(jnp.int32, (count, index_row.shape[1]), 0)
    return (rows == index_row).astype(F32).astype(dtype)


def merge(a, b, split_lane):
    lane = lax.broadcasted_iota(jnp.int32, a.shape, 1)
    return jnp.where(lane < split_lane, a, b)


def pick(values, index_row):
    return dot(values, onehot_columns(index_row, values.shape[1], F32), NN, HIGHEST)


def give_back(grads, index_row, count):
    return dot(grads, onehot_columns(index_row, count, F32), NT, HIGHEST)


def strip_x_kernel(rows_ref, ix_ref, out_ref):
    out_ref[...] = pick(rows_ref[...], ix_ref[...])


def strip_y_kernel(rows_ref, a_ref, b_ref, iy_ref, part_ref, out_ref):
    part = merge(a_ref[...], b_ref[...], 32)
    part_ref[...] = part
    out_ref[...] = pick(jnp.concatenate([rows_ref[...], part], 1), iy_ref[...])


def radial_tile(g, geo_ref, w1, w2, w3, r_ref, p_ref):
    spacing = CUTOFF / (NBASIS - 1)
    centre = lax.broadcasted_iota(jnp.int32, (NBASIS, 512), 0).astype(F32) * spacing

    def row(k):
        return jnp.concatenate([geo_ref[k, pl.ds(4 * g + j, 1), :] for j in range(4)], 1)

    d = row(3)
    gap = (d - centre) * (1.0 / spacing)
    basis = jnp.exp(-gap * gap)
    z1 = dot(w1, basis.astype(BF16))
    s1, h1 = gate(z1)
    z2 = dot(w2, h1.astype(BF16))
    s2, h2 = gate(z2)
    env = row(4)
    cols = pl.ds(pl.multiple_of(g * 512, 512), 512)
    r_ref[:, cols] = dot(w3, (h2 * env).astype(BF16)).astype(BF16)
    slope = basis * gap * (-2.0 / spacing)
    h1p = gate_slope(z1, s1) * dot(w1, slope.astype(BF16))
    h2p = gate_slope(z2, s2) * dot(w2, h1p.astype(BF16))
    p_ref[:, cols] = dot(w3, (h2p * row(6) + h2 * row(5)).astype(BF16)).astype(BF16)


def aggregate(r_ref, get_f, y_ref, a_ref):
    def body(cc, carry):
        r0 = pl.multiple_of(cc * 16, 16)
        acc = [jnp.zeros((16, 128), F32) for _ in range(9)]
        state = get_f(r0)
        for n in range(NB):
            cols = slice(n * 128, (n + 1) * 128)
            f = state(n)
            g0 = r_ref[pl.ds(r0, 16), cols].astype(F32) * f
            g1 = r_ref[pl.ds(128 + r0, 16), cols].astype(F32) * f
            g2 = r_ref[pl.ds(256 + r0, 16), cols].astype(F32) * f
            acc[0] = acc[0] + g0
            for m in range(3):
                acc[1 + m] = acc[1 + m] + g1 * y_ref[m, n : n + 1, :]
            for m in range(5):
                acc[4 + m] = acc[4 + m] + g2 * y_ref[3 + m, n : n + 1, :]
        for k in range(9):
            a_ref[k, pl.ds(r0, 16), :] = acc[k]
        return carry

    lax.fori_loop(0, 8, body, 0)


def invariants(a_ref):
    a1 = a_ref[1] * a_ref[1] + a_ref[2] * a_ref[2] + a_ref[3] * a_ref[3]
    a2 = a_ref[4] * a_ref[4] + a_ref[5] * a_ref[5] + a_ref[6] * a_ref[6]
    a2 = a2 + a_ref[7] * a_ref[7] + a_ref[8] * a_ref[8]
    return jnp.concatenate([a_ref[0].astype(BF16), a1.astype(BF16), a2.astype(BF16)], 0)


def take_lanes(tables, lane, group):
    got = [jnp.take_along_axis(t, lane, axis=1, mode="promise_in_bounds") for t in tables]
    return jnp.where(group == 0, got[0], jnp.where(group == 1, got[1], got[2]))


def first_kernel(
    box_x, box_y, rows_ref, part_ref, a_in, b_in, nb_ref, live_ref, ix_ref, emb_ref, w1_ref, w2_ref,
    w3_ref, mix_ref, geo_ref, y_ref, r_ref, p_ref, f_ref, a_ref, h_ref, strip_ref,
):
    own = rows_ref[...]
    tables = [own, part_ref[...], merge(a_in[...], b_in[...], 64)]
    nb = nb_ref[...]
    lane, group = nb & 127, nb >> 7

    def gathered(row):
        return jnp.concatenate(
            [
                take_lanes(
                    [jnp.broadcast_to(t[row : row + 1], (8, 128)) for t in tables],
                    lane[8 * b : 8 * b + 8],
                    group[8 * b : 8 * b + 8],
                )
                for b in range(NB // 8)
            ],
            0,
        )

    off_x = gathered(0) - own[0:1]
    off_y = gathered(1) - own[1:2]
    step_z = gathered(2) - own[2:3]
    step_x = off_x - box_x * jnp.floor(off_x * (1.0 / box_x) + 0.5)
    step_y = off_y - box_y * jnp.floor(off_y * (1.0 / box_y) + 0.5)
    square = step_x * step_x + step_y * step_y + step_z * step_z
    shifted = square + SOFTEN
    inverse = lax.rsqrt(shifted)
    live = live_ref[...].astype(F32)
    inside = jnp.maximum(1.0 - square * (1.0 / (CUTOFF * CUTOFF)), 0.0)
    env = inside * inside * live
    ux, uy, uz = step_x * (1.0 / CUTOFF), step_y * (1.0 / CUTOFF), step_z * (1.0 / CUTOFF)
    geo_ref[0] = ux
    geo_ref[1] = uy
    geo_ref[2] = uz
    geo_ref[3] = jnp.sqrt(shifted)
    geo_ref[4] = env
    geo_ref[5] = inside * live * (-2.0 / (CUTOFF * CUTOFF))
    geo_ref[6] = 0.5 * env * inverse
    y_ref[0] = ux
    y_ref[1] = uy
    y_ref[2] = uz
    y_ref[3] = ux * uy
    y_ref[4] = uy * uz
    y_ref[5] = uz * ux
    y_ref[6] = ux * ux - uy * uy
    y_ref[7] = (2.0 * uz * uz - ux * ux - uy * uy) * (1.0 / ROOT_THREE)

    species = gathered(3)
    emb = emb_ref[...]
    w1, w2, w3 = w1_ref[0], w2_ref[0], w3_ref[0]
    geo_ref[7] = species

    def tile(g, carry):
        radial_tile(g, geo_ref, w1, w2, w3, r_ref, p_ref)
        kinds = lax.broadcasted_iota(jnp.int32, (8, 512), 0).astype(F32)
        kind = jnp.concatenate([geo_ref[7, pl.ds(4 * g + j, 1), :] for j in range(4)], 1)
        cols = pl.ds(pl.multiple_of(g * 512, 512), 512)
        f_ref[:, cols] = dot(emb, (kinds == kind).astype(F32).astype(BF16)).astype(BF16)
        return carry

    lax.fori_loop(0, NB // 4, tile, 0)

    def get_f(r0):
        return lambda n: f_ref[pl.ds(r0, 16), n * 128 : (n + 1) * 128].astype(F32)

    aggregate(r_ref, get_f, y_ref, a_ref)
    kinds = lax.broadcasted_iota(jnp.int32, (8, 128), 0).astype(F32)
    h_zero = dot(emb, (kinds == own[3:4]).astype(F32).astype(BF16))
    h_one = h_zero + dot(mix_ref[0], invariants(a_ref))
    h_ref[...] = h_one
    strip_ref[...] = pick(h_one, ix_ref[...])


def radial_kernel(geo_ref, w1_ref, w2_ref, w3_ref, r_ref, p_ref):
    w1, w2, w3 = w1_ref[1], w2_ref[1], w3_ref[1]

    def tile(g, carry):
        radial_tile(g, geo_ref, w1, w2, w3, r_ref, p_ref)
        return carry

    lax.fori_loop(0, NB // 4, tile, 0)


def waves_kernel(box_x, box_y, rows_ref, wave_ref, cs_ref):
    own = rows_ref[...]
    x, y, z = own[0:1] * (1.0 / box_x), own[1:2] * (1.0 / box_y), own[2:3] * (1.0 / DEPTH_Z)
    x, y, z = x - jnp.floor(x), y - jnp.floor(y), z - jnp.floor(z)
    turns = jnp.concatenate([x, y, z, jnp.zeros((5, 128), F32)], 0)

    def tile(t, carry):
        cols = pl.ds(pl.multiple_of(t * 128, 128), 128)
        phase = dot(turns, wave_ref[:, cols], TN, HIGHEST)
        quarter = jnp.floor(4.0 * phase + 0.5)
        angle = (phase - 0.25 * quarter) * (2.0 * math.pi)
        sq = angle * angle
        sin = angle * (1.0 + sq * (-1.0 / 6 + sq * (1.0 / 120 + sq * (-1.0 / 5040 + sq * (1.0 / 362880)))))
        cos = 1.0 + sq * (-0.5 + sq * (1.0 / 24 + sq * (-1.0 / 720 + sq * (1.0 / 40320 - sq * (1.0 / 3628800)))))
        turn = quarter.astype(jnp.int32) & 3
        odd = (turn & 1) == 1
        c = jnp.where(odd, sin, cos)
        s = jnp.where(odd, cos, sin)
        c = jnp.where((turn == 1) | (turn == 2), -c, c)
        s = jnp.where(turn >= 2, -s, s)
        cs_ref[:, cols] = c
        cs_ref[:, pl.ds(pl.multiple_of(K + t * 128, 128), 128)] = s
        return carry

    lax.fori_loop(0, K // 128, tile, 0)


def feature_strip_kernel(h_ref, a_in, b_in, iy_ref, part_ref, out_ref):
    part = merge(a_in[...], b_in[...], 32)
    part_ref[...] = part
    out_ref[...] = pick(jnp.concatenate([h_ref[...], part], 1), iy_ref[...])


def second_kernel(
    h_ref, part_ref, a_in, b_in, nb_ref, y_ref, r_ref, cs_ref, mix_ref, read_hidden_ref,
    w_charge_ref, f_ref, a_ref, h2_ref, charge_ref, s_ref, ypart_ref,
):
    ypart_ref[...] = merge(a_in[...], b_in[...], 64)

    def get_f(r0):
        rows = pl.ds(r0, 16)
        tables = [h_ref[rows, :], part_ref[rows, :], ypart_ref[rows, :]]

        def state(n):
            nb = jnp.broadcast_to(nb_ref[n : n + 1, :], (16, 128))
            f = take_lanes(tables, nb & 127, nb >> 7)
            f_ref[rows, n * 128 : (n + 1) * 128] = f
            return f

        return state

    aggregate(r_ref, get_f, y_ref, a_ref)
    h_two = h_ref[...] + dot(mix_ref[1], invariants(a_ref))
    h2_ref[...] = h_two
    charge = dot(w_charge_ref[...], h_two.astype(BF16))
    charge_ref[...] = charge
    q_hi, q_lo = split(charge)
    q_both = jnp.concatenate([q_hi, q_lo], 0)
    for t in range(TILES // 2):
        c_hi, c_lo = split(cs_ref[:, t * 256 : (t + 1) * 256])
        both = dot(q_both, c_hi)
        part = both[:KC] + (both[KC:] + dot(q_hi, c_lo))
        s_ref[2 * t * KC : (2 * t + 1) * KC, :] = part[:, :128]
        s_ref[(2 * t + 1) * KC : (2 * t + 2) * KC, :] = part[:, 128:]


def backward(ga_ref, r_ref, p_ref, f_ref, y_ref, gf_ref, t_ref):
    def body(n, carry):
        cols = pl.ds(pl.multiple_of(n * 128, 128), 128)
        y = [y_ref[m, pl.ds(n, 1), :] for m in range(8)]
        acc = [jnp.zeros((16, 128), F32) for _ in range(9)]
        for cc in range(8):
            rows = slice(cc * 16, cc * 16 + 16)
            ga = [ga_ref[k, rows, :] for k in range(9)]
            f = f_ref[rows, cols].astype(F32)
            r = [r_ref[l * 128 + cc * 16 : l * 128 + cc * 16 + 16, cols].astype(F32) for l in range(3)]
            p = [p_ref[l * 128 + cc * 16 : l * 128 + cc * 16 + 16, cols].astype(F32) for l in range(3)]
            q1 = ga[1] * y[0] + ga[2] * y[1] + ga[3] * y[2]
            q2 = ga[4] * y[3] + ga[5] * y[4] + ga[6] * y[5] + ga[7] * y[6] + ga[8] * y[7]
            if gf_ref is not None:
                gf_ref[rows, cols] = (ga[0] * r[0] + q1 * r[1] + q2 * r[2]).astype(BF16)
            acc[0] = acc[0] + f * (ga[0] * p[0] + q1 * p[1] + q2 * p[2])
            g1, g2 = f * r[1], f * r[2]
            for m in range(3):
                acc[1 + m] = acc[1 + m] + g1 * ga[1 + m]
            for m in range(5):
                acc[4 + m] = acc[4 + m] + g2 * ga[4 + m]
        for k in range(9):
            t_ref[k, pl.ds(n, 1), :] = jnp.sum(acc[k], 0, keepdims=True)
        return carry

    lax.fori_loop(0, NB, body, 0)


def pull_invariants(g_inv, a_ref, ga_ref):
    ga_ref[0] = g_inv[:C]
    for k in range(1, 4):
        ga_ref[k] = 2.0 * a_ref[k] * g_inv[C : 2 * C]
    for k in range(4, 9):
        ga_ref[k] = 2.0 * a_ref[k] * g_inv[2 * C :]


def fill_onehot(nb_ref, oh_ref):
    for n in range(NB):
        oh_ref[:, n * 128 : (n + 1) * 128] = onehot_columns(nb_ref[n : n + 1, :], TABLE, BF16)


def ewald_kernel(
    box_x, box_y, scale, s_ref, spectral_ref, cs_ref, wave_ref, charge_ref, h_ref, h2_ref, a_ref, y_ref, r_ref, p_ref,
    f_ref, nb_ref, iy_ref, mix_ref, read_first_ref, read_hidden_ref, read_last_ref, w_charge_ref,
    energy_ref, gpos_ref, gown_ref, gpart_ref, gy_ref, t_ref, ga_ref, gf_ref, oh_ref,
):
    charge = charge_ref[...]
    q_t = charge.T
    qt_hi, qt_lo = split(q_t)
    potential = jnp.zeros((KC, ATOMS), F32)
    gpos = jnp.zeros((8, ATOMS), F32)
    for t in range(TILES // 2):
        cols = slice(t * 128, (t + 1) * 128)
        late = slice(K + t * 128, K + (t + 1) * 128)
        filt = spectral_ref[:, cols] * scale
        gc = filt * s_ref[t * KC : (t + 1) * KC, :]
        gs = filt * s_ref[(TILES // 2 + t) * KC : (TILES // 2 + t + 1) * KC, :]
        cos, sin = cs_ref[:, cols], cs_ref[:, late]
        potential = potential + dot3(gc, cos, NT) + dot3(gs, sin, NT)
        gphase = dot3(q_t, gs) * cos - dot3(q_t, gc) * sin
        gpos = gpos + dot3(wave_ref[:, cols], gphase, NT)
    gpos_ref[...] = jnp.concatenate(
        [
            gpos[0:1] * (2.0 * math.pi / box_x),
            gpos[1:2] * (2.0 * math.pi / box_y),
            gpos[2:3] * (2.0 * math.pi / DEPTH_Z),
            jnp.zeros((5, ATOMS), F32),
        ],
        0,
    )
    h_two = h2_ref[...].astype(BF16)
    z = dot(read_hidden_ref[...], h_two)
    s, hidden = gate(z)
    last = read_last_ref[...]
    site = jnp.sum(read_first_ref[...] * h_ref[...], 0, keepdims=True) + jnp.sum(last * hidden, 0, keepdims=True)
    energy_ref[...] = site + 0.5 * jnp.sum(charge * potential, 0, keepdims=True)
    g_hidden = (last * gate_slope(z, s)).astype(BF16)
    g_two = dot(w_charge_ref[...], potential.astype(BF16), TN) + dot(read_hidden_ref[...], g_hidden, TN)
    g_two = g_two.astype(BF16)
    g_inv = dot(mix_ref[1], g_two, TN).astype(BF16).astype(F32)
    pull_invariants(g_inv, a_ref, ga_ref)
    backward(ga_ref, r_ref, p_ref, f_ref, y_ref, gf_ref, t_ref)
    fill_onehot(nb_ref, oh_ref)
    grads = dot(gf_ref[...], oh_ref[...], NT)
    gown_ref[...] = grads[:, :128] + g_two.astype(F32) + read_first_ref[...]
    gpart_ref[...] = grads[:, 128:256]
    gy_ref[...] = grads[:, 256:]


def return_y_kernel(gown_ref, gpart_ref, a_in, b_in, iy_ref, own_ref, part_ref):
    back = give_back(merge(a_in[...], b_in[...], 64), iy_ref[...], 256)
    own_ref[...] = gown_ref[...] + back[:, :128]
    part_ref[...] = gpart_ref[...] + back[:, 128:]


def last_kernel(
    gown_ref, a_in, b_in, ix_ref, mix_ref, a_ref, r_ref, p_ref, f_ref, y_ref, t1_ref, geo_ref, nb_ref, gpos_ref,
    own_ref, part_ref, gy_ref, ga_ref, t_ref, oh_ref, rows_ref,
):
    g_one = gown_ref[...] + give_back(merge(a_in[...], b_in[...], 32), ix_ref[...], 128)
    g_inv = dot(mix_ref[0], g_one.astype(BF16), TN).astype(BF16).astype(F32)
    pull_invariants(g_inv, a_ref, ga_ref)
    backward(ga_ref, r_ref, p_ref, f_ref, y_ref, None, t_ref)
    t = [t_ref[k] + t1_ref[k] for k in range(9)]
    ux, uy, uz = geo_ref[0], geo_ref[1], geo_ref[2]
    root = 2.0 / ROOT_THREE
    gx = t[1] + t[4] * uy + t[6] * uz + ux * (2.0 * t[7] - root * t[8])
    gy = t[2] + t[4] * ux + t[5] * uz - uy * (2.0 * t[7] + root * t[8])
    gz = t[3] + t[5] * uy + t[6] * ux + (2.0 * root) * uz * t[8]
    steps = [g * (1.0 / CUTOFF) + (2.0 * CUTOFF) * u * t[0] for g, u in ((gx, ux), (gy, uy), (gz, uz))]
    rows_ref[...] = jnp.zeros(rows_ref.shape, F32)
    for k in range(3):
        high = steps[k].astype(BF16).astype(F32)
        low = steps[k] - high
        for n in range(NB):
            rows_ref[k : k + 1, n * 128 : (n + 1) * 128] = high[n : n + 1]
            rows_ref[8 + k : 9 + k, n * 128 : (n + 1) * 128] = low[n : n + 1]
    fill_onehot(nb_ref, oh_ref)
    both = dot(rows_ref[...].astype(BF16), oh_ref[...], NT)
    grads = both[:8] + both[8:]
    centre = jnp.concatenate([jnp.sum(g, 0, keepdims=True) for g in steps] + [jnp.zeros((5, 128), F32)], 0)
    own_ref[...] = grads[:, :128] - centre + gpos_ref[...]
    part_ref[...] = grads[:, 128:256]
    gy_ref[...] = grads[:, 256:]


def final_kernel(own_ref, a_in, b_in, ix_ref, out_ref):
    total = own_ref[...] + give_back(merge(a_in[...], b_in[...], 32), ix_ref[...], 128)
    out_ref[...] = -total[:3]


def sum_kernel(in_ref, out_ref):
    rows = out_ref.shape[0]
    total = in_ref[0:rows, :]
    for g in range(1, in_ref.shape[0] // rows):
        total = total + in_ref[g * rows : (g + 1) * rows, :]
    out_ref[...] = total


def call(kernel, outs, *operands, scratch=(), flops=0, moved=0):
    return pl.pallas_call(
        kernel,
        out_shape=[jax.ShapeDtypeStruct(s, d) for s, d in outs],
        scratch_shapes=[pltpu.VMEM(s, d) for s, d in scratch],
        compiler_params=pltpu.CompilerParams(vmem_limit_bytes=48 * 1024 * 1024),
        cost_estimate=pl.CostEstimate(flops=flops, bytes_accessed=moved, transcendentals=0),
    )(*operands)


def swap(value, axes, of):
    count = 1
    for axis in axes:
        count *= lax.axis_size(axis)
    return lax.ppermute(value, axes, [(i, of(i)) for i in range(count)])


BX = ("xh", "co")
CELL = ("y", "z", "xl")


def swap_x(rows):
    return swap(rows, BX, lambda i: i ^ 1), swap(rows, BX, lambda i: i ^ 3)


def swap_y(rows):
    def other(c):
        return (c - 1) % 64 if c % 2 == 0 else (c + 1) % 64

    return swap(rows, CELL, lambda c: c ^ 1), swap(rows, CELL, other)


def reduce_all(partial):
    rows = partial.shape[0] // NWIDE
    pieces = lax.all_to_all(partial, WIDE, 0, 0, tiled=True)
    (mine,) = call(sum_kernel, [((rows, 128), F32)], pieces)
    for mask in (1, 2, 4):
        mine = mine + swap(mine, ("z",), lambda i, mask=mask: i ^ mask)
    spread = jnp.broadcast_to(mine[None], (NWIDE, rows, 128)).reshape(NWIDE * rows, 128)
    return lax.all_to_all(spread, WIDE, 0, 0, tiled=True)


def body(
    positions, species, send_x, send_y, neighbours, live_slots, embedding, radial_in, radial_mid, radial_out, mixing,
    read_first, read_hidden, read_last, w_charge, spectral, wave_ids,
):
    count_x = lax.axis_size("xh") * lax.axis_size("co")
    count_y = lax.axis_size("y") * lax.axis_size("z") * lax.axis_size("xl")
    box_x = count_x * WIDTH_X
    box_y = count_y * WIDTH_Y
    scale = 1.0 / math.sqrt(K * ATOMS * count_x * count_y)
    px = lax.axis_index("co")
    py = lax.axis_index("xl")
    lower_x, upper_x = 160 - 32 * px, 128 + 32 * px
    lower_y, upper_y = 320 - 64 * py, 256 + 64 * py

    def place(index):
        far = jnp.where(index < 240, index - 192 + lower_y, index - 240 + upper_y)
        near = jnp.where(index < 160, index - 128 + lower_x, index - 160 + upper_x)
        return jnp.where(index < 128, index, jnp.where(index < 192, near, far))

    nb = place(neighbours)
    odd_x, odd_y = px == 1, py == 1
    none = jnp.full((64,), -1, jnp.int32)
    ix = jnp.concatenate(
        [jnp.where(odd_x, send_x[0], send_x[1]), jnp.where(odd_x, send_x[1], send_x[0]), none]
    )[None]
    sy = place(send_y)
    iy = jnp.concatenate(
        [jnp.where(odd_y, sy[0], sy[1]), none[:16], jnp.where(odd_y, sy[1], sy[0]), none[:16]]
    )[None]
    rows = jnp.concatenate([positions, species.astype(F32)[None], jnp.zeros((4, ATOMS), F32)], 0)
    wave = jnp.concatenate([wave_ids.astype(F32), jnp.zeros((5, K), F32)], 0)
    emb = jnp.pad(embedding, ((0, 0), (0, 8 - embedding.shape[1])))
    small = ((8, 128), F32)
    square = ((C, 128), F32)
    edge3 = ((3 * C, EDGES), BF16)

    (strip,) = call(strip_x_kernel, [small], rows, ix)
    xa, xb = swap_x(strip)
    part, strip = call(strip_y_kernel, [small, small], rows, xa, xb, iy)
    ya, yb = swap_y(strip)
    (cs,) = call(
        functools.partial(waves_kernel, box_x, box_y), [((ATOMS, 2 * K), F32)], rows, wave, flops=10**8, moved=10**6
    )
    geo, ylm, r_zero, p_zero, f_zero, a_zero, h_one, strip = call(
        functools.partial(first_kernel, box_x, box_y),
        [((8, NB, 128), F32), ((8, NB, 128), F32), edge3, edge3, ((C, EDGES), BF16), ((9, C, 128), F32), square, square],
        rows, part, ya, yb, nb, live_slots, ix, emb, radial_in, radial_mid, radial_out, mixing,
    )
    xa, xb = swap_x(strip)
    r_one, p_one = call(radial_kernel, [edge3, edge3], geo, radial_in, radial_mid, radial_out, flops=10**9, moved=10**7)
    fpart, strip = call(feature_strip_kernel, [square, square], h_one, xa, xb, iy)
    ya, yb = swap_y(strip)
    f_one, a_one, h_two, charge, s_part = call(
        second_kernel,
        [((C, EDGES), F32), ((9, C, 128), F32), square, ((KC, ATOMS), F32), ((TILES * KC, 128), F32)],
        h_one, fpart, ya, yb, nb, ylm, r_one, cs, mixing, read_hidden, w_charge,
        scratch=[square],
    )
    s_all = reduce_all(s_part)
    energy, gpos, gown, gpart, gy, t_one = call(
        functools.partial(ewald_kernel, box_x, box_y, scale),
        [((1, 128), F32), small, square, square, square, ((9, NB, 128), F32)],
        s_all, spectral, cs, wave, charge, h_one, h_two, a_one, ylm, r_one, p_one, f_one, nb, iy, mixing,
        read_first[:, None], read_hidden, read_last[:, None], w_charge,
        scratch=[((9, C, 128), F32), ((C, EDGES), BF16), ((TABLE, EDGES), BF16)],
    )
    ya, yb = swap_y(gy)
    gown, gpart = call(return_y_kernel, [square, square], gown, gpart, ya, yb, iy)
    xa, xb = swap_x(gpart)
    own, part, gy = call(
        last_kernel,
        [small, small, small],
        gown, xa, xb, ix, mixing, a_zero, r_zero, p_zero, f_zero, ylm, t_one, geo, nb, gpos,
        scratch=[((9, C, 128), F32), ((9, NB, 128), F32), ((TABLE, EDGES), BF16), ((16, EDGES), F32)],
    )
    ya, yb = swap_y(gy)
    own, part = call(return_y_kernel, [small, small], own, part, ya, yb, iy)
    xa, xb = swap_x(part)
    (forces,) = call(final_kernel, [((3, ATOMS), F32)], own, xa, xb, ix)
    return energy[0], forces


def solution(mesh):
    fine = Mesh(mesh.devices.reshape(2, 2, 4, 8, 2), AXES)
    rows, columns = P(AXES), P(None, AXES)
    placed = (columns, rows) + (columns,) * 4 + (P(),) * 11
    return jax.shard_map(body, mesh=fine, in_specs=placed, out_specs=(rows, columns), check_vma=False)
```

```python
import functools
import math

import jax
import jax.numpy as jnp
from jax import lax
from jax.experimental import pallas as pl
from jax.experimental.pallas import tpu as pltpu
from jax.sharding import Mesh, PartitionSpec as P

CUTOFF = 4.0
SOFTEN = 0.25
WIDTH_X = 16.0
WIDTH_Y = 16.0
DEPTH_Z = 16.0
ACT_GAIN = 1.679
ROOT_THREE = math.sqrt(3.0)
HIGHEST = lax.Precision.HIGHEST
F32 = jnp.float32
BF16 = jnp.bfloat16

C = 128
NB = 24
ATOMS = 128
EDGES = NB * ATOMS
TABLE = 384
NBASIS = 8
K = 1024
KC = 64
TILES = 2 * K // 128
AXES = ("xh", "co", "y", "z", "xl")
WIDE = ("xh", "co", "y", "xl")
NWIDE = 32

NN = (((1,), (0,)), ((), ()))
NT = (((1,), (1,)), ((), ()))
TN = (((0,), (0,)), ((), ()))


def dot(a, b, dims=NN, precision=None):
    return lax.dot_general(a, b, dims, precision=precision, preferred_element_type=F32)


def split(a):
    high = a.astype(BF16)
    return high, (a - high.astype(F32)).astype(BF16)


def dot3(a, b, dims=NN):
    a_hi, a_lo = split(a)
    b_hi, b_lo = split(b)
    return dot(a_hi, b_hi, dims) + (dot(a_lo, b_hi, dims) + dot(a_hi, b_lo, dims))


def gate(v):
    s = 0.5 + 0.5 * jnp.tanh(0.5 * v)
    return s, (ACT_GAIN * v) * s


def gate_slope(v, s):
    return ACT_GAIN * s * (1.0 + v * (1.0 - s))


def onehot_columns(index_row, count, dtype):
    rows = lax.broadcasted_iota(jnp.int32, (count, index_row.shape[1]), 0)
    return (rows == index_row).astype(F32).astype(dtype)


def merge(a, b, split_lane):
    lane = lax.broadcasted_iota(jnp.int32, a.shape, 1)
    return jnp.where(lane < split_lane, a, b)


def pick(values, index_row):
    return dot(values, onehot_columns(index_row, values.shape[1], F32), NN, HIGHEST)


def give_back(grads, index_row, count):
    return dot(grads, onehot_columns(index_row, count, F32), NT, HIGHEST)


def send_rows(values, count, gap, a_ref, b_ref):
    rows = values.T
    a_ref[...] = rows[:count]
    b_ref[...] = rows[gap : gap + count]


def received(a_ref, b_ref, gap):
    a, b = a_ref[...], b_ref[...]
    pieces = [a, b, jnp.zeros((128 - gap - b.shape[0], 128), F32)]
    if gap > a.shape[0]:
        pieces.insert(1, jnp.zeros((gap - a.shape[0], 128), F32))
    return jnp.concatenate(pieces, 0).T


def place(index):
    px, py = lax.axis_index("co"), lax.axis_index("xl")
    far = jnp.where(index < 240, index + (128 - 64 * py), index + (16 + 64 * py))
    near = jnp.where(index < 160, index + (32 - 32 * px), index + (32 * px - 32))
    return jnp.where(index < 128, index, jnp.where(index < 192, near, far))


def strip_x_kernel(pos_ref, species_ref, send_ref, rows_ref, ix_ref, out_ref):
    odd = lax.axis_index("co")
    lower, upper = send_ref[0:1, :], send_ref[1:2, :]
    first = upper + (lower - upper) * odd
    second = lower + (upper - lower) * odd
    index = jnp.concatenate([first, second, jnp.full((1, 64), -1, jnp.int32)], 1)
    rows = jnp.concatenate([pos_ref[...], species_ref[...].astype(F32), jnp.zeros((4, ATOMS), F32)], 0)
    ix_ref[...] = index
    rows_ref[...] = rows
    out_ref[...] = pick(rows, index)


def strip_y_kernel(rows_ref, a_ref, b_ref, send_ref, part_ref, iy_ref, out_ref):
    odd = lax.axis_index("xl")
    send = place(send_ref[...])
    lower, upper = send[0:1], send[1:2]
    first = upper + (lower - upper) * odd
    second = lower + (upper - lower) * odd
    none = jnp.full((1, 16), -1, jnp.int32)
    index = jnp.concatenate([first, none, second, none], 1)
    part = merge(a_ref[...], b_ref[...], 32)
    part_ref[...] = part
    iy_ref[...] = index
    out_ref[...] = pick(jnp.concatenate([rows_ref[...], part], 1), index)


WIDE_TILE = 1024


def flat(ref, k, g):
    count = WIDE_TILE // 128
    return jnp.concatenate([ref[k, count * g + j : count * g + j + 1, :] for j in range(count)], 1)


def radial(layer, geo_ref, w1_ref, w2_ref, w3_ref, r_ref, p_ref):
    w1 = w1_ref[layer].astype(BF16)
    w2 = w2_ref[layer]
    w3 = w3_ref[layer].astype(F32).T.astype(BF16)
    spacing = CUTOFF / (NBASIS - 1)
    centre = lax.broadcasted_iota(jnp.int32, (NBASIS, WIDE_TILE), 0).astype(F32) * spacing
    for g in range(EDGES // WIDE_TILE):
        cols = slice(g * WIDE_TILE, (g + 1) * WIDE_TILE)
        gap = (flat(geo_ref, 3, g) - centre) * (1.0 / spacing)
        basis = jnp.exp(-gap * gap)
        z1 = dot(w1, basis.astype(BF16), TN)
        s1, h1 = gate(z1)
        z2 = dot(w2, h1.astype(BF16))
        s2, h2 = gate(z2)
        if r_ref is not None:
            r_ref[:, cols] = dot(w3, (h2 * flat(geo_ref, 4, g)).astype(BF16)).astype(BF16)
        if p_ref is not None:
            slope = basis * gap * (-2.0 / spacing)
            h1p = gate_slope(z1, s1) * dot(w1, slope.astype(BF16), TN)
            h2p = gate_slope(z2, s2) * dot(w2, h1p.astype(BF16))
            mixed = h2p * flat(geo_ref, 6, g) + h2 * flat(geo_ref, 5, g)
            p_ref[:, cols] = dot(w3, mixed.astype(BF16)).astype(BF16)


def aggregate(r_ref, get_f, y_ref, a_ref):
    def body(cc, carry):
        r0 = pl.multiple_of(cc * 16, 16)
        acc = [jnp.zeros((16, 128), F32) for _ in range(9)]
        state = get_f(r0)
        for n in range(NB):
            cols = slice(n * 128, (n + 1) * 128)
            f = state(n)
            g0 = r_ref[pl.ds(r0, 16), cols].astype(F32) * f
            g1 = r_ref[pl.ds(128 + r0, 16), cols].astype(F32) * f
            g2 = r_ref[pl.ds(256 + r0, 16), cols].astype(F32) * f
            acc[0] = acc[0] + g0
            for m in range(3):
                acc[1 + m] = acc[1 + m] + g1 * y_ref[m, n : n + 1, :]
            for m in range(5):
                acc[4 + m] = acc[4 + m] + g2 * y_ref[3 + m, n : n + 1, :]
        for k in range(9):
            a_ref[k, pl.ds(r0, 16), :] = acc[k]
        return carry

    lax.fori_loop(0, 8, body, 0)


def invariants(a_ref):
    a1 = a_ref[1] * a_ref[1] + a_ref[2] * a_ref[2] + a_ref[3] * a_ref[3]
    a2 = a_ref[4] * a_ref[4] + a_ref[5] * a_ref[5] + a_ref[6] * a_ref[6]
    a2 = a2 + a_ref[7] * a_ref[7] + a_ref[8] * a_ref[8]
    return jnp.concatenate([a_ref[0].astype(BF16), a1.astype(BF16), a2.astype(BF16)], 0)


def take_lanes(tables, lane, group):
    got = [jnp.take_along_axis(t, lane, axis=1, mode="promise_in_bounds") for t in tables]
    return jnp.where(group == 0, got[0], jnp.where(group == 1, got[1], got[2]))


def first_kernel(
    box_x, box_y, rows_ref, part_ref, a_in, b_in, raw_ref, live_ref, ix_ref, emb_ref, w1_ref, w2_ref,
    w3_ref, mix_ref, nb_ref, geo_out, y_out, f_out, a_out, h_ref, h_out, xa_ref, xb_ref, r_ref,
):
    geo_ref, y_ref, f_ref, a_ref = geo_out.ref, y_out.ref, f_out.ref, a_out.ref
    own = rows_ref[...]
    tables = [own, part_ref[...], merge(a_in[...], b_in[...], 64)]
    nb = place(raw_ref[...])
    nb_ref[...] = nb
    lane, group = nb & 127, nb >> 7

    def gathered(row):
        return jnp.concatenate(
            [
                take_lanes(
                    [jnp.broadcast_to(t[row : row + 1], (8, 128)) for t in tables],
                    lane[8 * b : 8 * b + 8],
                    group[8 * b : 8 * b + 8],
                )
                for b in range(NB // 8)
            ],
            0,
        )

    off_x = gathered(0) - own[0:1]
    off_y = gathered(1) - own[1:2]
    step_z = gathered(2) - own[2:3]
    step_x = off_x - box_x * jnp.floor(off_x * (1.0 / box_x) + 0.5)
    step_y = off_y - box_y * jnp.floor(off_y * (1.0 / box_y) + 0.5)
    square = step_x * step_x + step_y * step_y + step_z * step_z
    shifted = square + SOFTEN
    inverse = lax.rsqrt(shifted)
    live = live_ref[...].astype(F32)
    inside = jnp.maximum(1.0 - square * (1.0 / (CUTOFF * CUTOFF)), 0.0)
    env = inside * inside * live
    ux, uy, uz = step_x * (1.0 / CUTOFF), step_y * (1.0 / CUTOFF), step_z * (1.0 / CUTOFF)
    geo_ref[0] = ux
    geo_ref[1] = uy
    geo_ref[2] = uz
    geo_ref[3] = jnp.sqrt(shifted)
    geo_ref[4] = env
    geo_ref[5] = inside * live * (-2.0 / (CUTOFF * CUTOFF))
    geo_ref[6] = 0.5 * env * inverse
    y_ref[0] = ux
    y_ref[1] = uy
    y_ref[2] = uz
    y_ref[3] = ux * uy
    y_ref[4] = uy * uz
    y_ref[5] = uz * ux
    y_ref[6] = ux * ux - uy * uy
    y_ref[7] = (2.0 * uz * uz - ux * ux - uy * uy) * (1.0 / ROOT_THREE)

    geo_ref[7] = gathered(3)
    geo_out.send()
    y_out.send()
    emb = jnp.concatenate([emb_ref[...], jnp.zeros((8 - emb_ref.shape[0], C), F32)], 0).astype(BF16)
    kinds = lax.broadcasted_iota(jnp.int32, (8, WIDE_TILE), 0).astype(F32)
    for g in range(EDGES // WIDE_TILE):
        cols = slice(g * WIDE_TILE, (g + 1) * WIDE_TILE)
        f_ref[:, cols] = dot(emb, (kinds == flat(geo_ref, 7, g)).astype(F32).astype(BF16), TN).astype(BF16)
    f_out.send()
    radial(0, geo_ref, w1_ref, w2_ref, w3_ref, r_ref, None)

    def get_f(r0):
        return lambda n: f_ref[pl.ds(r0, 16), n * 128 : (n + 1) * 128].astype(F32)

    aggregate(r_ref, get_f, y_ref, a_ref)
    a_out.send()
    h_zero = dot(emb, (kinds[:, :128] == own[3:4]).astype(F32).astype(BF16), TN)
    h_one = h_zero + dot(mix_ref[0], invariants(a_ref))
    h_ref[...] = h_one
    h_out.ref[...] = h_one
    h_out.send()
    send_rows(pick(h_one, ix_ref[...]), 32, 32, xa_ref, xb_ref)


def radial_kernel(geo_ref, w1_ref, w2_ref, w3_ref, r_ref, r_out):
    radial(1, geo_ref, w1_ref, w2_ref, w3_ref, r_ref, None)
    r_out.ref[...] = r_ref[...]


def slope_one_kernel(geo_ref, w1_ref, w2_ref, w3_ref, nb_ref, p_out, oh_out):
    fill_onehot(nb_ref, oh_out.ref)
    oh_out.send()
    radial(1, geo_ref, w1_ref, w2_ref, w3_ref, None, p_out.ref)


def slope_zero_kernel(geo_ref, w1_ref, w2_ref, w3_ref, r_ref, p_ref):
    radial(0, geo_ref, w1_ref, w2_ref, w3_ref, r_ref, p_ref)


def waves_kernel(box_x, box_y, rows_ref, wave_ref, cs_out):
    cs_ref = cs_out.ref
    own = rows_ref[...]
    x, y, z = own[0:1] * (1.0 / box_x), own[1:2] * (1.0 / box_y), own[2:3] * (1.0 / DEPTH_Z)
    turns = jnp.concatenate([x, y, z, jnp.zeros((5, ATOMS), F32)], 0)
    turns = turns - jnp.floor(turns)
    high = turns.astype(BF16).astype(F32)
    middle = (turns - high).astype(BF16).astype(F32)
    low = turns - high - middle
    parts = jnp.concatenate([high, middle, low, jnp.zeros((8, ATOMS), F32)], 0).astype(BF16)
    wave = jnp.concatenate([wave_ref[...].astype(F32), jnp.zeros((5, K), F32)], 0)
    wave = jnp.concatenate([wave, wave, wave, jnp.zeros((8, K), F32)], 0).astype(BF16)
    cs_ref[:, :K] = dot(parts, wave, TN)

    def tile(t, carry):
        cols = pl.ds(pl.multiple_of(t * 128, 128), 128)
        phase = cs_ref[:, cols]
        quarter = jnp.floor(4.0 * phase + 0.5)
        angle = (phase - 0.25 * quarter) * (2.0 * math.pi)
        sq = angle * angle
        sin = angle * (1.0 + sq * (-1.0 / 6 + sq * (1.0 / 120 + sq * (-1.0 / 5040 + sq * (1.0 / 362880)))))
        cos = 1.0 + sq * (-0.5 + sq * (1.0 / 24 + sq * (-1.0 / 720 + sq * (1.0 / 40320 - sq * (1.0 / 3628800)))))
        turn = quarter.astype(jnp.int32) & 3
        odd = (turn & 1) == 1
        c = jnp.where(odd, sin, cos)
        s = jnp.where(odd, cos, sin)
        c = jnp.where((turn == 1) | (turn == 2), -c, c)
        s = jnp.where(turn >= 2, -s, s)
        cs_ref[:, cols] = c
        cs_ref[:, pl.ds(pl.multiple_of(K + t * 128, 128), 128)] = s
        return carry

    lax.fori_loop(0, K // 128, tile, 0)


def feature_strip_kernel(h_ref, a_in, b_in, iy_ref, part_ref, ya_ref, yb_ref):
    part = received(a_in, b_in, 32)
    part_ref[...] = part
    send_rows(pick(jnp.concatenate([h_ref[...], part], 1), iy_ref[...]), 48, 64, ya_ref, yb_ref)


def second_kernel(
    h_ref, part_ref, a_in, b_in, nb_ref, y_ref, r_ref, cs_in, mix_in,
    w_charge_ref, f_out, a_out, h2_out, charge_out, s_ref, ypart_ref,
):
    f_ref, a_ref, h2_ref, charge_ref = f_out.ref, a_out.ref, h2_out.ref, charge_out.ref
    ypart_ref[...] = received(a_in, b_in, 64)

    def get_f(r0):
        rows = pl.ds(r0, 16)
        tables = [h_ref[rows, :], part_ref[rows, :], ypart_ref[rows, :]]

        def state(n):
            nb = jnp.broadcast_to(nb_ref[n : n + 1, :], (16, 128))
            f = take_lanes(tables, nb & 127, nb >> 7)
            f_ref[rows, n * 128 : (n + 1) * 128] = f
            return f

        return state

    aggregate(r_ref, get_f, y_ref, a_ref)
    f_out.send()
    a_out.send()
    mix_ref, cs_ref = mix_in.ready(), cs_in.ready()
    h_two = h_ref[...] + dot(mix_ref[1], invariants(a_ref))
    h2_ref[...] = h_two
    charge = dot(w_charge_ref[...], h_two.astype(BF16))
    charge_ref[...] = charge
    h2_out.send()
    charge_out.send()
    q_hi, q_lo = split(charge)
    q_both = jnp.concatenate([q_hi, q_lo], 0)
    for t in range(TILES // 2):
        c_hi, c_lo = split(cs_ref[:, t * 256 : (t + 1) * 256])
        both = dot(q_both, c_hi)
        part = both[:KC] + (both[KC:] + dot(q_hi, c_lo))
        s_ref[2 * t * KC : (2 * t + 1) * KC, :] = part[:, :128]
        s_ref[(2 * t + 1) * KC : (2 * t + 2) * KC, :] = part[:, 128:]


def backward(ga_ref, r_ref, p_ref, f_ref, y_ref, gf_ref, t_ref):
    def body(n, carry):
        cols = pl.ds(pl.multiple_of(n * 128, 128), 128)
        y = [y_ref[m, pl.ds(n, 1), :] for m in range(8)]
        acc = [jnp.zeros((16, 128), F32) for _ in range(9)]
        for cc in range(8):
            rows = slice(cc * 16, cc * 16 + 16)
            ga = [ga_ref[k, rows, :] for k in range(9)]
            f = f_ref[rows, cols].astype(F32)
            r = [r_ref[l * 128 + cc * 16 : l * 128 + cc * 16 + 16, cols].astype(F32) for l in range(3)]
            p = [p_ref[l * 128 + cc * 16 : l * 128 + cc * 16 + 16, cols].astype(F32) for l in range(3)]
            q1 = ga[1] * y[0] + ga[2] * y[1] + ga[3] * y[2]
            q2 = ga[4] * y[3] + ga[5] * y[4] + ga[6] * y[5] + ga[7] * y[6] + ga[8] * y[7]
            if gf_ref is not None:
                gf_ref[rows, cols] = (ga[0] * r[0] + q1 * r[1] + q2 * r[2]).astype(BF16)
            acc[0] = acc[0] + f * (ga[0] * p[0] + q1 * p[1] + q2 * p[2])
            g1, g2 = f * r[1], f * r[2]
            for m in range(3):
                acc[1 + m] = acc[1 + m] + g1 * ga[1 + m]
            for m in range(5):
                acc[4 + m] = acc[4 + m] + g2 * ga[4 + m]
        for k in range(9):
            t_ref[k, pl.ds(n, 1), :] = jnp.sum(acc[k], 0, keepdims=True)
        return carry

    lax.fori_loop(0, NB, body, 0)


def pull_invariants(g_inv, a_ref, ga_ref):
    ga_ref[0] = g_inv[:C]
    for k in range(1, 4):
        ga_ref[k] = 2.0 * a_ref[k] * g_inv[C : 2 * C]
    for k in range(4, 9):
        ga_ref[k] = 2.0 * a_ref[k] * g_inv[2 * C :]


def fill_onehot(nb_ref, oh_ref):
    for n in range(NB):
        oh_ref[:, n * 128 : (n + 1) * 128] = onehot_columns(nb_ref[n : n + 1, :], TABLE, BF16)


def ewald_kernel(
    box_x, box_y, scale, s_ref, spectral_ref, cs_ref, wave_ref, charge_ref, h_in, h2_in, a_in, y_in, r_in, p_in,
    f_in, oh_in, mix_in, first_in, last_in, read_hidden_in, w_charge_in,
    energy_ref, gpos_ref, gown_ref, gpart_ref, ya_ref, yb_ref, t_ref, ga_ref, gf_ref, gphase_ref,
):
    charge = charge_ref[...]
    qt_hi, qt_lo = split(charge.T)
    q_three = jnp.concatenate([qt_hi.astype(F32), qt_lo.astype(F32), qt_hi.astype(F32)], 1).astype(BF16)
    total = jnp.zeros((2 * KC, 2 * ATOMS), F32)
    for t in range(TILES // 2):
        cols = slice(t * 128, (t + 1) * 128)
        late = slice(K + t * 128, K + (t + 1) * 128)
        filt = spectral_ref[:, cols] * scale
        gc = filt * s_ref[t * KC : (t + 1) * KC, :]
        gs = filt * s_ref[(TILES // 2 + t) * KC : (TILES // 2 + t + 1) * KC, :]
        cos, sin = cs_ref[:, cols], cs_ref[:, late]
        g_hi, g_lo = split(jnp.concatenate([gc, gs], 1))
        c_hi, c_lo = split(jnp.concatenate([cos, sin], 1))
        total = total + dot(jnp.concatenate([g_hi, g_lo], 0), jnp.concatenate([c_hi, c_lo], 0), NT)
        phase = dot(q_three, jnp.concatenate([g_hi, g_hi, g_lo], 0))
        p_hi, p_lo = split(phase[:, 128:] * cos - phase[:, :128] * sin)
        gphase_ref[:ATOMS, cols] = p_hi
        gphase_ref[ATOMS:, cols] = p_lo
    potential = total[:KC, :ATOMS] + (total[KC:, :ATOMS] + total[:KC, ATOMS:])
    wave = jnp.concatenate([wave_ref[...].astype(F32), jnp.zeros((5, K), F32)], 0).astype(BF16)
    gpos = dot(wave, gphase_ref[...], NT)
    gpos = gpos[:, :ATOMS] + gpos[:, ATOMS:]
    gpos_ref[...] = jnp.concatenate(
        [
            gpos[0:1] * (2.0 * math.pi / box_x),
            gpos[1:2] * (2.0 * math.pi / box_y),
            gpos[2:3] * (2.0 * math.pi / DEPTH_Z),
            jnp.zeros((5, ATOMS), F32),
        ],
        0,
    )
    h_ref, h2_ref, first_ref, last_ref = h_in.ready(), h2_in.ready(), first_in.ready(), last_in.ready()
    read_hidden_ref, w_charge_ref, mix_ref = read_hidden_in.ready(), w_charge_in.ready(), mix_in.ready()
    h_two = h2_ref[...].astype(BF16)
    z = dot(read_hidden_ref[...], h_two)
    s, hidden = gate(z)
    last = jnp.broadcast_to(last_ref[...], (128, last_ref.shape[1])).T
    first = jnp.broadcast_to(first_ref[...], (128, 128)).T
    site = jnp.sum(first * h_ref[...], 0, keepdims=True) + jnp.sum(last * hidden, 0, keepdims=True)
    energy_ref[...] = site + 0.5 * jnp.sum(charge * potential, 0, keepdims=True)
    g_hidden = (last * gate_slope(z, s)).astype(BF16)
    g_two = dot(w_charge_ref[...], potential.astype(BF16), TN) + dot(read_hidden_ref[...], g_hidden, TN)
    g_two = g_two.astype(BF16)
    g_inv = dot(mix_ref[1], g_two, TN).astype(BF16).astype(F32)
    a_ref, y_ref, r_ref, p_ref, f_ref = a_in.ready(), y_in.ready(), r_in.ready(), p_in.ready(), f_in.ready()
    pull_invariants(g_inv, a_ref, ga_ref)
    backward(ga_ref, r_ref, p_ref, f_ref, y_ref, gf_ref, t_ref)
    oh_ref = oh_in.ready()
    grads = dot(gf_ref[...], oh_ref[...], NT)
    gown_ref[...] = grads[:, :128] + g_two.astype(F32) + first
    gpart_ref[...] = grads[:, 128:256]
    send_rows(grads[:, 256:], 48, 64, ya_ref, yb_ref)


def return_features_kernel(gown_ref, gpart_ref, a_in, b_in, iy_ref, own_ref, xa_ref, xb_ref):
    back = give_back(received(a_in, b_in, 64), iy_ref[...], 256)
    own_ref[...] = gown_ref[...] + back[:, :128]
    send_rows(gpart_ref[...] + back[:, 128:], 32, 32, xa_ref, xb_ref)


def return_y_kernel(gown_ref, gpart_ref, a_in, b_in, iy_ref, own_ref, part_ref):
    back = give_back(merge(a_in[...], b_in[...], 64), iy_ref[...], 256)
    own_ref[...] = gown_ref[...] + back[:, :128]
    part_ref[...] = gpart_ref[...] + back[:, 128:]


def last_kernel(
    gown_ref, a_in, b_in, ix_ref, mix_ref, a_ref, r_ref, p_ref, f_ref, y_ref, t1_ref, geo_ref, oh_ref, gpos_ref,
    own_ref, part_ref, gy_ref, ga_ref, t_ref, rows_ref,
):
    g_one = gown_ref[...] + give_back(received(a_in, b_in, 32), ix_ref[...], 128)
    g_inv = dot(mix_ref[0], g_one.astype(BF16), TN).astype(BF16).astype(F32)
    pull_invariants(g_inv, a_ref, ga_ref)
    backward(ga_ref, r_ref, p_ref, f_ref, y_ref, None, t_ref)
    t = [t_ref[k] + t1_ref[k] for k in range(9)]
    ux, uy, uz = geo_ref[0], geo_ref[1], geo_ref[2]
    root = 2.0 / ROOT_THREE
    gx = t[1] + t[4] * uy + t[6] * uz + ux * (2.0 * t[7] - root * t[8])
    gy = t[2] + t[4] * ux + t[5] * uz - uy * (2.0 * t[7] + root * t[8])
    gz = t[3] + t[5] * uy + t[6] * ux + (2.0 * root) * uz * t[8]
    steps = [g * (1.0 / CUTOFF) + (2.0 * CUTOFF) * u * t[0] for g, u in ((gx, ux), (gy, uy), (gz, uz))]
    rows_ref[...] = jnp.zeros(rows_ref.shape, F32)
    for k in range(3):
        high = steps[k].astype(BF16).astype(F32)
        low = steps[k] - high
        for n in range(NB):
            rows_ref[k : k + 1, n * 128 : (n + 1) * 128] = high[n : n + 1]
            rows_ref[8 + k : 9 + k, n * 128 : (n + 1) * 128] = low[n : n + 1]
    both = dot(rows_ref[...].astype(BF16), oh_ref[...], NT)
    grads = both[:8] + both[8:]
    centre = jnp.concatenate([jnp.sum(g, 0, keepdims=True) for g in steps] + [jnp.zeros((5, 128), F32)], 0)
    own_ref[...] = grads[:, :128] - centre + gpos_ref[...]
    part_ref[...] = grads[:, 128:256]
    gy_ref[...] = grads[:, 256:]


def final_kernel(own_ref, a_in, b_in, ix_ref, out_ref):
    total = own_ref[...] + give_back(merge(a_in[...], b_in[...], 32), ix_ref[...], 128)
    out_ref[...] = -total[:3]


def sum_kernel(pieces, copies, in_ref, out_ref):
    out_ref = getattr(out_ref, "ref", out_ref)
    rows = in_ref.shape[0] // pieces
    total = in_ref[0:rows, :]
    for g in range(1, pieces):
        total = total + in_ref[g * rows : (g + 1) * rows, :]
    for g in range(copies):
        out_ref[g * rows : (g + 1) * rows, :] = total


class Far:
    def __init__(self, array, late=False):
        self.array = array
        self.late = late


class Late:
    def __init__(self, copy, ref):
        self.copy = copy
        self.ref = ref

    def ready(self):
        self.copy.wait()
        return self.ref


class Out:
    def __init__(self, copy, ref):
        self.copy = copy
        self.ref = ref
        self.sent = False

    def send(self):
        self.copy.start()
        self.sent = True


def call(kernel, outs, *operands, scratch=(), flops=0, moved=0):
    n_in, n_out = len(operands), len(outs)
    far_in = [i for i, o in enumerate(operands) if isinstance(o, Far)]
    far_out = [i for i, o in enumerate(outs) if len(o) == 3]
    arrays = [pltpu.with_memory_space_constraint(o.array, pltpu.HBM) if isinstance(o, Far) else o for o in operands]
    n_far = len(far_in) + len(far_out)
    buffers = [pltpu.VMEM(arrays[i].shape, arrays[i].dtype) for i in far_in]
    buffers += [pltpu.VMEM(outs[i][0], outs[i][1]) for i in far_out]

    def wrapped(*refs):
        ins, results, rest = list(refs[:n_in]), list(refs[n_in : n_in + n_out]), refs[n_in + n_out :]
        own, held = rest[: len(scratch)], rest[len(scratch) : len(scratch) + n_far]
        sems = rest[-1]
        waits = []
        for k, i in enumerate(far_in):
            copy = pltpu.make_async_copy(ins[i], held[k], sems.at[k])
            copy.start()
            if operands[i].late:
                ins[i] = Late(copy, held[k])
            else:
                waits.append(copy)
                ins[i] = held[k]
        sent = []
        for k, i in enumerate(far_out, len(far_in)):
            results[i] = Out(pltpu.make_async_copy(held[k], results[i], sems.at[k]), held[k])
            sent.append(results[i])
        for copy in waits:
            copy.wait()
        kernel(*ins, *results, *own)
        for out in sent:
            if not out.sent:
                out.send()
        for out in sent:
            out.copy.wait()

    def place_of(far):
        return pl.BlockSpec(memory_space=pltpu.HBM if far else pltpu.VMEM)

    return pl.pallas_call(
        wrapped,
        out_shape=[pltpu.HBM(o[0], o[1]) if len(o) == 3 else jax.ShapeDtypeStruct(o[0], o[1]) for o in outs],
        in_specs=[place_of(isinstance(o, Far)) for o in operands],
        out_specs=[place_of(len(o) == 3) for o in outs],
        scratch_shapes=[pltpu.VMEM(s, d) for s, d in scratch] + buffers + [pltpu.SemaphoreType.DMA((max(n_far, 1),))],
        compiler_params=pltpu.CompilerParams(vmem_limit_bytes=24 * 1024 * 1024),
        cost_estimate=pl.CostEstimate(flops=flops, bytes_accessed=moved, transcendentals=0),
    )(*arrays)


def swap(value, axes, of):
    count = 1
    for axis in axes:
        count *= lax.axis_size(axis)
    return lax.ppermute(value, axes, [(i, of(i)) for i in range(count)])


BX = ("xh", "co")
CELL = ("y", "z", "xl")


def swap_x(a, b):
    return swap(a, BX, lambda i: i ^ 1), swap(b, BX, lambda i: i ^ 3)


def swap_y(a, b):
    def other(c):
        return (c - 1) % 64 if c % 2 == 0 else (c + 1) % 64

    return swap(a, CELL, lambda c: c ^ 1), swap(b, CELL, other)


def reduce_all(partial):
    rows = partial.shape[0] // NWIDE
    pieces = lax.all_to_all(partial, WIDE, 0, 0, tiled=True)
    (mine,) = call(functools.partial(sum_kernel, NWIDE, 8), [((8 * rows, 128), F32)], pieces)
    mine = lax.all_to_all(mine, ("z",), 0, 0, tiled=True)
    (spread,) = call(functools.partial(sum_kernel, 8, NWIDE), [((NWIDE * rows, 128), F32, True)], mine)
    return lax.all_to_all(spread, WIDE, 0, 0, tiled=True)


def body(
    positions, species, send_x, send_y, neighbours, live_slots, embedding, radial_in, radial_mid, radial_out, mixing,
    read_first, read_hidden, read_last, w_charge, spectral, wave_ids,
):
    count_x = lax.axis_size("xh") * lax.axis_size("co")
    count_y = lax.axis_size("y") * lax.axis_size("z") * lax.axis_size("xl")
    box_x = count_x * WIDTH_X
    box_y = count_y * WIDTH_Y
    scale = 1.0 / math.sqrt(K * ATOMS * count_x * count_y)
    small = ((8, 128), F32)
    square = ((C, 128), F32)
    edge3 = ((3 * C, EDGES), BF16)
    index = ((1, 128), jnp.int32)
    strip_32, strip_48 = ((32, 128), F32), ((48, 128), F32)
    w1, w3, emb = radial_in.swapaxes(1, 2).astype(F32), radial_out.swapaxes(1, 2), embedding.T.astype(F32)

    with_box = functools.partial

    rows, ix, strip = call(strip_x_kernel, [small, index, small], Far(positions), Far(species[None]), Far(send_x))
    xa, xb = swap_x(strip, strip)
    part, iy, strip = call(strip_y_kernel, [small, index, small], rows, xa, xb, Far(send_y))
    ya, yb = swap_y(strip, strip)
    nets = (Far(w1), Far(radial_mid), Far(w3))
    nb, geo, ylm, f_zero, a_zero, h_one, h_far, xa, xb = call(
        with_box(first_kernel, box_x, box_y),
        [
            ((NB, 128), jnp.int32), ((8, NB, 128), F32, True), ((8, NB, 128), F32, True),
            ((C, EDGES), BF16, True), ((9, C, 128), F32, True), square, square + (True,), strip_32, strip_32,
        ],
        rows, part, ya, yb, Far(neighbours), Far(live_slots), ix, Far(emb), *nets, Far(mixing),
        scratch=[edge3],
    )
    rows_later, geo_soon, _, _ = lax.optimization_barrier((rows, geo, xa, xb))
    xa, xb = swap_x(xa, xb)
    (cs,) = call(
        with_box(waves_kernel, box_x, box_y), [((ATOMS, 2 * K), F32, True)], rows_later, Far(wave_ids), flops=10**8, moved=10**6
    )
    xa, xb, cs = lax.optimization_barrier((xa, xb, cs))
    fpart, ya, yb = call(feature_strip_kernel, [square, strip_48, strip_48], h_one, xa, xb, iy)
    geo_soon, _, _ = lax.optimization_barrier((geo_soon, ya, yb))
    ya, yb = swap_y(ya, yb)
    r_one, r_far = call(radial_kernel, [edge3, edge3 + (True,)], Far(geo_soon), *nets, flops=5 * 10**8, moved=10**7)
    f_one, a_one, h_two, charge, s_part = call(
        second_kernel,
        [((C, EDGES), F32, True), ((9, C, 128), F32, True), square + (True,), ((KC, ATOMS), F32, True), ((TILES * KC, 128), F32)],
        h_one, fpart, ya, yb, nb, Far(ylm), r_one, Far(cs, True), Far(mixing, True), Far(w_charge),
        scratch=[square],
    )
    geo_later, _ = lax.optimization_barrier((geo, s_part))
    p_one, oh = call(
        slope_one_kernel, [edge3 + (True,), ((TABLE, EDGES), BF16, True)], Far(geo_later), *nets, Far(nb), flops=10**9, moved=10**7
    )
    s_all = reduce_all(s_part)
    late = lambda array: Far(array, True)
    energy, gpos, gown, gpart, ya, yb, t_one = call(
        with_box(ewald_kernel, box_x, box_y, scale),
        [((1, 128), F32), small, square, square, strip_48, strip_48, ((9, NB, 128), F32)],
        Far(s_all), Far(spectral), Far(cs), Far(wave_ids), Far(charge), late(h_far), late(h_two), late(a_one), late(ylm), late(r_far),
        late(p_one), late(f_one), late(oh), late(mixing), late(read_first[None]), late(read_last[None]), late(read_hidden), late(w_charge),
        scratch=[((9, C, 128), F32), ((C, EDGES), BF16), ((2 * ATOMS, K), BF16)],
    )
    geo_last, _, _ = lax.optimization_barrier((geo, ya, yb))
    ya, yb = swap_y(ya, yb)
    r_zero, p_zero = call(slope_zero_kernel, [edge3, edge3], Far(geo_last), *nets, flops=10**9, moved=10**7)
    gown, xa, xb = call(return_features_kernel, [square, strip_32, strip_32], gown, gpart, ya, yb, iy)
    xa, xb = swap_x(xa, xb)
    own, part, gy = call(
        last_kernel,
        [small, small, small],
        gown, xa, xb, ix, mixing, a_zero, r_zero, p_zero, f_zero, ylm, t_one, geo, oh, gpos,
        scratch=[((9, C, 128), F32), ((9, NB, 128), F32), ((16, EDGES), F32)],
    )
    ya, yb = swap_y(gy, gy)
    own, part = call(return_y_kernel, [small, small], own, part, ya, yb, iy)
    xa, xb = swap_x(part, part)
    (forces,) = call(final_kernel, [((3, ATOMS), F32)], own, xa, xb, ix)
    return energy[0], forces


def solution(mesh):
    fine = Mesh(mesh.devices.reshape(2, 2, 4, 8, 2), AXES)
    rows, columns = P(AXES), P(None, AXES)
    placed = (columns, rows) + (columns,) * 4 + (P(),) * 11
    return jax.shard_map(body, mesh=fine, in_specs=placed, out_specs=(rows, columns), check_vma=False)
```

```python
import functools
import math

import jax
import jax.numpy as jnp
from jax import lax
from jax.experimental import pallas as pl
from jax.experimental.pallas import tpu as pltpu
from jax.sharding import Mesh, PartitionSpec as P

CUTOFF = 4.0
SOFTEN = 0.25
WIDTH_X = 16.0
WIDTH_Y = 16.0
DEPTH_Z = 16.0
ACT_GAIN = 1.679
ROOT_THREE = math.sqrt(3.0)
HIGHEST = lax.Precision.HIGHEST
F32 = jnp.float32
BF16 = jnp.bfloat16

C = 128
NB = 24
ATOMS = 128
EDGES = NB * ATOMS
TABLE = 384
NBASIS = 8
BLOCKS = 4
K = 1024
KC = 64
TILES = 2 * K // 128
AXES = ("xh", "co", "y", "z", "xl")
WIDE = ("xh", "co", "y", "xl")
NWIDE = 32

NN = (((1,), (0,)), ((), ()))
NT = (((1,), (1,)), ((), ()))
TN = (((0,), (0,)), ((), ()))


def dot(a, b, dims=NN, precision=None):
    return lax.dot_general(a, b, dims, precision=precision, preferred_element_type=F32)


def split(a):
    high = a.astype(BF16)
    return high, (a - high.astype(F32)).astype(BF16)


def dot3(a, b, dims=NN):
    a_hi, a_lo = split(a)
    b_hi, b_lo = split(b)
    return dot(a_hi, b_hi, dims) + (dot(a_lo, b_hi, dims) + dot(a_hi, b_lo, dims))


def gate(v):
    s = 0.5 + 0.5 * jnp.tanh(0.5 * v)
    return s, (ACT_GAIN * v) * s


def gate_slope(v, s):
    return ACT_GAIN * s * (1.0 + v * (1.0 - s))


def onehot_columns(index_row, count, dtype):
    rows = lax.broadcasted_iota(jnp.int32, (count, index_row.shape[1]), 0)
    return (rows == index_row).astype(F32).astype(dtype)


def merge(a, b, split_lane):
    lane = lax.broadcasted_iota(jnp.int32, a.shape, 1)
    return jnp.where(lane < split_lane, a, b)


def pick(values, index_row):
    return dot(values, onehot_columns(index_row, values.shape[1], F32), NN, HIGHEST)


def give_back(grads, index_row, count):
    return dot(grads, onehot_columns(index_row, count, F32), NT, HIGHEST)


def send_rows(values, count, gap, a_ref, b_ref):
    rows = values.T
    a_ref[...] = rows[:count]
    b_ref[...] = rows[gap : gap + count]


def received(a_ref, b_ref, gap):
    a, b = a_ref[...], b_ref[...]
    pieces = [a, b, jnp.zeros((128 - gap - b.shape[0], 128), F32)]
    if gap > a.shape[0]:
        pieces.insert(1, jnp.zeros((gap - a.shape[0], 128), F32))
    return jnp.concatenate(pieces, 0).T


def place(index):
    px, py = lax.axis_index("co"), lax.axis_index("xl")
    far = jnp.where(index < 240, index + (128 - 64 * py), index + (16 + 64 * py))
    near = jnp.where(index < 160, index + (32 - 32 * px), index + (32 * px - 32))
    return jnp.where(index < 128, index, jnp.where(index < 192, near, far))


def strip_x_kernel(pos_ref, species_ref, send_ref, rows_ref, ix_ref, out_ref):
    odd = lax.axis_index("co")
    lower, upper = send_ref[0:1, :], send_ref[1:2, :]
    first = upper + (lower - upper) * odd
    second = lower + (upper - lower) * odd
    index = jnp.concatenate([first, second, jnp.full((1, 64), -1, jnp.int32)], 1)
    rows = jnp.concatenate([pos_ref[...], species_ref[...].astype(F32), jnp.zeros((4, ATOMS), F32)], 0)
    ix_ref[...] = index
    rows_ref[...] = rows
    out_ref[...] = pick(rows, index)


def strip_y_kernel(rows_ref, a_ref, b_ref, send_ref, part_ref, iy_ref, out_ref):
    odd = lax.axis_index("xl")
    send = place(send_ref[...])
    lower, upper = send[0:1], send[1:2]
    first = upper + (lower - upper) * odd
    second = lower + (upper - lower) * odd
    none = jnp.full((1, 16), -1, jnp.int32)
    index = jnp.concatenate([first, none, second, none], 1)
    part = merge(a_ref[...], b_ref[...], 32)
    part_ref[...] = part
    iy_ref[...] = index
    out_ref[...] = pick(jnp.concatenate([rows_ref[...], part], 1), index)


WIDE_TILE = 1024


def flat(ref, k, g):
    count = WIDE_TILE // 128
    return jnp.concatenate([ref[k, count * g + j : count * g + j + 1, :] for j in range(count)], 1)


def radial(layer, geo_ref, w1_ref, w2_ref, w3_ref, r_ref, p_ref):
    w1 = w1_ref[layer].astype(BF16)
    w2 = w2_ref[layer]
    w3 = w3_ref[layer]
    if w3.shape[0] < w3.shape[1]:
        w3 = w3.astype(F32).T.astype(BF16)
    spacing = CUTOFF / (NBASIS - 1)
    centre = lax.broadcasted_iota(jnp.int32, (NBASIS, WIDE_TILE), 0).astype(F32) * spacing
    for g in range(EDGES // WIDE_TILE):
        cols = slice(g * WIDE_TILE, (g + 1) * WIDE_TILE)
        gap = (flat(geo_ref, 3, g) - centre) * (1.0 / spacing)
        basis = jnp.exp(-gap * gap)
        z1 = dot(w1, basis.astype(BF16), TN)
        s1, h1 = gate(z1)
        z2 = dot(w2, h1.astype(BF16))
        s2, h2 = gate(z2)
        if r_ref is not None:
            r_ref[:, cols] = dot(w3, (h2 * flat(geo_ref, 4, g)).astype(BF16)).astype(BF16)
        if p_ref is not None:
            slope = basis * gap * (-2.0 / spacing)
            h1p = gate_slope(z1, s1) * dot(w1, slope.astype(BF16), TN)
            h2p = gate_slope(z2, s2) * dot(w2, h1p.astype(BF16))
            mixed = h2p * flat(geo_ref, 6, g) + h2 * flat(geo_ref, 5, g)
            p_ref[:, cols] = dot(w3, mixed.astype(BF16)).astype(BF16)


def aggregate(r_ref, get_f, y_ref, a_ref):
    def body(cc, carry):
        r0 = pl.multiple_of(cc * 16, 16)
        acc = [jnp.zeros((16, 128), F32) for _ in range(9)]
        state = get_f(r0)
        for n in range(NB):
            cols = slice(n * 128, (n + 1) * 128)
            f = state(n)
            g0 = r_ref[pl.ds(r0, 16), cols].astype(F32) * f
            g1 = r_ref[pl.ds(128 + r0, 16), cols].astype(F32) * f
            g2 = r_ref[pl.ds(256 + r0, 16), cols].astype(F32) * f
            acc[0] = acc[0] + g0
            for m in range(3):
                acc[1 + m] = acc[1 + m] + g1 * y_ref[m, n : n + 1, :]
            for m in range(5):
                acc[4 + m] = acc[4 + m] + g2 * y_ref[3 + m, n : n + 1, :]
        for k in range(9):
            a_ref[k, pl.ds(r0, 16), :] = acc[k]
        return carry

    lax.fori_loop(0, 8, body, 0)


def invariants(a_ref):
    a1 = a_ref[1] * a_ref[1] + a_ref[2] * a_ref[2] + a_ref[3] * a_ref[3]
    a2 = a_ref[4] * a_ref[4] + a_ref[5] * a_ref[5] + a_ref[6] * a_ref[6]
    a2 = a2 + a_ref[7] * a_ref[7] + a_ref[8] * a_ref[8]
    return jnp.concatenate([a_ref[0].astype(BF16), a1.astype(BF16), a2.astype(BF16)], 0)


def take_lanes(tables, lane, group):
    got = [jnp.take_along_axis(t, lane, axis=1, mode="promise_in_bounds") for t in tables]
    return jnp.where(group == 0, got[0], jnp.where(group == 1, got[1], got[2]))


def fetch_kernel(nb_ref, live_ref, emb_ref, w1_ref, w2_ref, w3_ref, mix_ref, wave_ref, nb_out, live_out, emb_out, w1_out, w2_out, w3_out, mix_out, wave_out):
    wave_out[...] = jnp.concatenate([wave_ref[...].astype(F32), jnp.zeros((5, K), F32)], 0)
    nb_out[...] = place(nb_ref[...])
    live_out[...] = live_ref[...].astype(F32)
    emb_out[...] = jnp.concatenate([emb_ref[...], jnp.zeros((8 - emb_ref.shape[0], C), F32)], 0)
    w1_out[...] = w1_ref[...]
    w2_out[...] = w2_ref[...]
    mix_out[...] = mix_ref[...]
    for layer in range(2):
        w3_out[layer] = w3_ref[layer].astype(F32).T.astype(BF16)


def first_kernel(
    box_x, box_y, rows_ref, part_ref, a_in, b_in, nb_ref, live_ref, ix_ref, emb_ref, w1_ref, w2_ref,
    w3_ref, mix_ref, geo_ref, y_ref, f_out, r_out, a_ref, h_ref, xa_ref, xb_ref,
):
    f_ref, r_ref = f_out.ref, r_out.ref
    own = rows_ref[...]
    tables = [own, part_ref[...], merge(a_in[...], b_in[...], 64)]
    nb = nb_ref[...]
    lane, group = nb & 127, nb >> 7

    def gathered(row):
        return jnp.concatenate(
            [
                take_lanes(
                    [jnp.broadcast_to(t[row : row + 1], (8, 128)) for t in tables],
                    lane[8 * b : 8 * b + 8],
                    group[8 * b : 8 * b + 8],
                )
                for b in range(NB // 8)
            ],
            0,
        )

    off_x = gathered(0) - own[0:1]
    off_y = gathered(1) - own[1:2]
    step_z = gathered(2) - own[2:3]
    step_x = off_x - box_x * jnp.floor(off_x * (1.0 / box_x) + 0.5)
    step_y = off_y - box_y * jnp.floor(off_y * (1.0 / box_y) + 0.5)
    square = step_x * step_x + step_y * step_y + step_z * step_z
    shifted = square + SOFTEN
    inverse = lax.rsqrt(shifted)
    live = live_ref[...]
    inside = jnp.maximum(1.0 - square * (1.0 / (CUTOFF * CUTOFF)), 0.0)
    env = inside * inside * live
    ux, uy, uz = step_x * (1.0 / CUTOFF), step_y * (1.0 / CUTOFF), step_z * (1.0 / CUTOFF)
    geo_ref[0] = ux
    geo_ref[1] = uy
    geo_ref[2] = uz
    geo_ref[3] = jnp.sqrt(shifted)
    geo_ref[4] = env
    geo_ref[5] = inside * live * (-2.0 / (CUTOFF * CUTOFF))
    geo_ref[6] = 0.5 * env * inverse
    y_ref[0] = ux
    y_ref[1] = uy
    y_ref[2] = uz
    y_ref[3] = ux * uy
    y_ref[4] = uy * uz
    y_ref[5] = uz * ux
    y_ref[6] = ux * ux - uy * uy
    y_ref[7] = (2.0 * uz * uz - ux * ux - uy * uy) * (1.0 / ROOT_THREE)

    geo_ref[7] = gathered(3)
    emb = emb_ref[...].astype(BF16)
    kinds = lax.broadcasted_iota(jnp.int32, (8, WIDE_TILE), 0).astype(F32)
    for g in range(EDGES // WIDE_TILE):
        cols = slice(g * WIDE_TILE, (g + 1) * WIDE_TILE)
        f_ref[:, cols] = dot(emb, (kinds == flat(geo_ref, 7, g)).astype(F32).astype(BF16), TN).astype(BF16)
    f_out.send()
    radial(0, geo_ref, w1_ref, w2_ref, w3_ref, r_ref, None)
    r_out.send()

    def get_f(r0):
        return lambda n: f_ref[pl.ds(r0, 16), n * 128 : (n + 1) * 128].astype(F32)

    aggregate(r_ref, get_f, y_ref, a_ref)
    h_zero = dot(emb, (kinds[:, :128] == own[3:4]).astype(F32).astype(BF16), TN)
    h_one = h_zero + dot(mix_ref[0], invariants(a_ref))
    h_ref[...] = h_one
    send_rows(pick(h_one, ix_ref[...]), 32, 32, xa_ref, xb_ref)


def radial_kernel(geo_ref, w1_ref, w2_ref, w3_ref, r_ref):
    radial(1, geo_ref, w1_ref, w2_ref, w3_ref, r_ref, None)


def slope_kernel(geo_ref, w1_ref, w2_ref, w3_ref, nb_ref, p_out, p_zero_out, oh_out):
    radial(1, geo_ref, w1_ref, w2_ref, w3_ref, None, p_out.ref)
    p_out.send()
    radial(0, geo_ref, w1_ref, w2_ref, w3_ref, None, p_zero_out.ref)
    p_zero_out.send()
    fill_onehot(nb_ref, oh_out.ref)


def prepare_one_kernel(a_ref, r_in, p_in, f_in, y_ref, w_out, g_out, u_out):
    def arrived(block):
        for late in (r_in, p_in, f_in):
            late.ready(block)

    def ready(block):
        for out in (w_out, g_out, u_out):
            out.send(block)

    prepare(a_ref, r_in.ref, p_in.ref, f_in.ref, y_ref, w_out.ref, g_out.ref, u_out.ref, arrived, ready)


def prepare_zero_kernel(a_ref, r_in, p_in, f_in, y_ref, g_out, u_out):
    def arrived(block):
        for late in (r_in, p_in, f_in):
            late.ready(block)

    def ready(block):
        g_out.send(block)
        u_out.send(block)

    prepare(a_ref, r_in.ref, p_in.ref, f_in.ref, y_ref, None, g_out.ref, u_out.ref, arrived, ready)


def waves_kernel(box_x, box_y, rows_ref, wave_ref, cs_ref):
    own = rows_ref[...]
    x, y, z = own[0:1] * (1.0 / box_x), own[1:2] * (1.0 / box_y), own[2:3] * (1.0 / DEPTH_Z)
    turns = jnp.concatenate([x, y, z, jnp.zeros((5, ATOMS), F32)], 0)
    turns = turns - jnp.floor(turns)
    high = turns.astype(BF16).astype(F32)
    middle = (turns - high).astype(BF16).astype(F32)
    low = turns - high - middle
    parts = jnp.concatenate([high, middle, low, jnp.zeros((8, ATOMS), F32)], 0).astype(BF16)
    wave = wave_ref[...]
    wave = jnp.concatenate([wave, wave, wave, jnp.zeros((8, K), F32)], 0).astype(BF16)
    cs_ref[:, :K] = dot(parts, wave, TN)

    def tile(t, carry):
        cols = pl.ds(pl.multiple_of(t * 128, 128), 128)
        phase = cs_ref[:, cols]
        quarter = jnp.floor(4.0 * phase + 0.5)
        angle = (phase - 0.25 * quarter) * (2.0 * math.pi)
        sq = angle * angle
        sin = angle * (1.0 + sq * (-1.0 / 6 + sq * (1.0 / 120 + sq * (-1.0 / 5040 + sq * (1.0 / 362880)))))
        cos = 1.0 + sq * (-0.5 + sq * (1.0 / 24 + sq * (-1.0 / 720 + sq * (1.0 / 40320 - sq * (1.0 / 3628800)))))
        turn = quarter.astype(jnp.int32) & 3
        odd = (turn & 1) == 1
        c = jnp.where(odd, sin, cos)
        s = jnp.where(odd, cos, sin)
        c = jnp.where((turn == 1) | (turn == 2), -c, c)
        s = jnp.where(turn >= 2, -s, s)
        cs_ref[:, cols] = c
        cs_ref[:, pl.ds(pl.multiple_of(K + t * 128, 128), 128)] = s
        return carry

    lax.fori_loop(0, K // 128, tile, 0)


def feature_strip_kernel(h_ref, a_in, b_in, iy_ref, part_ref, ya_ref, yb_ref):
    part = received(a_in, b_in, 32)
    part_ref[...] = part
    send_rows(pick(jnp.concatenate([h_ref[...], part], 1), iy_ref[...]), 48, 64, ya_ref, yb_ref)


def second_kernel(
    h_ref, part_ref, a_in, b_in, nb_ref, y_ref, r_ref, cs_ref, mix_ref,
    w_charge_ref, geo_ref, a_zero_ref, f_out, a_out, h2_out, charge_out, s_ref, ypart_ref,
):
    f_ref, a_ref, h2_ref, charge_ref = f_out.ref, a_out.ref, h2_out.ref, charge_out.ref
    ypart_ref[...] = received(a_in, b_in, 64)

    def get_f(r0):
        rows = pl.ds(r0, 16)
        tables = [h_ref[rows, :], part_ref[rows, :], ypart_ref[rows, :]]

        def state(n):
            nb = jnp.broadcast_to(nb_ref[n : n + 1, :], (16, 128))
            f = take_lanes(tables, nb & 127, nb >> 7)
            f_ref[rows, n * 128 : (n + 1) * 128] = f.astype(BF16)
            return f

        return state

    aggregate(r_ref, get_f, y_ref, a_ref)
    f_out.send()
    a_out.send()
    h_two = h_ref[...] + dot(mix_ref[1], invariants(a_ref))
    h2_ref[...] = h_two
    charge = dot(w_charge_ref[...], h_two.astype(BF16))
    charge_ref[...] = charge
    h2_out.send()
    charge_out.send()
    q_hi, q_lo = split(charge)
    q_both = jnp.concatenate([q_hi, q_lo], 0)
    for t in range(TILES // 2):
        c_hi, c_lo = split(cs_ref[:, t * 256 : (t + 1) * 256])
        both = dot(q_both, c_hi)
        part = both[:KC] + (both[KC:] + dot(q_hi, c_lo))
        s_ref[2 * t * KC : (2 * t + 1) * KC, :] = part[:, :128]
        s_ref[(2 * t + 1) * KC : (2 * t + 2) * KC, :] = part[:, 128:]


def prepare(a_ref, r_ref, p_ref, f_ref, y_ref, w_ref, g_ref, u_ref, arrived=lambda block: None, ready=lambda block: None):
    count = NB // BLOCKS

    def block_of(block):
        def body(cc, carry):
            r0 = pl.multiple_of(cc * 16, 16)
            rows = pl.ds(r0, 16)
            late = [pl.ds(pl.multiple_of(l * 128 + r0, 16), 16) for l in range(3)]
            a = [a_ref[k, rows, :] for k in range(9)]
            for n in range(block * count, (block + 1) * count):
                cols = slice(n * 128, (n + 1) * 128)
                y = [2.0 * y_ref[m, n : n + 1, :] for m in range(8)]
                f = f_ref[rows, cols].astype(F32)
                r = [r_ref[late[l], cols].astype(F32) for l in range(3)]
                q1 = a[1] * y[0] + a[2] * y[1] + a[3] * y[2]
                q2 = a[4] * y[3] + a[5] * y[4] + a[6] * y[5] + a[7] * y[6] + a[8] * y[7]
                g_ref[late[0], cols] = (f * r[1]).astype(BF16)
                g_ref[late[1], cols] = (f * r[2]).astype(BF16)
                u_ref[late[0], cols] = (f * p_ref[late[0], cols].astype(F32)).astype(BF16)
                u_ref[late[1], cols] = (f * q1 * p_ref[late[1], cols].astype(F32)).astype(BF16)
                u_ref[late[2], cols] = (f * q2 * p_ref[late[2], cols].astype(F32)).astype(BF16)
                if w_ref is not None:
                    w_ref[late[0], cols] = r_ref[late[0], cols]
                    w_ref[late[1], cols] = (q1 * r[1]).astype(BF16)
                    w_ref[late[2], cols] = (q2 * r[2]).astype(BF16)
            return carry

        lax.fori_loop(0, 8, body, 0)

    for block in range(BLOCKS):
        arrived(block)
        block_of(block)
        ready(block)


TOGETHER = 3


def backward(ginv_ref, ga_ref, w_ref, g_ref, u_ref, gf_ref, t_ref, arrived=lambda block: None):
    def body(b, carry):
        acc = [[jnp.zeros((8, 128), F32) for _ in range(9)] for _ in range(TOGETHER)]
        for cc in range(8):
            rows = slice(cc * 16, cc * 16 + 16)
            late = [slice(l * 128 + cc * 16, l * 128 + cc * 16 + 16) for l in range(3)]
            gi = [ginv_ref[late[l], :] for l in range(3)]
            ga = [ga_ref[k, rows, :] for k in range(8)]
            for j in range(TOGETHER):
                cols = pl.ds(pl.multiple_of((b * TOGETHER + j) * 128, 128), 128)
                if gf_ref is not None:
                    w = [w_ref[late[l], cols].astype(F32) for l in range(3)]
                    gf_ref[rows, cols] = (gi[0] * w[0] + gi[1] * w[1] + gi[2] * w[2]).astype(BF16)
                u = [u_ref[late[l], cols].astype(F32) for l in range(3)]
                g1, g2 = g_ref[late[0], cols].astype(F32), g_ref[late[1], cols].astype(F32)
                terms = [gi[0] * u[0] + gi[1] * u[1] + gi[2] * u[2]]
                terms += [g1 * ga[m] for m in range(3)] + [g2 * ga[m] for m in range(3, 8)]
                acc[j] = [old + (new[:8] + new[8:]) for old, new in zip(acc[j], terms)]
        for j in range(TOGETHER):
            for k in range(9):
                t_ref[k, pl.ds(b * TOGETHER + j, 1), :] = jnp.sum(acc[j][k], 0, keepdims=True)
        return carry

    count = NB // TOGETHER // BLOCKS
    for block in range(BLOCKS):
        arrived(block)
        lax.fori_loop(block * count, (block + 1) * count, body, 0)


def pull_invariants(g_inv, a_ref, ginv_ref, ga_ref):
    ginv_ref[...] = g_inv
    for k in range(1, 4):
        ga_ref[k - 1] = 2.0 * a_ref[k] * g_inv[C : 2 * C]
    for k in range(4, 9):
        ga_ref[k - 1] = 2.0 * a_ref[k] * g_inv[2 * C :]


def fill_onehot(nb_ref, oh_ref):
    for n in range(NB):
        oh_ref[:, n * 128 : (n + 1) * 128] = onehot_columns(nb_ref[n : n + 1, :], TABLE, BF16)


def ewald_kernel(
    box_x, box_y, scale, s_ref, spectral_ref, cs_ref, wave_ref, charge_ref, h_in, h2_in, a_in, w_in, g_in, u_in,
    oh_in, mix_in, first_in, last_in, read_hidden_in, w_charge_in,
    energy_ref, gpos_ref, gown_ref, gpart_ref, ya_ref, yb_ref, t_ref, ginv_ref, ga_ref, gf_ref, gphase_ref,
):
    charge = charge_ref[...]
    qt_hi, qt_lo = split(charge.T)
    q_three = jnp.concatenate([qt_hi.astype(F32), qt_lo.astype(F32), qt_hi.astype(F32)], 1).astype(BF16)
    total = jnp.zeros((2 * KC, 2 * ATOMS), F32)
    for t in range(TILES // 2):
        cols = slice(t * 128, (t + 1) * 128)
        late = slice(K + t * 128, K + (t + 1) * 128)
        filt = spectral_ref[:, cols] * scale
        gc = filt * s_ref[t * KC : (t + 1) * KC, :]
        gs = filt * s_ref[(TILES // 2 + t) * KC : (TILES // 2 + t + 1) * KC, :]
        cos, sin = cs_ref[:, cols], cs_ref[:, late]
        g_hi, g_lo = split(jnp.concatenate([gc, gs], 1))
        c_hi, c_lo = split(jnp.concatenate([cos, sin], 1))
        total = total + dot(jnp.concatenate([g_hi, g_lo], 0), jnp.concatenate([c_hi, c_lo], 0), NT)
        phase = dot(q_three, jnp.concatenate([g_hi, g_hi, g_lo], 0))
        p_hi, p_lo = split(phase[:, 128:] * cos - phase[:, :128] * sin)
        gphase_ref[:ATOMS, cols] = p_hi
        gphase_ref[ATOMS:, cols] = p_lo
    potential = total[:KC, :ATOMS] + (total[KC:, :ATOMS] + total[:KC, ATOMS:])
    wave = jnp.concatenate([wave_ref[...].astype(F32), jnp.zeros((5, K), F32)], 0).astype(BF16)
    gpos = dot(wave, gphase_ref[...], NT)
    gpos = gpos[:, :ATOMS] + gpos[:, ATOMS:]
    gpos_ref[...] = jnp.concatenate(
        [
            gpos[0:1] * (2.0 * math.pi / box_x),
            gpos[1:2] * (2.0 * math.pi / box_y),
            gpos[2:3] * (2.0 * math.pi / DEPTH_Z),
            jnp.zeros((5, ATOMS), F32),
        ],
        0,
    )
    h_ref, h2_ref, first_ref, last_ref = h_in.ready(), h2_in.ready(), first_in.ready(), last_in.ready()
    read_hidden_ref, w_charge_ref, mix_ref = read_hidden_in.ready(), w_charge_in.ready(), mix_in.ready()
    h_two = h2_ref[...].astype(BF16)
    z = dot(read_hidden_ref[...], h_two)
    s, hidden = gate(z)
    last = jnp.broadcast_to(last_ref[...], (128, last_ref.shape[1])).T
    first = jnp.broadcast_to(first_ref[...], (128, 128)).T
    site = jnp.sum(first * h_ref[...], 0, keepdims=True) + jnp.sum(last * hidden, 0, keepdims=True)
    energy_ref[...] = site + 0.5 * jnp.sum(charge * potential, 0, keepdims=True)
    g_hidden = (last * gate_slope(z, s)).astype(BF16)
    g_two = dot(w_charge_ref[...], potential.astype(BF16), TN) + dot(read_hidden_ref[...], g_hidden, TN)
    g_two = g_two.astype(BF16)
    g_inv = dot(mix_ref[1], g_two, TN).astype(BF16).astype(F32)
    pull_invariants(g_inv, a_in.ready(), ginv_ref, ga_ref)

    def arrived(block):
        for late in (w_in, g_in, u_in):
            late.ready(block)

    backward(ginv_ref, ga_ref, w_in.ref, g_in.ref, u_in.ref, gf_ref, t_ref, arrived)
    oh_ref = oh_in.ready()
    grads = dot(gf_ref[...], oh_ref[...], NT)
    gown_ref[...] = grads[:, :128] + g_two.astype(F32) + first
    gpart_ref[...] = grads[:, 128:256]
    send_rows(grads[:, 256:], 48, 64, ya_ref, yb_ref)


def return_features_kernel(gown_ref, gpart_ref, a_in, b_in, iy_ref, own_ref, xa_ref, xb_ref):
    back = give_back(received(a_in, b_in, 64), iy_ref[...], 256)
    own_ref[...] = gown_ref[...] + back[:, :128]
    send_rows(gpart_ref[...] + back[:, 128:], 32, 32, xa_ref, xb_ref)


def return_y_kernel(gown_ref, gpart_ref, a_in, b_in, iy_ref, own_ref, part_ref):
    back = give_back(merge(a_in[...], b_in[...], 64), iy_ref[...], 256)
    own_ref[...] = gown_ref[...] + back[:, :128]
    part_ref[...] = gpart_ref[...] + back[:, 128:]


def last_kernel(
    gown_ref, a_in, b_in, ix_ref, mix_ref, a_ref, g_ref, u_ref, t1_ref, geo_ref, oh_ref, gpos_ref,
    own_ref, part_ref, gy_ref, ginv_ref, ga_ref, t_ref, rows_ref,
):
    g_one = gown_ref[...] + give_back(received(a_in, b_in, 32), ix_ref[...], 128)
    g_inv = dot(mix_ref[0], g_one.astype(BF16), TN).astype(BF16).astype(F32)
    pull_invariants(g_inv, a_ref, ginv_ref, ga_ref)
    backward(ginv_ref, ga_ref, None, g_ref, u_ref, None, t_ref)
    t = [t_ref[k] + t1_ref[k] for k in range(9)]
    ux, uy, uz = geo_ref[0], geo_ref[1], geo_ref[2]
    root = 2.0 / ROOT_THREE
    gx = t[1] + t[4] * uy + t[6] * uz + ux * (2.0 * t[7] - root * t[8])
    gy = t[2] + t[4] * ux + t[5] * uz - uy * (2.0 * t[7] + root * t[8])
    gz = t[3] + t[5] * uy + t[6] * ux + (2.0 * root) * uz * t[8]
    steps = [g * (1.0 / CUTOFF) + (2.0 * CUTOFF) * u * t[0] for g, u in ((gx, ux), (gy, uy), (gz, uz))]
    rows_ref[...] = jnp.zeros(rows_ref.shape, F32)
    for k in range(3):
        high = steps[k].astype(BF16).astype(F32)
        low = steps[k] - high
        for n in range(NB):
            rows_ref[k : k + 1, n * 128 : (n + 1) * 128] = high[n : n + 1]
            rows_ref[8 + k : 9 + k, n * 128 : (n + 1) * 128] = low[n : n + 1]
    both = dot(rows_ref[...].astype(BF16), oh_ref[...], NT)
    grads = both[:8] + both[8:]
    centre = jnp.concatenate([jnp.sum(g, 0, keepdims=True) for g in steps] + [jnp.zeros((5, 128), F32)], 0)
    own_ref[...] = grads[:, :128] - centre + gpos_ref[...]
    part_ref[...] = grads[:, 128:256]
    gy_ref[...] = grads[:, 256:]


def final_kernel(own_ref, a_in, b_in, ix_ref, out_ref):
    total = own_ref[...] + give_back(merge(a_in[...], b_in[...], 32), ix_ref[...], 128)
    out_ref[...] = -total[:3]


def sum_kernel(pieces, copies, in_ref, out_ref):
    out_ref = getattr(out_ref, "ref", out_ref)
    rows = in_ref.shape[0] // pieces
    total = in_ref[0:rows, :]
    for g in range(1, pieces):
        total = total + in_ref[g * rows : (g + 1) * rows, :]
    for g in range(copies):
        out_ref[g * rows : (g + 1) * rows, :] = total


class Far:
    def __init__(self, array, late=False, blocks=1):
        self.array = array
        self.late = late
        self.blocks = blocks


class Late:
    def __init__(self, copies, ref):
        self.copies = copies
        self.ref = ref

    def ready(self, block=0):
        self.copies[block].wait()
        return self.ref


class Out:
    def __init__(self, copies, ref):
        self.copies = copies
        self.ref = ref
        self.sent = set()

    def send(self, block=0):
        self.copies[block].start()
        self.sent.add(block)

    def finish(self):
        for block in range(len(self.copies)):
            if block not in self.sent:
                self.send(block)


def column_copies(source, target, blocks, sems):
    if blocks == 1:
        return [pltpu.make_async_copy(source, target, next(sems))]
    width = source.shape[1] // blocks
    cols = [pl.ds(b * width, width) for b in range(blocks)]
    return [pltpu.make_async_copy(source.at[:, c], target.at[:, c], next(sems)) for c in cols]


def call(kernel, outs, *operands, scratch=(), flops=0, moved=0):
    n_in, n_out = len(operands), len(outs)
    far_in = [i for i, o in enumerate(operands) if isinstance(o, Far)]
    far_out = [i for i, o in enumerate(outs) if len(o) in (3, 5)]
    forwarded = [i for i, o in enumerate(outs) if len(o) == 4]
    arrays = [pltpu.with_memory_space_constraint(o.array, pltpu.HBM) if isinstance(o, Far) else o for o in operands]
    n_far = len(far_in) + len(far_out)
    n_sems = sum(operands[i].blocks for i in far_in) + BLOCKS * len(far_out) + len(forwarded)
    buffers = [pltpu.VMEM(arrays[i].shape, arrays[i].dtype) for i in far_in]
    buffers += [pltpu.VMEM(outs[i][0], outs[i][1]) for i in far_out]

    def wrapped(*refs):
        ins, results, rest = list(refs[:n_in]), list(refs[n_in : n_in + n_out]), refs[n_in + n_out :]
        own, held = rest[: len(scratch)], rest[len(scratch) : len(scratch) + n_far]
        sems = rest[-1]
        waits, later, sent = [], [], []
        sem = (sems.at[k] for k in range(n_sems))
        for k, i in enumerate(far_in):
            copies = column_copies(ins[i], held[k], operands[i].blocks, sem)
            if operands[i].late:
                big = len(copies) == 1 and math.prod(held[k].shape) > 10**6
                later += [(BLOCKS if big else b, copy) for b, copy in enumerate(copies)]
                ins[i] = Late(copies, held[k])
            else:
                copies[0].start()
                waits.append(copies[0])
                ins[i] = held[k]
        for _, copy in sorted(later, key=lambda item: item[0]):
            copy.start()
        for k, i in enumerate(far_out, len(far_in)):
            blocks = outs[i][4] if len(outs[i]) == 5 else 1
            results[i] = Out(column_copies(held[k], results[i], blocks, sem), held[k])
            sent.append(results[i])
        for copy in waits:
            copy.wait()
        for i in forwarded:
            out = Out(column_copies(ins[outs[i][3]], results[i], 1, sem), None)
            out.send()
            sent.append(out)
        kernel(*ins, *[r for i, r in enumerate(results) if i not in forwarded], *own)
        for out in sent:
            out.finish()
        for out in sent:
            for copy in out.copies:
                copy.wait()

    def place_of(far):
        return pl.BlockSpec(memory_space=pltpu.HBM if far else pltpu.VMEM)

    return pl.pallas_call(
        wrapped,
        out_shape=[pltpu.HBM(o[0], o[1]) if len(o) > 2 else jax.ShapeDtypeStruct(o[0], o[1]) for o in outs],
        in_specs=[place_of(isinstance(o, Far)) for o in operands],
        out_specs=[place_of(len(o) > 2) for o in outs],
        scratch_shapes=[pltpu.VMEM(s, d) for s, d in scratch] + buffers + [pltpu.SemaphoreType.DMA((max(n_sems, 1),))],
        compiler_params=pltpu.CompilerParams(vmem_limit_bytes=24 * 1024 * 1024),
        cost_estimate=pl.CostEstimate(flops=flops, bytes_accessed=moved, transcendentals=0),
    )(*arrays)


def swap(value, axes, of):
    count = 1
    for axis in axes:
        count *= lax.axis_size(axis)
    return lax.ppermute(value, axes, [(i, of(i)) for i in range(count)])


BX = ("xh", "co")
CELL = ("y", "z", "xl")


def swap_x(a, b):
    return swap(a, BX, lambda i: i ^ 1), swap(b, BX, lambda i: i ^ 3)


def swap_y(a, b):
    def other(c):
        return (c - 1) % 64 if c % 2 == 0 else (c + 1) % 64

    return swap(a, CELL, lambda c: c ^ 1), swap(b, CELL, other)


def body(
    positions, species, send_x, send_y, neighbours, live_slots, embedding, radial_in, radial_mid, radial_out, mixing,
    read_first, read_hidden, read_last, w_charge, spectral, wave_ids,
):
    count_x = lax.axis_size("xh") * lax.axis_size("co")
    count_y = lax.axis_size("y") * lax.axis_size("z") * lax.axis_size("xl")
    box_x = count_x * WIDTH_X
    box_y = count_y * WIDTH_Y
    scale = 1.0 / math.sqrt(K * ATOMS * count_x * count_y)
    small = ((8, 128), F32)
    square = ((C, 128), F32)
    edge3 = ((3 * C, EDGES), BF16)
    index = ((1, 128), jnp.int32)
    strip_32, strip_48 = ((32, 128), F32), ((48, 128), F32)
    w1, w3, emb = radial_in.swapaxes(1, 2).astype(F32), radial_out.swapaxes(1, 2), embedding.T.astype(F32)

    with_box = functools.partial

    rows, ix, strip = call(strip_x_kernel, [small, index, small], Far(positions), Far(species[None]), Far(send_x))
    xa, xb = swap_x(strip, strip)
    nb, live, emb, *near_nets, mix_near, wave = call(
        fetch_kernel,
        [((NB, 128), jnp.int32), ((NB, 128), F32), ((8, C), F32), (w1.shape, F32), (radial_mid.shape, BF16), (radial_out.shape, BF16), (mixing.shape, BF16), ((8, K), F32)],
        Far(neighbours), Far(live_slots), emb, w1, Far(radial_mid), Far(w3), Far(mixing), Far(wave_ids), flops=10**8, moved=10**6,
    )
    xa, xb, nb, live, emb, near_nets, mix_near, wave = lax.optimization_barrier((xa, xb, nb, live, emb, near_nets, mix_near, wave))
    part, iy, strip = call(strip_y_kernel, [small, index, small], rows, xa, xb, Far(send_y))
    ya, yb = swap_y(strip, strip)
    nets = (Far(w1), Far(radial_mid), Far(w3))
    ylm_shape, a_shape, cs_shape = ((8, NB, 128), F32), ((9, C, 128), F32), ((ATOMS, 2 * K), F32)
    geo, ylm, f_zero, r_zero, a_zero, h_one, xa, xb = call(
        with_box(first_kernel, box_x, box_y),
        [ylm_shape, ylm_shape, ((C, EDGES), BF16, True), edge3 + (True,), a_shape, square, strip_32, strip_32],
        rows, part, ya, yb, nb, live, ix, emb, *near_nets, mix_near,
    )
    rows_later, _, _ = lax.optimization_barrier((rows, xa, xb))
    xa, xb = swap_x(xa, xb)
    (cs,) = call(with_box(waves_kernel, box_x, box_y), [cs_shape], rows_later, wave, flops=10**8, moved=10**6)
    xa, xb, cs = lax.optimization_barrier((xa, xb, cs))
    fpart, ya, yb = call(feature_strip_kernel, [square, strip_48, strip_48], h_one, xa, xb, iy)
    geo_soon, _, _ = lax.optimization_barrier((geo, ya, yb))
    ya, yb = swap_y(ya, yb)
    (r_one,) = call(radial_kernel, [edge3], geo_soon, *near_nets, flops=5 * 10**8, moved=10**7)
    f_one, a_one, h_two, charge, s_part, h_far, ylm, r_far, cs, geo, a_zero = call(
        second_kernel,
        [
            ((C, EDGES), BF16, True), a_shape + (True,), square + (True,), ((KC, ATOMS), F32, True), ((TILES * KC, 128), F32),
            square + (True, 0), ylm_shape + (True, 5), edge3 + (True, 6), cs_shape + (True, 7), ylm_shape + (True, 10),
            a_shape + (True, 11),
        ],
        h_one, fpart, ya, yb, nb, ylm, r_one, cs, mix_near, w_charge, geo, a_zero,
        scratch=[square],
    )
    late = lambda array: Far(array, True)
    edge2 = ((2 * C, EDGES), BF16)
    blocked = (True, None, BLOCKS)
    geo_later, _ = lax.optimization_barrier((geo, s_part))
    p_one, p_zero, oh = call(
        slope_kernel, [edge3 + (True,), edge3 + (True,), ((TABLE, EDGES), BF16, True)], Far(geo_later), *nets, Far(nb), flops=10**9, moved=2 * 10**7
    )
    rows_each = s_part.shape[0] // NWIDE
    pieces = lax.all_to_all(s_part, WIDE, 0, 0, tiled=True)
    pieces, p_one, p_zero, oh = lax.optimization_barrier((pieces, p_one, p_zero, oh))
    (mine,) = call(functools.partial(sum_kernel, NWIDE, 8), [((8 * rows_each, 128), F32)], pieces)
    a_later, _ = lax.optimization_barrier((a_zero, mine))
    g_zero, u_zero = call(
        prepare_zero_kernel, [edge2 + blocked, edge3 + blocked],
        Far(a_later), Far(r_zero, True, BLOCKS), Far(p_zero, True, BLOCKS), Far(f_zero, True, BLOCKS), Far(ylm), flops=10**9, moved=2 * 10**7,
    )
    mine = lax.all_to_all(mine, ("z",), 0, 0, tiled=True)
    mine, g_zero, u_zero = lax.optimization_barrier((mine, g_zero, u_zero))
    (spread,) = call(functools.partial(sum_kernel, 8, NWIDE), [((NWIDE * rows_each, 128), F32, True)], mine)
    a_later, _ = lax.optimization_barrier((a_one, spread))
    w_one, g_one, u_one = call(
        prepare_one_kernel, [edge3 + blocked, edge2 + blocked, edge3 + blocked],
        Far(a_later), Far(r_far, True, BLOCKS), Far(p_one, True, BLOCKS), Far(f_one, True, BLOCKS), Far(ylm), flops=10**9, moved=2 * 10**7,
    )
    s_all = lax.all_to_all(spread, WIDE, 0, 0, tiled=True)
    s_all, w_one, g_one, u_one = lax.optimization_barrier((s_all, w_one, g_one, u_one))
    energy, gpos, gown, gpart, ya, yb, t_one = call(
        with_box(ewald_kernel, box_x, box_y, scale),
        [((1, 128), F32), small, square, square, strip_48, strip_48, ((9, NB, 128), F32)],
        s_all, Far(spectral), Far(cs), Far(wave_ids), Far(charge), late(h_far), late(h_two), late(a_one),
        Far(w_one, True, BLOCKS), Far(g_one, True, BLOCKS), Far(u_one, True, BLOCKS), late(oh), late(mixing), late(read_first[None]), late(read_last[None]), late(read_hidden),
        late(w_charge),
        scratch=[((3 * C, 128), F32), ((8, C, 128), F32), ((C, EDGES), BF16), ((2 * ATOMS, K), BF16)],
    )
    ya, yb = swap_y(ya, yb)
    gown, xa, xb = call(return_features_kernel, [square, strip_32, strip_32], gown, gpart, ya, yb, iy)
    xa, xb = swap_x(xa, xb)
    own, part, gy = call(
        last_kernel,
        [small, small, small],
        gown, xa, xb, ix, mixing, a_zero, g_zero, u_zero, t_one, geo, oh, gpos,
        scratch=[((3 * C, 128), F32), ((8, C, 128), F32), ((9, NB, 128), F32), ((16, EDGES), F32)],
    )
    ya, yb = swap_y(gy, gy)
    own, part = call(return_y_kernel, [small, small], own, part, ya, yb, iy)
    xa, xb = swap_x(part, part)
    (forces,) = call(final_kernel, [((3, ATOMS), F32)], own, xa, xb, ix)
    return energy[0], forces


def solution(mesh):
    fine = Mesh(mesh.devices.reshape(2, 2, 4, 8, 2), AXES)
    rows, columns = P(AXES), P(None, AXES)
    placed = (columns, rows) + (columns,) * 4 + (P(),) * 11
    return jax.shard_map(body, mesh=fine, in_specs=placed, out_specs=(rows, columns), check_vma=False)
```

```python
import functools
import math

import jax
import jax.numpy as jnp
from jax import lax
from jax.experimental import pallas as pl
from jax.experimental.pallas import tpu as pltpu
from jax.sharding import Mesh, PartitionSpec as P

CUTOFF = 4.0
SOFTEN = 0.25
WIDTH_X = 16.0
WIDTH_Y = 16.0
DEPTH_Z = 16.0
ACT_GAIN = 1.679
ROOT_THREE = math.sqrt(3.0)
HIGHEST = lax.Precision.HIGHEST
F32 = jnp.float32
BF16 = jnp.bfloat16

C = 128
NB = 24
ATOMS = 128
EDGES = NB * ATOMS
TABLE = 384
NBASIS = 8
BLOCKS = 4
K = 1024
KC = 64
TILES = 2 * K // 128
AXES = ("xh", "co", "y", "z", "xl")
WIDE = ("xh", "co", "y", "xl")
NWIDE = 32

NN = (((1,), (0,)), ((), ()))
NT = (((1,), (1,)), ((), ()))
TN = (((0,), (0,)), ((), ()))


def dot(a, b, dims=NN, precision=None):
    return lax.dot_general(a, b, dims, precision=precision, preferred_element_type=F32)


def split(a):
    high = a.astype(BF16)
    return high, (a - high.astype(F32)).astype(BF16)


def dot3(a, b, dims=NN):
    a_hi, a_lo = split(a)
    b_hi, b_lo = split(b)
    return dot(a_hi, b_hi, dims) + (dot(a_lo, b_hi, dims) + dot(a_hi, b_lo, dims))


def gate(v):
    s = 0.5 + 0.5 * jnp.tanh(0.5 * v)
    return s, (ACT_GAIN * v) * s


def gate_slope(v, s):
    return ACT_GAIN * s * (1.0 + v * (1.0 - s))


def onehot_columns(index_row, count, dtype):
    rows = lax.broadcasted_iota(jnp.int32, (count, index_row.shape[1]), 0)
    return (rows == index_row).astype(F32).astype(dtype)


def merge(a, b, split_lane):
    lane = lax.broadcasted_iota(jnp.int32, a.shape, 1)
    return jnp.where(lane < split_lane, a, b)


def pick(values, index_row):
    return dot(values, onehot_columns(index_row, values.shape[1], F32), NN, HIGHEST)


def give_back(grads, index_row, count):
    return dot(grads, onehot_columns(index_row, count, F32), NT, HIGHEST)


def send_rows(values, count, gap, a_ref, b_ref):
    rows = values.T
    a_ref[...] = rows[:count]
    b_ref[...] = rows[gap : gap + count]


def received(a_ref, b_ref, gap):
    a, b = a_ref[...], b_ref[...]
    pieces = [a, b, jnp.zeros((128 - gap - b.shape[0], 128), F32)]
    if gap > a.shape[0]:
        pieces.insert(1, jnp.zeros((gap - a.shape[0], 128), F32))
    return jnp.concatenate(pieces, 0).T


def place(index):
    px, py = lax.axis_index("co"), lax.axis_index("xl")
    far = jnp.where(index < 240, index + (128 - 64 * py), index + (16 + 64 * py))
    near = jnp.where(index < 160, index + (32 - 32 * px), index + (32 * px - 32))
    return jnp.where(index < 128, index, jnp.where(index < 192, near, far))


def strip_x_kernel(pos_ref, species_ref, send_ref, rows_ref, ix_ref, out_ref):
    odd = lax.axis_index("co")
    lower, upper = send_ref[0:1, :], send_ref[1:2, :]
    first = upper + (lower - upper) * odd
    second = lower + (upper - lower) * odd
    index = jnp.concatenate([first, second, jnp.full((1, 64), -1, jnp.int32)], 1)
    rows = jnp.concatenate([pos_ref[...], species_ref[...].astype(F32), jnp.zeros((4, ATOMS), F32)], 0)
    ix_ref[...] = index
    rows_ref[...] = rows
    out_ref[...] = pick(rows, index)


def strip_y_kernel(rows_ref, a_ref, b_ref, send_ref, part_ref, iy_ref, out_ref):
    odd = lax.axis_index("xl")
    send = place(send_ref[...])
    lower, upper = send[0:1], send[1:2]
    first = upper + (lower - upper) * odd
    second = lower + (upper - lower) * odd
    none = jnp.full((1, 16), -1, jnp.int32)
    index = jnp.concatenate([first, none, second, none], 1)
    part = merge(a_ref[...], b_ref[...], 32)
    part_ref[...] = part
    iy_ref[...] = index
    out_ref[...] = pick(jnp.concatenate([rows_ref[...], part], 1), index)


WIDE_TILE = 1024


def flat(ref, k, g):
    count = WIDE_TILE // 128
    return jnp.concatenate([ref[k, count * g + j : count * g + j + 1, :] for j in range(count)], 1)


def radial(layer, geo_ref, w1_ref, w2_ref, w3_ref, r_ref, p_ref):
    w1 = w1_ref[layer].astype(BF16)
    w2 = w2_ref[layer]
    w3 = w3_ref[layer]
    if w3.shape[0] < w3.shape[1]:
        w3 = w3.astype(F32).T.astype(BF16)
    spacing = CUTOFF / (NBASIS - 1)
    centre = lax.broadcasted_iota(jnp.int32, (NBASIS, WIDE_TILE), 0).astype(F32) * spacing
    for g in range(EDGES // WIDE_TILE):
        cols = slice(g * WIDE_TILE, (g + 1) * WIDE_TILE)
        gap = (flat(geo_ref, 3, g) - centre) * (1.0 / spacing)
        basis = jnp.exp(-gap * gap)
        z1 = dot(w1, basis.astype(BF16), TN)
        s1, h1 = gate(z1)
        z2 = dot(w2, h1.astype(BF16))
        s2, h2 = gate(z2)
        if r_ref is not None:
            r_ref[:, cols] = dot(w3, (h2 * flat(geo_ref, 4, g)).astype(BF16)).astype(BF16)
        if p_ref is not None:
            slope = basis * gap * (-2.0 / spacing)
            h1p = gate_slope(z1, s1) * dot(w1, slope.astype(BF16), TN)
            h2p = gate_slope(z2, s2) * dot(w2, h1p.astype(BF16))
            mixed = h2p * flat(geo_ref, 6, g) + h2 * flat(geo_ref, 5, g)
            p_ref[:, cols] = dot(w3, mixed.astype(BF16)).astype(BF16)


def aggregate(r_ref, get_f, y_ref, a_ref):
    def body(cc, carry):
        r0 = pl.multiple_of(cc * 16, 16)
        acc = [jnp.zeros((16, 128), F32) for _ in range(9)]
        state = get_f(r0)
        for n in range(NB):
            cols = slice(n * 128, (n + 1) * 128)
            f = state(n)
            g0 = r_ref[pl.ds(r0, 16), cols].astype(F32) * f
            g1 = r_ref[pl.ds(128 + r0, 16), cols].astype(F32) * f
            g2 = r_ref[pl.ds(256 + r0, 16), cols].astype(F32) * f
            acc[0] = acc[0] + g0
            for m in range(3):
                acc[1 + m] = acc[1 + m] + g1 * y_ref[m, n : n + 1, :]
            for m in range(5):
                acc[4 + m] = acc[4 + m] + g2 * y_ref[3 + m, n : n + 1, :]
        for k in range(9):
            a_ref[k, pl.ds(r0, 16), :] = acc[k]
        return carry

    lax.fori_loop(0, 8, body, 0)


def invariants(a_ref):
    a1 = a_ref[1] * a_ref[1] + a_ref[2] * a_ref[2] + a_ref[3] * a_ref[3]
    a2 = a_ref[4] * a_ref[4] + a_ref[5] * a_ref[5] + a_ref[6] * a_ref[6]
    a2 = a2 + a_ref[7] * a_ref[7] + a_ref[8] * a_ref[8]
    return jnp.concatenate([a_ref[0].astype(BF16), a1.astype(BF16), a2.astype(BF16)], 0)


def take_lanes(tables, lane, group):
    got = [jnp.take_along_axis(t, lane, axis=1, mode="promise_in_bounds") for t in tables]
    return jnp.where(group == 0, got[0], jnp.where(group == 1, got[1], got[2]))


def fetch_kernel(nb_ref, live_ref, emb_ref, w1_ref, w2_ref, w3_ref, mix_ref, wave_ref, send_ref, nb_out, live_out, emb_out, w1_out, w2_out, w3_out, mix_out, wave_out, send_out):
    send_out[...] = send_ref[...]
    wave_out[...] = jnp.concatenate([wave_ref[...].astype(F32), jnp.zeros((5, K), F32)], 0)
    nb_out[...] = place(nb_ref[...])
    live_out[...] = live_ref[...].astype(F32)
    emb_out[...] = jnp.concatenate([emb_ref[...], jnp.zeros((8 - emb_ref.shape[0], C), F32)], 0)
    w1_out[...] = w1_ref[...]
    w2_out[...] = w2_ref[...]
    mix_out[...] = mix_ref[...]
    for layer in range(2):
        w3_out[layer] = w3_ref[layer].astype(F32).T.astype(BF16)


def first_kernel(
    box_x, box_y, rows_ref, part_ref, a_in, b_in, nb_ref, live_ref, ix_ref, emb_ref, w1_ref, w2_ref,
    w3_ref, mix_ref, geo_ref, y_ref, f_out, r_out, a_ref, h_ref, xa_ref, xb_ref,
):
    f_ref, r_ref = f_out.ref, r_out.ref
    own = rows_ref[...]
    tables = [own, part_ref[...], merge(a_in[...], b_in[...], 64)]
    nb = nb_ref[...]
    lane, group = nb & 127, nb >> 7

    def gathered(row):
        return jnp.concatenate(
            [
                take_lanes(
                    [jnp.broadcast_to(t[row : row + 1], (8, 128)) for t in tables],
                    lane[8 * b : 8 * b + 8],
                    group[8 * b : 8 * b + 8],
                )
                for b in range(NB // 8)
            ],
            0,
        )

    off_x = gathered(0) - own[0:1]
    off_y = gathered(1) - own[1:2]
    step_z = gathered(2) - own[2:3]
    step_x = off_x - box_x * jnp.floor(off_x * (1.0 / box_x) + 0.5)
    step_y = off_y - box_y * jnp.floor(off_y * (1.0 / box_y) + 0.5)
    square = step_x * step_x + step_y * step_y + step_z * step_z
    shifted = square + SOFTEN
    inverse = lax.rsqrt(shifted)
    live = live_ref[...]
    inside = jnp.maximum(1.0 - square * (1.0 / (CUTOFF * CUTOFF)), 0.0)
    env = inside * inside * live
    ux, uy, uz = step_x * (1.0 / CUTOFF), step_y * (1.0 / CUTOFF), step_z * (1.0 / CUTOFF)
    geo_ref[0] = ux
    geo_ref[1] = uy
    geo_ref[2] = uz
    geo_ref[3] = jnp.sqrt(shifted)
    geo_ref[4] = env
    geo_ref[5] = inside * live * (-2.0 / (CUTOFF * CUTOFF))
    geo_ref[6] = 0.5 * env * inverse
    y_ref[0] = ux
    y_ref[1] = uy
    y_ref[2] = uz
    y_ref[3] = ux * uy
    y_ref[4] = uy * uz
    y_ref[5] = uz * ux
    y_ref[6] = ux * ux - uy * uy
    y_ref[7] = (2.0 * uz * uz - ux * ux - uy * uy) * (1.0 / ROOT_THREE)

    geo_ref[7] = gathered(3)
    emb = emb_ref[...].astype(BF16)
    kinds = lax.broadcasted_iota(jnp.int32, (8, WIDE_TILE), 0).astype(F32)
    for g in range(EDGES // WIDE_TILE):
        cols = slice(g * WIDE_TILE, (g + 1) * WIDE_TILE)
        f_ref[:, cols] = dot(emb, (kinds == flat(geo_ref, 7, g)).astype(F32).astype(BF16), TN).astype(BF16)
    f_out.send()
    radial(0, geo_ref, w1_ref, w2_ref, w3_ref, r_ref, None)
    r_out.send()

    def get_f(r0):
        return lambda n: f_ref[pl.ds(r0, 16), n * 128 : (n + 1) * 128].astype(F32)

    aggregate(r_ref, get_f, y_ref, a_ref)
    h_zero = dot(emb, (kinds[:, :128] == own[3:4]).astype(F32).astype(BF16), TN)
    h_one = h_zero + dot(mix_ref[0], invariants(a_ref))
    h_ref[...] = h_one
    send_rows(pick(h_one, ix_ref[...]), 32, 32, xa_ref, xb_ref)


def radial_kernel(geo_ref, w1_ref, w2_ref, w3_ref, r_ref):
    radial(1, geo_ref, w1_ref, w2_ref, w3_ref, r_ref, None)


def slope_kernel(geo_ref, w1_ref, w2_ref, w3_ref, nb_ref, p_out, p_zero_out, oh_out):
    radial(1, geo_ref, w1_ref, w2_ref, w3_ref, None, p_out.ref)
    p_out.send()
    radial(0, geo_ref, w1_ref, w2_ref, w3_ref, None, p_zero_out.ref)
    p_zero_out.send()
    fill_onehot(nb_ref, oh_out.ref)


def prepare_one_kernel(a_ref, r_in, p_in, f_in, y_ref, w_out, g_out, u_out):
    def arrived(block):
        for late in (r_in, p_in, f_in):
            late.ready(block)

    def ready(block):
        for out in (w_out, g_out, u_out):
            out.send(block)

    prepare(a_ref, r_in.ref, p_in.ref, f_in.ref, y_ref, w_out.ref, g_out.ref, u_out.ref, arrived, ready)


def prepare_zero_kernel(a_ref, r_in, p_in, f_in, y_ref, g_out, u_out):
    def arrived(block):
        for late in (r_in, p_in, f_in):
            late.ready(block)

    def ready(block):
        g_out.send(block)
        u_out.send(block)

    prepare(a_ref, r_in.ref, p_in.ref, f_in.ref, y_ref, None, g_out.ref, u_out.ref, arrived, ready)


def waves_kernel(box_x, box_y, rows_ref, wave_ref, cs_ref):
    own = rows_ref[...]
    x, y, z = own[0:1] * (1.0 / box_x), own[1:2] * (1.0 / box_y), own[2:3] * (1.0 / DEPTH_Z)
    turns = jnp.concatenate([x, y, z, jnp.zeros((5, ATOMS), F32)], 0)
    turns = turns - jnp.floor(turns)
    high = turns.astype(BF16).astype(F32)
    middle = (turns - high).astype(BF16).astype(F32)
    low = turns - high - middle
    parts = jnp.concatenate([high, middle, low, jnp.zeros((8, ATOMS), F32)], 0).astype(BF16)
    wave = wave_ref[...]
    wave = jnp.concatenate([wave, wave, wave, jnp.zeros((8, K), F32)], 0).astype(BF16)
    cs_ref[:, :K] = dot(parts, wave, TN)

    def tile(t, carry):
        cols = pl.ds(pl.multiple_of(t * 128, 128), 128)
        phase = cs_ref[:, cols]
        quarter = jnp.floor(4.0 * phase + 0.5)
        angle = (phase - 0.25 * quarter) * (2.0 * math.pi)
        sq = angle * angle
        sin = angle * (1.0 + sq * (-1.0 / 6 + sq * (1.0 / 120 + sq * (-1.0 / 5040 + sq * (1.0 / 362880)))))
        cos = 1.0 + sq * (-0.5 + sq * (1.0 / 24 + sq * (-1.0 / 720 + sq * (1.0 / 40320 - sq * (1.0 / 3628800)))))
        turn = quarter.astype(jnp.int32) & 3
        odd = (turn & 1) == 1
        c = jnp.where(odd, sin, cos)
        s = jnp.where(odd, cos, sin)
        c = jnp.where((turn == 1) | (turn == 2), -c, c)
        s = jnp.where(turn >= 2, -s, s)
        cs_ref[:, cols] = c
        cs_ref[:, pl.ds(pl.multiple_of(K + t * 128, 128), 128)] = s
        return carry

    lax.fori_loop(0, K // 128, tile, 0)


def feature_strip_kernel(h_ref, a_in, b_in, iy_ref, part_ref, ya_ref, yb_ref):
    part = received(a_in, b_in, 32)
    part_ref[...] = part
    send_rows(pick(jnp.concatenate([h_ref[...], part], 1), iy_ref[...]), 48, 64, ya_ref, yb_ref)


def second_kernel(
    h_ref, part_ref, a_in, b_in, nb_ref, y_ref, r_ref, cs_ref, mix_ref,
    w_charge_ref, geo_ref, a_zero_ref, f_out, a_out, h2_out, charge_out, s_ref, ypart_ref,
):
    f_ref, a_ref, h2_ref, charge_ref = f_out.ref, a_out.ref, h2_out.ref, charge_out.ref
    ypart_ref[...] = received(a_in, b_in, 64)

    def get_f(r0):
        rows = pl.ds(r0, 16)
        tables = [h_ref[rows, :], part_ref[rows, :], ypart_ref[rows, :]]

        def state(n):
            nb = jnp.broadcast_to(nb_ref[n : n + 1, :], (16, 128))
            f = take_lanes(tables, nb & 127, nb >> 7)
            f_ref[rows, n * 128 : (n + 1) * 128] = f.astype(BF16)
            return f

        return state

    aggregate(r_ref, get_f, y_ref, a_ref)
    f_out.send()
    a_out.send()
    h_two = h_ref[...] + dot(mix_ref[1], invariants(a_ref))
    h2_ref[...] = h_two
    charge = dot(w_charge_ref[...], h_two.astype(BF16))
    charge_ref[...] = charge
    h2_out.send()
    charge_out.send()
    q_hi, q_lo = split(charge)
    q_both = jnp.concatenate([q_hi, q_lo], 0)
    for t in range(TILES // 2):
        c_hi, c_lo = split(cs_ref[:, t * 256 : (t + 1) * 256])
        both = dot(q_both, c_hi)
        part = both[:KC] + (both[KC:] + dot(q_hi, c_lo))
        s_ref[2 * t * KC : (2 * t + 1) * KC, :] = part[:, :128]
        s_ref[(2 * t + 1) * KC : (2 * t + 2) * KC, :] = part[:, 128:]


def prepare(a_ref, r_ref, p_ref, f_ref, y_ref, w_ref, g_ref, u_ref, arrived=lambda block: None, ready=lambda block: None):
    count = NB // BLOCKS

    def block_of(block):
        def body(cc, carry):
            r0 = pl.multiple_of(cc * 16, 16)
            rows = pl.ds(r0, 16)
            late = [pl.ds(pl.multiple_of(l * 128 + r0, 16), 16) for l in range(3)]
            a = [a_ref[k, rows, :] for k in range(9)]
            for n in range(block * count, (block + 1) * count):
                cols = slice(n * 128, (n + 1) * 128)
                y = [2.0 * y_ref[m, n : n + 1, :] for m in range(8)]
                f = f_ref[rows, cols].astype(F32)
                r = [r_ref[late[l], cols].astype(F32) for l in range(3)]
                q1 = a[1] * y[0] + a[2] * y[1] + a[3] * y[2]
                q2 = a[4] * y[3] + a[5] * y[4] + a[6] * y[5] + a[7] * y[6] + a[8] * y[7]
                g_ref[late[0], cols] = (f * r[1]).astype(BF16)
                g_ref[late[1], cols] = (f * r[2]).astype(BF16)
                u_ref[late[0], cols] = (f * p_ref[late[0], cols].astype(F32)).astype(BF16)
                u_ref[late[1], cols] = (f * q1 * p_ref[late[1], cols].astype(F32)).astype(BF16)
                u_ref[late[2], cols] = (f * q2 * p_ref[late[2], cols].astype(F32)).astype(BF16)
                if w_ref is not None:
                    w_ref[late[0], cols] = r_ref[late[0], cols]
                    w_ref[late[1], cols] = (q1 * r[1]).astype(BF16)
                    w_ref[late[2], cols] = (q2 * r[2]).astype(BF16)
            return carry

        lax.fori_loop(0, 8, body, 0)

    for block in range(BLOCKS):
        arrived(block)
        block_of(block)
        ready(block)


TOGETHER = 3


def backward(ginv_ref, ga_ref, w_ref, g_ref, u_ref, gf_ref, t_ref, arrived=lambda block: None):
    def body(b, carry):
        acc = [[jnp.zeros((8, 128), F32) for _ in range(9)] for _ in range(TOGETHER)]
        for cc in range(8):
            rows = slice(cc * 16, cc * 16 + 16)
            late = [slice(l * 128 + cc * 16, l * 128 + cc * 16 + 16) for l in range(3)]
            gi = [ginv_ref[late[l], :] for l in range(3)]
            ga = [ga_ref[k, rows, :] for k in range(8)]
            for j in range(TOGETHER):
                cols = pl.ds(pl.multiple_of((b * TOGETHER + j) * 128, 128), 128)
                if gf_ref is not None:
                    w = [w_ref[late[l], cols].astype(F32) for l in range(3)]
                    gf_ref[rows, cols] = (gi[0] * w[0] + gi[1] * w[1] + gi[2] * w[2]).astype(BF16)
                u = [u_ref[late[l], cols].astype(F32) for l in range(3)]
                g1, g2 = g_ref[late[0], cols].astype(F32), g_ref[late[1], cols].astype(F32)
                terms = [gi[0] * u[0] + gi[1] * u[1] + gi[2] * u[2]]
                terms += [g1 * ga[m] for m in range(3)] + [g2 * ga[m] for m in range(3, 8)]
                acc[j] = [old + (new[:8] + new[8:]) for old, new in zip(acc[j], terms)]
        for j in range(TOGETHER):
            for k in range(9):
                t_ref[k, pl.ds(b * TOGETHER + j, 1), :] = jnp.sum(acc[j][k], 0, keepdims=True)
        return carry

    count = NB // TOGETHER // BLOCKS
    for block in range(BLOCKS):
        arrived(block)
        lax.fori_loop(block * count, (block + 1) * count, body, 0)


def pull_invariants(g_inv, a_ref, ginv_ref, ga_ref):
    ginv_ref[...] = g_inv
    for k in range(1, 4):
        ga_ref[k - 1] = 2.0 * a_ref[k] * g_inv[C : 2 * C]
    for k in range(4, 9):
        ga_ref[k - 1] = 2.0 * a_ref[k] * g_inv[2 * C :]


def fill_onehot(nb_ref, oh_ref):
    for n in range(NB):
        oh_ref[:, n * 128 : (n + 1) * 128] = onehot_columns(nb_ref[n : n + 1, :], TABLE, BF16)


def ewald_kernel(
    box_x, box_y, scale, s_own_ref, s_other_ref, spectral_ref, cs_ref, wave_ref, charge_ref, h_in, h2_in, a_in, w_in, g_in, u_in,
    oh_in, mix_in, first_in, last_in, read_hidden_in, w_charge_in,
    energy_ref, gpos_ref, gown_ref, gpart_ref, ya_ref, yb_ref, t_ref, ginv_ref, ga_ref, gf_ref, gphase_ref,
):
    charge = charge_ref[...]
    qt_hi, qt_lo = split(charge.T)
    q_three = jnp.concatenate([qt_hi.astype(F32), qt_lo.astype(F32), qt_hi.astype(F32)], 1).astype(BF16)
    total = jnp.zeros((2 * KC, 2 * ATOMS), F32)
    core = lax.axis_index("co")

    def structure(t):
        half = t // 8 * 4 + t % 4
        rows = slice(half * KC, (half + 1) * KC)
        return jnp.where(core == t // 4 % 2, s_own_ref[rows, :], s_other_ref[rows, :])

    for t in range(TILES // 2):
        cols = slice(t * 128, (t + 1) * 128)
        late = slice(K + t * 128, K + (t + 1) * 128)
        filt = spectral_ref[:, cols] * scale
        gc = filt * structure(t)
        gs = filt * structure(TILES // 2 + t)
        cos, sin = cs_ref[:, cols], cs_ref[:, late]
        g_hi, g_lo = split(jnp.concatenate([gc, gs], 1))
        c_hi, c_lo = split(jnp.concatenate([cos, sin], 1))
        total = total + dot(jnp.concatenate([g_hi, g_lo], 0), jnp.concatenate([c_hi, c_lo], 0), NT)
        phase = dot(q_three, jnp.concatenate([g_hi, g_hi, g_lo], 0))
        p_hi, p_lo = split(phase[:, 128:] * cos - phase[:, :128] * sin)
        gphase_ref[:ATOMS, cols] = p_hi
        gphase_ref[ATOMS:, cols] = p_lo
    potential = total[:KC, :ATOMS] + (total[KC:, :ATOMS] + total[:KC, ATOMS:])
    wave = jnp.concatenate([wave_ref[...].astype(F32), jnp.zeros((5, K), F32)], 0).astype(BF16)
    gpos = dot(wave, gphase_ref[...], NT)
    gpos = gpos[:, :ATOMS] + gpos[:, ATOMS:]
    gpos_ref[...] = jnp.concatenate(
        [
            gpos[0:1] * (2.0 * math.pi / box_x),
            gpos[1:2] * (2.0 * math.pi / box_y),
            gpos[2:3] * (2.0 * math.pi / DEPTH_Z),
            jnp.zeros((5, ATOMS), F32),
        ],
        0,
    )
    h_ref, h2_ref, first_ref, last_ref = h_in.ready(), h2_in.ready(), first_in.ready(), last_in.ready()
    read_hidden_ref, w_charge_ref, mix_ref = read_hidden_in.ready(), w_charge_in.ready(), mix_in.ready()
    h_two = h2_ref[...].astype(BF16)
    z = dot(read_hidden_ref[...], h_two)
    s, hidden = gate(z)
    last = jnp.broadcast_to(last_ref[...], (128, last_ref.shape[1])).T
    first = jnp.broadcast_to(first_ref[...], (128, 128)).T
    site = jnp.sum(first * h_ref[...], 0, keepdims=True) + jnp.sum(last * hidden, 0, keepdims=True)
    energy_ref[...] = site + 0.5 * jnp.sum(charge * potential, 0, keepdims=True)
    g_hidden = (last * gate_slope(z, s)).astype(BF16)
    g_two = dot(w_charge_ref[...], potential.astype(BF16), TN) + dot(read_hidden_ref[...], g_hidden, TN)
    g_two = g_two.astype(BF16)
    g_inv = dot(mix_ref[1], g_two, TN).astype(BF16).astype(F32)
    pull_invariants(g_inv, a_in.ready(), ginv_ref, ga_ref)

    def arrived(block):
        for late in (w_in, g_in, u_in):
            late.ready(block)

    backward(ginv_ref, ga_ref, w_in.ref, g_in.ref, u_in.ref, gf_ref, t_ref, arrived)
    oh_ref = oh_in.ready()
    grads = dot(gf_ref[...], oh_ref[...], NT)
    gown_ref[...] = grads[:, :128] + g_two.astype(F32) + first
    gpart_ref[...] = grads[:, 128:256]
    send_rows(grads[:, 256:], 48, 64, ya_ref, yb_ref)


def return_features_kernel(gown_ref, gpart_ref, a_in, b_in, iy_ref, own_ref, xa_ref, xb_ref):
    back = give_back(received(a_in, b_in, 64), iy_ref[...], 256)
    own_ref[...] = gown_ref[...] + back[:, :128]
    send_rows(gpart_ref[...] + back[:, 128:], 32, 32, xa_ref, xb_ref)


def return_y_kernel(gown_ref, gpart_ref, a_in, b_in, iy_ref, own_ref, part_ref):
    back = give_back(merge(a_in[...], b_in[...], 64), iy_ref[...], 256)
    own_ref[...] = gown_ref[...] + back[:, :128]
    part_ref[...] = gpart_ref[...] + back[:, 128:]


def last_kernel(
    gown_ref, a_in, b_in, ix_ref, mix_ref, a_ref, g_ref, u_ref, t1_ref, geo_ref, oh_ref, gpos_ref,
    own_ref, part_ref, gy_ref, ginv_ref, ga_ref, t_ref, rows_ref,
):
    g_one = gown_ref[...] + give_back(received(a_in, b_in, 32), ix_ref[...], 128)
    g_inv = dot(mix_ref[0], g_one.astype(BF16), TN).astype(BF16).astype(F32)
    pull_invariants(g_inv, a_ref, ginv_ref, ga_ref)
    backward(ginv_ref, ga_ref, None, g_ref, u_ref, None, t_ref)
    t = [t_ref[k] + t1_ref[k] for k in range(9)]
    ux, uy, uz = geo_ref[0], geo_ref[1], geo_ref[2]
    root = 2.0 / ROOT_THREE
    gx = t[1] + t[4] * uy + t[6] * uz + ux * (2.0 * t[7] - root * t[8])
    gy = t[2] + t[4] * ux + t[5] * uz - uy * (2.0 * t[7] + root * t[8])
    gz = t[3] + t[5] * uy + t[6] * ux + (2.0 * root) * uz * t[8]
    steps = [g * (1.0 / CUTOFF) + (2.0 * CUTOFF) * u * t[0] for g, u in ((gx, ux), (gy, uy), (gz, uz))]
    rows_ref[...] = jnp.zeros(rows_ref.shape, F32)
    for k in range(3):
        high = steps[k].astype(BF16).astype(F32)
        low = steps[k] - high
        for n in range(NB):
            rows_ref[k : k + 1, n * 128 : (n + 1) * 128] = high[n : n + 1]
            rows_ref[8 + k : 9 + k, n * 128 : (n + 1) * 128] = low[n : n + 1]
    both = dot(rows_ref[...].astype(BF16), oh_ref[...], NT)
    grads = both[:8] + both[8:]
    centre = jnp.concatenate([jnp.sum(g, 0, keepdims=True) for g in steps] + [jnp.zeros((5, 128), F32)], 0)
    own_ref[...] = grads[:, :128] - centre + gpos_ref[...]
    part_ref[...] = grads[:, 128:256]
    gy_ref[...] = grads[:, 256:]


def final_kernel(own_ref, a_in, b_in, ix_ref, out_ref):
    total = own_ref[...] + give_back(merge(a_in[...], b_in[...], 32), ix_ref[...], 128)
    out_ref[...] = -total[:3]


def sum_kernel(pieces, copies, in_ref, out_ref):
    out_ref = getattr(out_ref, "ref", out_ref)
    rows = in_ref.shape[0] // pieces
    total = in_ref[0:rows, :]
    for g in range(1, pieces):
        total = total + in_ref[g * rows : (g + 1) * rows, :]
    for g in range(copies):
        out_ref[g * rows : (g + 1) * rows, :] = total


class Far:
    def __init__(self, array, late=False, blocks=1):
        self.array = array
        self.late = late
        self.blocks = blocks


class Late:
    def __init__(self, copies, ref):
        self.copies = copies
        self.ref = ref

    def ready(self, block=0):
        self.copies[block].wait()
        return self.ref


class Out:
    def __init__(self, copies, ref):
        self.copies = copies
        self.ref = ref
        self.sent = set()

    def send(self, block=0):
        self.copies[block].start()
        self.sent.add(block)

    def finish(self):
        for block in range(len(self.copies)):
            if block not in self.sent:
                self.send(block)


def column_copies(source, target, blocks, sems):
    if blocks == 1:
        return [pltpu.make_async_copy(source, target, next(sems))]
    width = source.shape[1] // blocks
    cols = [pl.ds(b * width, width) for b in range(blocks)]
    return [pltpu.make_async_copy(source.at[:, c], target.at[:, c], next(sems)) for c in cols]


def call(kernel, outs, *operands, scratch=(), flops=0, moved=0):
    n_in, n_out = len(operands), len(outs)
    far_in = [i for i, o in enumerate(operands) if isinstance(o, Far)]
    far_out = [i for i, o in enumerate(outs) if len(o) in (3, 5)]
    forwarded = [i for i, o in enumerate(outs) if len(o) == 4]
    arrays = [pltpu.with_memory_space_constraint(o.array, pltpu.HBM) if isinstance(o, Far) else o for o in operands]
    n_far = len(far_in) + len(far_out)
    n_sems = sum(operands[i].blocks for i in far_in) + BLOCKS * len(far_out) + len(forwarded)
    buffers = [pltpu.VMEM(arrays[i].shape, arrays[i].dtype) for i in far_in]
    buffers += [pltpu.VMEM(outs[i][0], outs[i][1]) for i in far_out]

    def wrapped(*refs):
        ins, results, rest = list(refs[:n_in]), list(refs[n_in : n_in + n_out]), refs[n_in + n_out :]
        own, held = rest[: len(scratch)], rest[len(scratch) : len(scratch) + n_far]
        sems = rest[-1]
        waits, later, sent = [], [], []
        sem = (sems.at[k] for k in range(n_sems))
        for k, i in enumerate(far_in):
            copies = column_copies(ins[i], held[k], operands[i].blocks, sem)
            if operands[i].late:
                big = len(copies) == 1 and math.prod(held[k].shape) > 10**6
                later += [(BLOCKS if big else b, copy) for b, copy in enumerate(copies)]
                ins[i] = Late(copies, held[k])
            else:
                copies[0].start()
                waits.append(copies[0])
                ins[i] = held[k]
        for _, copy in sorted(later, key=lambda item: item[0]):
            copy.start()
        for k, i in enumerate(far_out, len(far_in)):
            blocks = outs[i][4] if len(outs[i]) == 5 else 1
            results[i] = Out(column_copies(held[k], results[i], blocks, sem), held[k])
            sent.append(results[i])
        for copy in waits:
            copy.wait()
        for i in forwarded:
            out = Out(column_copies(ins[outs[i][3]], results[i], 1, sem), None)
            out.send()
            sent.append(out)
        kernel(*ins, *[r for i, r in enumerate(results) if i not in forwarded], *own)
        for out in sent:
            out.finish()
        for out in sent:
            for copy in out.copies:
                copy.wait()

    def place_of(far):
        return pl.BlockSpec(memory_space=pltpu.HBM if far else pltpu.VMEM)

    return pl.pallas_call(
        wrapped,
        out_shape=[pltpu.HBM(o[0], o[1]) if len(o) > 2 else jax.ShapeDtypeStruct(o[0], o[1]) for o in outs],
        in_specs=[place_of(isinstance(o, Far)) for o in operands],
        out_specs=[place_of(len(o) > 2) for o in outs],
        scratch_shapes=[pltpu.VMEM(s, d) for s, d in scratch] + buffers + [pltpu.SemaphoreType.DMA((max(n_sems, 1),))],
        compiler_params=pltpu.CompilerParams(vmem_limit_bytes=24 * 1024 * 1024),
        cost_estimate=pl.CostEstimate(flops=flops, bytes_accessed=moved, transcendentals=0),
    )(*arrays)


def swap(value, axes, of):
    count = 1
    for axis in axes:
        count *= lax.axis_size(axis)
    return lax.ppermute(value, axes, [(i, of(i)) for i in range(count)])


BX = ("xh", "co")
CELL = ("y", "z", "xl")


def swap_x(a, b):
    return swap(a, BX, lambda i: i ^ 1), swap(b, BX, lambda i: i ^ 3)


def swap_y(a, b):
    def other(c):
        return (c - 1) % 64 if c % 2 == 0 else (c + 1) % 64

    return swap(a, CELL, lambda c: c ^ 1), swap(b, CELL, other)


def body(
    positions, species, send_x, send_y, neighbours, live_slots, embedding, radial_in, radial_mid, radial_out, mixing,
    read_first, read_hidden, read_last, w_charge, spectral, wave_ids,
):
    count_x = lax.axis_size("xh") * lax.axis_size("co")
    count_y = lax.axis_size("y") * lax.axis_size("z") * lax.axis_size("xl")
    box_x = count_x * WIDTH_X
    box_y = count_y * WIDTH_Y
    scale = 1.0 / math.sqrt(K * ATOMS * count_x * count_y)
    small = ((8, 128), F32)
    square = ((C, 128), F32)
    edge3 = ((3 * C, EDGES), BF16)
    index = ((1, 128), jnp.int32)
    strip_32, strip_48 = ((32, 128), F32), ((48, 128), F32)
    w1, w3, emb = radial_in.swapaxes(1, 2).astype(F32), radial_out.swapaxes(1, 2), embedding.T.astype(F32)

    with_box = functools.partial

    rows, ix, strip = call(strip_x_kernel, [small, index, small], Far(positions), Far(species[None]), Far(send_x))
    xa, xb = swap_x(strip, strip)
    nb, live, emb, *near_nets, mix_near, wave, send_near = call(
        fetch_kernel,
        [((NB, 128), jnp.int32), ((NB, 128), F32), ((8, C), F32), (w1.shape, F32), (radial_mid.shape, BF16), (radial_out.shape, BF16), (mixing.shape, BF16), ((8, K), F32), (send_y.shape, jnp.int32)],
        Far(neighbours), Far(live_slots), emb, w1, Far(radial_mid), Far(w3), Far(mixing), Far(wave_ids), Far(send_y), flops=10**8, moved=10**6,
    )
    xa, xb, nb, live, emb, near_nets, mix_near, wave, send_near = lax.optimization_barrier(
        (xa, xb, nb, live, emb, near_nets, mix_near, wave, send_near)
    )
    part, iy, strip = call(strip_y_kernel, [small, index, small], rows, xa, xb, send_near)
    ya, yb = swap_y(strip, strip)
    nets = (Far(w1), Far(radial_mid), Far(w3))
    ylm_shape, a_shape, cs_shape = ((8, NB, 128), F32), ((9, C, 128), F32), ((ATOMS, 2 * K), F32)
    geo, ylm, f_zero, r_zero, a_zero, h_one, xa, xb = call(
        with_box(first_kernel, box_x, box_y),
        [ylm_shape, ylm_shape, ((C, EDGES), BF16, True), edge3 + (True,), a_shape, square, strip_32, strip_32],
        rows, part, ya, yb, nb, live, ix, emb, *near_nets, mix_near,
    )
    rows_later, _, _ = lax.optimization_barrier((rows, xa, xb))
    xa, xb = swap_x(xa, xb)
    (cs,) = call(with_box(waves_kernel, box_x, box_y), [cs_shape], rows_later, wave, flops=10**8, moved=10**6)
    xa, xb, cs = lax.optimization_barrier((xa, xb, cs))
    fpart, ya, yb = call(feature_strip_kernel, [square, strip_48, strip_48], h_one, xa, xb, iy)
    geo_soon, _, _ = lax.optimization_barrier((geo, ya, yb))
    ya, yb = swap_y(ya, yb)
    (r_one,) = call(radial_kernel, [edge3], geo_soon, *near_nets, flops=5 * 10**8, moved=10**7)
    f_one, a_one, h_two, charge, s_part, h_far, ylm, r_far, cs, geo, a_zero = call(
        second_kernel,
        [
            ((C, EDGES), BF16, True), a_shape + (True,), square + (True,), ((KC, ATOMS), F32, True), ((TILES * KC, 128), F32),
            square + (True, 0), ylm_shape + (True, 5), edge3 + (True, 6), cs_shape + (True, 7), ylm_shape + (True, 10),
            a_shape + (True, 11),
        ],
        h_one, fpart, ya, yb, nb, ylm, r_one, cs, mix_near, w_charge, geo, a_zero,
        scratch=[square],
    )
    late = lambda array: Far(array, True)
    edge2 = ((2 * C, EDGES), BF16)
    blocked = (True, None, BLOCKS)
    geo_later, _ = lax.optimization_barrier((geo, s_part))
    p_one, p_zero, oh = call(
        slope_kernel, [edge3 + (True,), edge3 + (True,), ((TABLE, EDGES), BF16, True)], Far(geo_later), *nets, Far(nb), flops=10**9, moved=2 * 10**7
    )
    rows_each = s_part.shape[0] // NWIDE
    pieces = lax.all_to_all(s_part, WIDE, 0, 0, tiled=True)
    pieces, p_one, p_zero, oh = lax.optimization_barrier((pieces, p_one, p_zero, oh))
    (mine,) = call(functools.partial(sum_kernel, NWIDE, 8), [((8 * rows_each, 128), F32)], pieces)
    a_later, _ = lax.optimization_barrier((a_zero, mine))
    g_zero, u_zero = call(
        prepare_zero_kernel, [edge2 + blocked, edge3 + blocked],
        Far(a_later), Far(r_zero, True, BLOCKS), Far(p_zero, True, BLOCKS), Far(f_zero, True, BLOCKS), Far(ylm), flops=10**9, moved=2 * 10**7,
    )
    mine = lax.all_to_all(mine, ("z",), 0, 0, tiled=True)
    mine, g_zero, u_zero = lax.optimization_barrier((mine, g_zero, u_zero))
    (spread,) = call(functools.partial(sum_kernel, 8, NWIDE // 2), [((NWIDE // 2 * rows_each, 128), F32, True)], mine)
    a_later, _ = lax.optimization_barrier((a_one, spread))
    w_one, g_one, u_one = call(
        prepare_one_kernel, [edge3 + blocked, edge2 + blocked, edge3 + blocked],
        Far(a_later), Far(r_far, True, BLOCKS), Far(p_one, True, BLOCKS), Far(f_one, True, BLOCKS), Far(ylm), flops=10**9, moved=2 * 10**7,
    )
    s_own = lax.all_to_all(spread, ("xh", "y", "xl"), 0, 0, tiled=True)
    s_own, w_one, g_one, u_one = lax.optimization_barrier((s_own, w_one, g_one, u_one))
    s_other = swap(s_own, ("co",), lambda i: i ^ 1)
    energy, gpos, gown, gpart, ya, yb, t_one = call(
        with_box(ewald_kernel, box_x, box_y, scale),
        [((1, 128), F32), small, square, square, strip_48, strip_48, ((9, NB, 128), F32)],
        s_own, s_other, Far(spectral), Far(cs), Far(wave_ids), Far(charge), late(h_far), late(h_two), late(a_one),
        Far(w_one, True, BLOCKS), Far(g_one, True, BLOCKS), Far(u_one, True, BLOCKS), late(oh), late(mixing), late(read_first[None]), late(read_last[None]), late(read_hidden),
        late(w_charge),
        scratch=[((3 * C, 128), F32), ((8, C, 128), F32), ((C, EDGES), BF16), ((2 * ATOMS, K), BF16)],
    )
    ya, yb = swap_y(ya, yb)
    gown, xa, xb = call(return_features_kernel, [square, strip_32, strip_32], gown, gpart, ya, yb, iy)
    xa, xb = swap_x(xa, xb)
    own, part, gy = call(
        last_kernel,
        [small, small, small],
        gown, xa, xb, ix, mixing, a_zero, g_zero, u_zero, t_one, geo, oh, gpos,
        scratch=[((3 * C, 128), F32), ((8, C, 128), F32), ((9, NB, 128), F32), ((16, EDGES), F32)],
    )
    ya, yb = swap_y(gy, gy)
    own, part = call(return_y_kernel, [small, small], own, part, ya, yb, iy)
    xa, xb = swap_x(part, part)
    (forces,) = call(final_kernel, [((3, ATOMS), F32)], own, xa, xb, ix)
    return energy[0], forces


def solution(mesh):
    fine = Mesh(mesh.devices.reshape(2, 2, 4, 8, 2), AXES)
    rows, columns = P(AXES), P(None, AXES)
    placed = (columns, rows) + (columns,) * 4 + (P(),) * 11
    return jax.shard_map(body, mesh=fine, in_specs=placed, out_specs=(rows, columns), check_vma=False)
```

```python
import functools
import math

import jax
import jax.numpy as jnp
from jax import lax
from jax.experimental import pallas as pl
from jax.experimental.pallas import tpu as pltpu
from jax.sharding import Mesh, PartitionSpec as P

CUTOFF = 4.0
SOFTEN = 0.25
WIDTH_X = 16.0
WIDTH_Y = 16.0
DEPTH_Z = 16.0
ACT_GAIN = 1.679
ROOT_THREE = math.sqrt(3.0)
HIGHEST = lax.Precision.HIGHEST
F32 = jnp.float32
BF16 = jnp.bfloat16

C = 128
NB = 24
ATOMS = 128
EDGES = NB * ATOMS
TABLE = 384
NBASIS = 8
BLOCKS = 4
K = 1024
KC = 64
TILES = 2 * K // 128
AXES = ("xh", "co", "y", "z", "xl")
WIDE = ("xh", "co", "y", "xl")
NWIDE = 32

NN = (((1,), (0,)), ((), ()))
NT = (((1,), (1,)), ((), ()))
TN = (((0,), (0,)), ((), ()))


def dot(a, b, dims=NN, precision=None):
    return lax.dot_general(a, b, dims, precision=precision, preferred_element_type=F32)


def split(a):
    high = a.astype(BF16)
    return high, (a - high.astype(F32)).astype(BF16)


def dot3(a, b, dims=NN):
    a_hi, a_lo = split(a)
    b_hi, b_lo = split(b)
    return dot(a_hi, b_hi, dims) + (dot(a_lo, b_hi, dims) + dot(a_hi, b_lo, dims))


def gate(v):
    s = 0.5 + 0.5 * jnp.tanh(0.5 * v)
    return s, (ACT_GAIN * v) * s


def gate_slope(v, s):
    return ACT_GAIN * s * (1.0 + v * (1.0 - s))


def onehot_columns(index_row, count, dtype):
    rows = lax.broadcasted_iota(jnp.int32, (count, index_row.shape[1]), 0)
    return (rows == index_row).astype(F32).astype(dtype)


def merge(a, b, split_lane):
    lane = lax.broadcasted_iota(jnp.int32, a.shape, 1)
    return jnp.where(lane < split_lane, a, b)


def pick(values, index_row):
    return dot(values, onehot_columns(index_row, values.shape[1], F32), NN, HIGHEST)


def give_back(grads, index_row, count):
    return dot(grads, onehot_columns(index_row, count, F32), NT, HIGHEST)


def send_rows(values, count, gap, a_ref, b_ref):
    rows = values.T
    a_ref[...] = rows[:count]
    b_ref[...] = rows[gap : gap + count]


def received(a_ref, b_ref, gap):
    a, b = a_ref[...], b_ref[...]
    pieces = [a, b, jnp.zeros((128 - gap - b.shape[0], 128), F32)]
    if gap > a.shape[0]:
        pieces.insert(1, jnp.zeros((gap - a.shape[0], 128), F32))
    return jnp.concatenate(pieces, 0).T


def place(index):
    px, py = lax.axis_index("co"), lax.axis_index("xl")
    far = jnp.where(index < 240, index + (128 - 64 * py), index + (16 + 64 * py))
    near = jnp.where(index < 160, index + (32 - 32 * px), index + (32 * px - 32))
    return jnp.where(index < 128, index, jnp.where(index < 192, near, far))


def strip_x_kernel(pos_ref, species_ref, send_ref, rows_ref, ix_ref, out_ref):
    odd = lax.axis_index("co")
    lower, upper = send_ref[0:1, :], send_ref[1:2, :]
    first = upper + (lower - upper) * odd
    second = lower + (upper - lower) * odd
    index = jnp.concatenate([first, second, jnp.full((1, 64), -1, jnp.int32)], 1)
    rows = jnp.concatenate([pos_ref[...], species_ref[...].astype(F32), jnp.zeros((4, ATOMS), F32)], 0)
    ix_ref[...] = index
    rows_ref[...] = rows
    out_ref[...] = pick(rows, index)


def strip_y_kernel(rows_ref, a_ref, b_ref, send_ref, part_ref, iy_ref, out_ref):
    odd = lax.axis_index("xl")
    send = place(send_ref[...])
    lower, upper = send[0:1], send[1:2]
    first = upper + (lower - upper) * odd
    second = lower + (upper - lower) * odd
    none = jnp.full((1, 16), -1, jnp.int32)
    index = jnp.concatenate([first, none, second, none], 1)
    part = merge(a_ref[...], b_ref[...], 32)
    part_ref[...] = part
    iy_ref[...] = index
    out_ref[...] = pick(jnp.concatenate([rows_ref[...], part], 1), index)


WIDE_TILE = 1024


def flat(ref, k, g):
    count = WIDE_TILE // 128
    return jnp.concatenate([ref[k, count * g + j : count * g + j + 1, :] for j in range(count)], 1)


def radial(layer, geo_ref, w1_ref, w2_ref, w3_ref, r_ref, p_ref):
    w1 = w1_ref[layer].astype(BF16)
    w2 = w2_ref[layer]
    w3 = w3_ref[layer]
    if w3.shape[0] < w3.shape[1]:
        w3 = w3.astype(F32).T.astype(BF16)
    spacing = CUTOFF / (NBASIS - 1)
    centre = lax.broadcasted_iota(jnp.int32, (NBASIS, WIDE_TILE), 0).astype(F32) * spacing
    for g in range(EDGES // WIDE_TILE):
        cols = slice(g * WIDE_TILE, (g + 1) * WIDE_TILE)
        gap = (flat(geo_ref, 3, g) - centre) * (1.0 / spacing)
        basis = jnp.exp(-gap * gap)
        z1 = dot(w1, basis.astype(BF16), TN)
        s1, h1 = gate(z1)
        z2 = dot(w2, h1.astype(BF16))
        s2, h2 = gate(z2)
        if r_ref is not None:
            r_ref[:, cols] = dot(w3, (h2 * flat(geo_ref, 4, g)).astype(BF16)).astype(BF16)
        if p_ref is not None:
            slope = basis * gap * (-2.0 / spacing)
            h1p = gate_slope(z1, s1) * dot(w1, slope.astype(BF16), TN)
            h2p = gate_slope(z2, s2) * dot(w2, h1p.astype(BF16))
            mixed = h2p * flat(geo_ref, 6, g) + h2 * flat(geo_ref, 5, g)
            p_ref[:, cols] = dot(w3, mixed.astype(BF16)).astype(BF16)


def aggregate(r_ref, get_f, y_ref, a_ref):
    def body(cc, carry):
        r0 = pl.multiple_of(cc * 16, 16)
        acc = [jnp.zeros((16, 128), F32) for _ in range(9)]
        state = get_f(r0)
        for n in range(NB):
            cols = slice(n * 128, (n + 1) * 128)
            f = state(n)
            g0 = r_ref[pl.ds(r0, 16), cols].astype(F32) * f
            g1 = r_ref[pl.ds(128 + r0, 16), cols].astype(F32) * f
            g2 = r_ref[pl.ds(256 + r0, 16), cols].astype(F32) * f
            acc[0] = acc[0] + g0
            for m in range(3):
                acc[1 + m] = acc[1 + m] + g1 * y_ref[m, n : n + 1, :]
            for m in range(5):
                acc[4 + m] = acc[4 + m] + g2 * y_ref[3 + m, n : n + 1, :]
        for k in range(9):
            a_ref[k, pl.ds(r0, 16), :] = acc[k]
        return carry

    lax.fori_loop(0, 8, body, 0)


def invariants(a_ref):
    a1 = a_ref[1] * a_ref[1] + a_ref[2] * a_ref[2] + a_ref[3] * a_ref[3]
    a2 = a_ref[4] * a_ref[4] + a_ref[5] * a_ref[5] + a_ref[6] * a_ref[6]
    a2 = a2 + a_ref[7] * a_ref[7] + a_ref[8] * a_ref[8]
    return jnp.concatenate([a_ref[0].astype(BF16), a1.astype(BF16), a2.astype(BF16)], 0)


def take_lanes(tables, lane, group):
    got = [jnp.take_along_axis(t, lane, axis=1, mode="promise_in_bounds") for t in tables]
    return jnp.where(group == 0, got[0], jnp.where(group == 1, got[1], got[2]))


def fetch_kernel(nb_ref, live_ref, emb_ref, w1_ref, w2_ref, w3_ref, mix_ref, wave_ref, send_ref, nb_out, live_out, emb_out, w1_out, w2_out, w3_out, mix_out, wave_out, send_out):
    send_out[...] = send_ref[...]
    wave_out[...] = jnp.concatenate([wave_ref[...].astype(F32), jnp.zeros((5, K), F32)], 0)
    nb_out[...] = place(nb_ref[...])
    live_out[...] = live_ref[...].astype(F32)
    emb_out[...] = jnp.concatenate([emb_ref[...], jnp.zeros((8 - emb_ref.shape[0], C), F32)], 0)
    w1_out[...] = w1_ref[...]
    w2_out[...] = w2_ref[...]
    mix_out[...] = mix_ref[...]
    for layer in range(2):
        w3_out[layer] = w3_ref[layer].astype(F32).T.astype(BF16)


def first_kernel(
    box_x, box_y, rows_ref, part_ref, a_in, b_in, nb_ref, live_ref, ix_ref, emb_ref, w1_ref, w2_ref,
    w3_ref, mix_ref, geo_ref, y_ref, f_out, r_out, a_ref, h_ref, xa_ref, xb_ref,
):
    f_ref, r_ref = f_out.ref, r_out.ref
    own = rows_ref[...]
    tables = [own, part_ref[...], merge(a_in[...], b_in[...], 64)]
    nb = nb_ref[...]
    lane, group = nb & 127, nb >> 7

    def gathered(row):
        return jnp.concatenate(
            [
                take_lanes(
                    [jnp.broadcast_to(t[row : row + 1], (8, 128)) for t in tables],
                    lane[8 * b : 8 * b + 8],
                    group[8 * b : 8 * b + 8],
                )
                for b in range(NB // 8)
            ],
            0,
        )

    off_x = gathered(0) - own[0:1]
    off_y = gathered(1) - own[1:2]
    step_z = gathered(2) - own[2:3]
    step_x = off_x - box_x * jnp.floor(off_x * (1.0 / box_x) + 0.5)
    step_y = off_y - box_y * jnp.floor(off_y * (1.0 / box_y) + 0.5)
    square = step_x * step_x + step_y * step_y + step_z * step_z
    shifted = square + SOFTEN
    inverse = lax.rsqrt(shifted)
    live = live_ref[...]
    inside = jnp.maximum(1.0 - square * (1.0 / (CUTOFF * CUTOFF)), 0.0)
    env = inside * inside * live
    ux, uy, uz = step_x * (1.0 / CUTOFF), step_y * (1.0 / CUTOFF), step_z * (1.0 / CUTOFF)
    geo_ref[0] = ux
    geo_ref[1] = uy
    geo_ref[2] = uz
    geo_ref[3] = jnp.sqrt(shifted)
    geo_ref[4] = env
    geo_ref[5] = inside * live * (-2.0 / (CUTOFF * CUTOFF))
    geo_ref[6] = 0.5 * env * inverse
    y_ref[0] = ux
    y_ref[1] = uy
    y_ref[2] = uz
    y_ref[3] = ux * uy
    y_ref[4] = uy * uz
    y_ref[5] = uz * ux
    y_ref[6] = ux * ux - uy * uy
    y_ref[7] = (2.0 * uz * uz - ux * ux - uy * uy) * (1.0 / ROOT_THREE)

    geo_ref[7] = gathered(3)
    emb = emb_ref[...].astype(BF16)
    kinds = lax.broadcasted_iota(jnp.int32, (8, WIDE_TILE), 0).astype(F32)
    for g in range(EDGES // WIDE_TILE):
        cols = slice(g * WIDE_TILE, (g + 1) * WIDE_TILE)
        f_ref[:, cols] = dot(emb, (kinds == flat(geo_ref, 7, g)).astype(F32).astype(BF16), TN).astype(BF16)
    f_out.send()
    radial(0, geo_ref, w1_ref, w2_ref, w3_ref, r_ref, None)
    r_out.send()

    def get_f(r0):
        return lambda n: f_ref[pl.ds(r0, 16), n * 128 : (n + 1) * 128].astype(F32)

    aggregate(r_ref, get_f, y_ref, a_ref)
    h_zero = dot(emb, (kinds[:, :128] == own[3:4]).astype(F32).astype(BF16), TN)
    h_one = h_zero + dot(mix_ref[0], invariants(a_ref))
    h_ref[...] = h_one
    send_rows(pick(h_one, ix_ref[...]), 32, 32, xa_ref, xb_ref)


def radial_kernel(geo_ref, w1_ref, w2_ref, w3_ref, r_ref):
    radial(1, geo_ref, w1_ref, w2_ref, w3_ref, r_ref, None)


def slope_kernel(geo_ref, w1_ref, w2_ref, w3_ref, nb_ref, p_out, p_zero_out, oh_out):
    radial(1, geo_ref, w1_ref, w2_ref, w3_ref, None, p_out.ref)
    p_out.send()
    radial(0, geo_ref, w1_ref, w2_ref, w3_ref, None, p_zero_out.ref)
    p_zero_out.send()
    fill_onehot(nb_ref, oh_out.ref)


def prepare_one_kernel(a_ref, r_in, p_in, f_in, y_ref, w_out, g_out, u_out):
    def arrived(block):
        for late in (r_in, p_in, f_in):
            late.ready(block)

    def ready(block):
        for out in (w_out, g_out, u_out):
            out.send(block)

    prepare(a_ref, r_in.ref, p_in.ref, f_in.ref, y_ref, w_out.ref, g_out.ref, u_out.ref, arrived, ready)


def prepare_zero_kernel(a_ref, r_in, p_in, f_in, y_ref, g_out, u_out):
    def arrived(block):
        for late in (r_in, p_in, f_in):
            late.ready(block)

    def ready(block):
        g_out.send(block)
        u_out.send(block)

    prepare(a_ref, r_in.ref, p_in.ref, f_in.ref, y_ref, None, g_out.ref, u_out.ref, arrived, ready)


def waves_kernel(box_x, box_y, rows_ref, wave_ref, cs_ref):
    own = rows_ref[...]
    x, y, z = own[0:1] * (1.0 / box_x), own[1:2] * (1.0 / box_y), own[2:3] * (1.0 / DEPTH_Z)
    turns = jnp.concatenate([x, y, z, jnp.zeros((5, ATOMS), F32)], 0)
    turns = turns - jnp.floor(turns)
    high = turns.astype(BF16).astype(F32)
    middle = (turns - high).astype(BF16).astype(F32)
    low = turns - high - middle
    parts = jnp.concatenate([high, middle, low, jnp.zeros((8, ATOMS), F32)], 0).astype(BF16)
    wave = wave_ref[...]
    wave = jnp.concatenate([wave, wave, wave, jnp.zeros((8, K), F32)], 0).astype(BF16)
    cs_ref[:, :K] = dot(parts, wave, TN)

    def tile(t, carry):
        cols = pl.ds(pl.multiple_of(t * 128, 128), 128)
        phase = cs_ref[:, cols]
        quarter = jnp.floor(4.0 * phase + 0.5)
        angle = (phase - 0.25 * quarter) * (2.0 * math.pi)
        sq = angle * angle
        sin = angle * (1.0 + sq * (-1.0 / 6 + sq * (1.0 / 120 + sq * (-1.0 / 5040 + sq * (1.0 / 362880)))))
        cos = 1.0 + sq * (-0.5 + sq * (1.0 / 24 + sq * (-1.0 / 720 + sq * (1.0 / 40320 - sq * (1.0 / 3628800)))))
        turn = quarter.astype(jnp.int32) & 3
        odd = (turn & 1) == 1
        c = jnp.where(odd, sin, cos)
        s = jnp.where(odd, cos, sin)
        c = jnp.where((turn == 1) | (turn == 2), -c, c)
        s = jnp.where(turn >= 2, -s, s)
        cs_ref[:, cols] = c
        cs_ref[:, pl.ds(pl.multiple_of(K + t * 128, 128), 128)] = s
        return carry

    lax.fori_loop(0, K // 128, tile, 0)


def feature_strip_kernel(h_ref, a_in, b_in, iy_ref, part_ref, ya_ref, yb_ref):
    part = received(a_in, b_in, 32)
    part_ref[...] = part
    send_rows(pick(jnp.concatenate([h_ref[...], part], 1), iy_ref[...]), 48, 64, ya_ref, yb_ref)


def second_kernel(
    h_ref, part_ref, a_in, b_in, nb_ref, y_ref, r_ref, cs_ref, mix_ref,
    w_charge_ref, geo_ref, a_zero_ref, f_out, a_out, h2_out, charge_out, s_ref, ypart_ref, lane_ref, group_ref,
):
    lane_ref[...] = nb_ref[...] & 127
    group_ref[...] = nb_ref[...] >> 7
    f_ref, a_ref, h2_ref, charge_ref = f_out.ref, a_out.ref, h2_out.ref, charge_out.ref
    ypart_ref[...] = received(a_in, b_in, 64)

    def get_f(r0):
        rows = pl.ds(r0, 16)
        tables = [h_ref[rows, :], part_ref[rows, :], ypart_ref[rows, :]]

        def state(n):
            lane = jnp.broadcast_to(lane_ref[n : n + 1, :], (8, 128))
            group = jnp.broadcast_to(group_ref[n : n + 1, :], (8, 128))
            f = jnp.concatenate([take_lanes([t[half : half + 8] for t in tables], lane, group) for half in (0, 8)], 0)
            f_ref[rows, n * 128 : (n + 1) * 128] = f.astype(BF16)
            return f

        return state

    aggregate(r_ref, get_f, y_ref, a_ref)
    f_out.send()
    a_out.send()
    h_two = h_ref[...] + dot(mix_ref[1], invariants(a_ref))
    h2_ref[...] = h_two
    charge = dot(w_charge_ref[...], h_two.astype(BF16))
    charge_ref[...] = charge
    h2_out.send()
    charge_out.send()
    q_hi, q_lo = split(charge)
    q_both = jnp.concatenate([q_hi, q_lo], 0)
    for t in range(TILES // 2):
        c_hi, c_lo = split(cs_ref[:, t * 256 : (t + 1) * 256])
        both = dot(q_both, c_hi)
        part = both[:KC] + (both[KC:] + dot(q_hi, c_lo))
        s_ref[2 * t * KC : (2 * t + 1) * KC, :] = part[:, :128]
        s_ref[(2 * t + 1) * KC : (2 * t + 2) * KC, :] = part[:, 128:]


def prepare(a_ref, r_ref, p_ref, f_ref, y_ref, w_ref, g_ref, u_ref, arrived=lambda block: None, ready=lambda block: None):
    count = NB // BLOCKS

    def block_of(block):
        def body(cc, carry):
            r0 = pl.multiple_of(cc * 16, 16)
            rows = pl.ds(r0, 16)
            late = [pl.ds(pl.multiple_of(l * 128 + r0, 16), 16) for l in range(3)]
            a = [a_ref[k, rows, :] for k in range(9)]
            for n in range(block * count, (block + 1) * count):
                cols = slice(n * 128, (n + 1) * 128)
                y = [2.0 * y_ref[m, n : n + 1, :] for m in range(8)]
                f = f_ref[rows, cols].astype(F32)
                r = [r_ref[late[l], cols].astype(F32) for l in range(3)]
                q1 = a[1] * y[0] + a[2] * y[1] + a[3] * y[2]
                q2 = a[4] * y[3] + a[5] * y[4] + a[6] * y[5] + a[7] * y[6] + a[8] * y[7]
                g_ref[late[0], cols] = (f * r[1]).astype(BF16)
                g_ref[late[1], cols] = (f * r[2]).astype(BF16)
                u_ref[late[0], cols] = (f * p_ref[late[0], cols].astype(F32)).astype(BF16)
                u_ref[late[1], cols] = (f * q1 * p_ref[late[1], cols].astype(F32)).astype(BF16)
                u_ref[late[2], cols] = (f * q2 * p_ref[late[2], cols].astype(F32)).astype(BF16)
                if w_ref is not None:
                    w_ref[late[0], cols] = r_ref[late[0], cols]
                    w_ref[late[1], cols] = (q1 * r[1]).astype(BF16)
                    w_ref[late[2], cols] = (q2 * r[2]).astype(BF16)
            return carry

        lax.fori_loop(0, 8, body, 0)

    for block in range(BLOCKS):
        arrived(block)
        block_of(block)
        ready(block)


TOGETHER = 3


def backward(ginv_ref, ga_ref, w_ref, g_ref, u_ref, gf_ref, t_ref, arrived=lambda block: None):
    def body(b, carry):
        acc = [[jnp.zeros((8, 128), F32) for _ in range(9)] for _ in range(TOGETHER)]
        for cc in range(8):
            rows = slice(cc * 16, cc * 16 + 16)
            late = [slice(l * 128 + cc * 16, l * 128 + cc * 16 + 16) for l in range(3)]
            gi = [ginv_ref[late[l], :] for l in range(3)]
            ga = [ga_ref[k, rows, :] for k in range(8)]
            for j in range(TOGETHER):
                cols = pl.ds(pl.multiple_of((b * TOGETHER + j) * 128, 128), 128)
                if gf_ref is not None:
                    w = [w_ref[late[l], cols].astype(F32) for l in range(3)]
                    gf_ref[rows, cols] = (gi[0] * w[0] + gi[1] * w[1] + gi[2] * w[2]).astype(BF16)
                u = [u_ref[late[l], cols].astype(F32) for l in range(3)]
                g1, g2 = g_ref[late[0], cols].astype(F32), g_ref[late[1], cols].astype(F32)
                terms = [gi[0] * u[0] + gi[1] * u[1] + gi[2] * u[2]]
                terms += [g1 * ga[m] for m in range(3)] + [g2 * ga[m] for m in range(3, 8)]
                acc[j] = [old + (new[:8] + new[8:]) for old, new in zip(acc[j], terms)]
        for j in range(TOGETHER):
            for k in range(9):
                t_ref[k, pl.ds(b * TOGETHER + j, 1), :] = jnp.sum(acc[j][k], 0, keepdims=True)
        return carry

    count = NB // TOGETHER // BLOCKS
    for block in range(BLOCKS):
        arrived(block)
        lax.fori_loop(block * count, (block + 1) * count, body, 0)


def pull_invariants(g_inv, a_ref, ginv_ref, ga_ref):
    ginv_ref[...] = g_inv
    for k in range(1, 4):
        ga_ref[k - 1] = 2.0 * a_ref[k] * g_inv[C : 2 * C]
    for k in range(4, 9):
        ga_ref[k - 1] = 2.0 * a_ref[k] * g_inv[2 * C :]


def fill_onehot(nb_ref, oh_ref):
    for n in range(NB):
        oh_ref[:, n * 128 : (n + 1) * 128] = onehot_columns(nb_ref[n : n + 1, :], TABLE, BF16)


def ewald_kernel(
    box_x, box_y, scale, s_own_ref, s_other_ref, spectral_ref, cs_ref, wave_ref, charge_ref, h_in, h2_in, a_in, w_in, g_in, u_in,
    oh_in, mix_in, first_in, last_in, read_hidden_in, w_charge_in,
    energy_ref, gpos_ref, gown_ref, gpart_ref, ya_ref, yb_ref, t_ref, ginv_ref, ga_ref, gf_ref, gphase_ref,
):
    charge = charge_ref[...]
    qt_hi, qt_lo = split(charge.T)
    q_three = jnp.concatenate([qt_hi.astype(F32), qt_lo.astype(F32), qt_hi.astype(F32)], 1).astype(BF16)
    total = jnp.zeros((2 * KC, 2 * ATOMS), F32)
    core = lax.axis_index("co")

    def structure(t):
        half = t // 8 * 4 + t % 4
        rows = slice(half * KC, (half + 1) * KC)
        return jnp.where(core == t // 4 % 2, s_own_ref[rows, :], s_other_ref[rows, :])

    for t in range(TILES // 2):
        cols = slice(t * 128, (t + 1) * 128)
        late = slice(K + t * 128, K + (t + 1) * 128)
        filt = spectral_ref[:, cols] * scale
        gc = filt * structure(t)
        gs = filt * structure(TILES // 2 + t)
        cos, sin = cs_ref[:, cols], cs_ref[:, late]
        g_hi, g_lo = split(jnp.concatenate([gc, gs], 1))
        c_hi, c_lo = split(jnp.concatenate([cos, sin], 1))
        total = total + dot(jnp.concatenate([g_hi, g_lo], 0), jnp.concatenate([c_hi, c_lo], 0), NT)
        phase = dot(q_three, jnp.concatenate([g_hi, g_hi, g_lo], 0))
        p_hi, p_lo = split(phase[:, 128:] * cos - phase[:, :128] * sin)
        gphase_ref[:ATOMS, cols] = p_hi
        gphase_ref[ATOMS:, cols] = p_lo
    potential = total[:KC, :ATOMS] + (total[KC:, :ATOMS] + total[:KC, ATOMS:])
    wave = jnp.concatenate([wave_ref[...].astype(F32), jnp.zeros((5, K), F32)], 0).astype(BF16)
    gpos = dot(wave, gphase_ref[...], NT)
    gpos = gpos[:, :ATOMS] + gpos[:, ATOMS:]
    gpos_ref[...] = jnp.concatenate(
        [
            gpos[0:1] * (2.0 * math.pi / box_x),
            gpos[1:2] * (2.0 * math.pi / box_y),
            gpos[2:3] * (2.0 * math.pi / DEPTH_Z),
            jnp.zeros((5, ATOMS), F32),
        ],
        0,
    )
    h_ref, h2_ref, first_ref, last_ref = h_in.ready(), h2_in.ready(), first_in.ready(), last_in.ready()
    read_hidden_ref, w_charge_ref, mix_ref = read_hidden_in.ready(), w_charge_in.ready(), mix_in.ready()
    h_two = h2_ref[...].astype(BF16)
    z = dot(read_hidden_ref[...], h_two)
    s, hidden = gate(z)
    last = jnp.broadcast_to(last_ref[...], (128, last_ref.shape[1])).T
    first = jnp.broadcast_to(first_ref[...], (128, 128)).T
    site = jnp.sum(first * h_ref[...], 0, keepdims=True) + jnp.sum(last * hidden, 0, keepdims=True)
    energy_ref[...] = site + 0.5 * jnp.sum(charge * potential, 0, keepdims=True)
    g_hidden = (last * gate_slope(z, s)).astype(BF16)
    g_two = dot(w_charge_ref[...], potential.astype(BF16), TN) + dot(read_hidden_ref[...], g_hidden, TN)
    g_two = g_two.astype(BF16)
    g_inv = dot(mix_ref[1], g_two, TN).astype(BF16).astype(F32)
    pull_invariants(g_inv, a_in.ready(), ginv_ref, ga_ref)

    def arrived(block):
        for late in (w_in, g_in, u_in):
            late.ready(block)

    backward(ginv_ref, ga_ref, w_in.ref, g_in.ref, u_in.ref, gf_ref, t_ref, arrived)
    oh_ref = oh_in.ready()
    grads = dot(gf_ref[...], oh_ref[...], NT)
    gown_ref[...] = grads[:, :128] + g_two.astype(F32) + first
    gpart_ref[...] = grads[:, 128:256]
    send_rows(grads[:, 256:], 48, 64, ya_ref, yb_ref)


def return_features_kernel(gown_ref, gpart_ref, a_in, b_in, iy_ref, own_ref, xa_ref, xb_ref):
    back = give_back(received(a_in, b_in, 64), iy_ref[...], 256)
    own_ref[...] = gown_ref[...] + back[:, :128]
    send_rows(gpart_ref[...] + back[:, 128:], 32, 32, xa_ref, xb_ref)


def return_y_kernel(gown_ref, gpart_ref, a_in, b_in, iy_ref, own_ref, part_ref):
    back = give_back(merge(a_in[...], b_in[...], 64), iy_ref[...], 256)
    own_ref[...] = gown_ref[...] + back[:, :128]
    part_ref[...] = gpart_ref[...] + back[:, 128:]


def last_kernel(
    gown_ref, a_in, b_in, ix_ref, mix_ref, a_ref, g_ref, u_ref, t1_ref, geo_ref, oh_ref, gpos_ref,
    own_ref, part_ref, gy_ref, ginv_ref, ga_ref, t_ref, rows_ref,
):
    g_one = gown_ref[...] + give_back(received(a_in, b_in, 32), ix_ref[...], 128)
    g_inv = dot(mix_ref[0], g_one.astype(BF16), TN).astype(BF16).astype(F32)
    pull_invariants(g_inv, a_ref, ginv_ref, ga_ref)
    backward(ginv_ref, ga_ref, None, g_ref, u_ref, None, t_ref)
    t = [t_ref[k] + t1_ref[k] for k in range(9)]
    ux, uy, uz = geo_ref[0], geo_ref[1], geo_ref[2]
    root = 2.0 / ROOT_THREE
    gx = t[1] + t[4] * uy + t[6] * uz + ux * (2.0 * t[7] - root * t[8])
    gy = t[2] + t[4] * ux + t[5] * uz - uy * (2.0 * t[7] + root * t[8])
    gz = t[3] + t[5] * uy + t[6] * ux + (2.0 * root) * uz * t[8]
    steps = [g * (1.0 / CUTOFF) + (2.0 * CUTOFF) * u * t[0] for g, u in ((gx, ux), (gy, uy), (gz, uz))]
    rows_ref[...] = jnp.zeros(rows_ref.shape, F32)
    for k in range(3):
        high = steps[k].astype(BF16).astype(F32)
        low = steps[k] - high
        for n in range(NB):
            rows_ref[k : k + 1, n * 128 : (n + 1) * 128] = high[n : n + 1]
            rows_ref[8 + k : 9 + k, n * 128 : (n + 1) * 128] = low[n : n + 1]
    both = dot(rows_ref[...].astype(BF16), oh_ref[...], NT)
    grads = both[:8] + both[8:]
    centre = jnp.concatenate([jnp.sum(g, 0, keepdims=True) for g in steps] + [jnp.zeros((5, 128), F32)], 0)
    own_ref[...] = grads[:, :128] - centre + gpos_ref[...]
    part_ref[...] = grads[:, 128:256]
    gy_ref[...] = grads[:, 256:]


def final_kernel(own_ref, a_in, b_in, ix_ref, out_ref):
    total = own_ref[...] + give_back(merge(a_in[...], b_in[...], 32), ix_ref[...], 128)
    out_ref[...] = -total[:3]


def sum_kernel(pieces, copies, in_ref, out_ref):
    out_ref = getattr(out_ref, "ref", out_ref)
    rows = in_ref.shape[0] // pieces
    total = in_ref[0:rows, :]
    for g in range(1, pieces):
        total = total + in_ref[g * rows : (g + 1) * rows, :]
    for g in range(copies):
        out_ref[g * rows : (g + 1) * rows, :] = total


class Far:
    def __init__(self, array, late=False, blocks=1):
        self.array = array
        self.late = late
        self.blocks = blocks


class Late:
    def __init__(self, copies, ref):
        self.copies = copies
        self.ref = ref

    def ready(self, block=0):
        self.copies[block].wait()
        return self.ref


class Out:
    def __init__(self, copies, ref):
        self.copies = copies
        self.ref = ref
        self.sent = set()

    def send(self, block=0):
        self.copies[block].start()
        self.sent.add(block)

    def finish(self):
        for block in range(len(self.copies)):
            if block not in self.sent:
                self.send(block)


def column_copies(source, target, blocks, sems):
    if blocks == 1:
        return [pltpu.make_async_copy(source, target, next(sems))]
    width = source.shape[1] // blocks
    cols = [pl.ds(b * width, width) for b in range(blocks)]
    return [pltpu.make_async_copy(source.at[:, c], target.at[:, c], next(sems)) for c in cols]


def call(kernel, outs, *operands, scratch=(), flops=0, moved=0):
    n_in, n_out = len(operands), len(outs)
    far_in = [i for i, o in enumerate(operands) if isinstance(o, Far)]
    far_out = [i for i, o in enumerate(outs) if len(o) in (3, 5)]
    forwarded = [i for i, o in enumerate(outs) if len(o) == 4]
    arrays = [pltpu.with_memory_space_constraint(o.array, pltpu.HBM) if isinstance(o, Far) else o for o in operands]
    n_far = len(far_in) + len(far_out)
    n_sems = sum(operands[i].blocks for i in far_in) + BLOCKS * len(far_out) + len(forwarded)
    buffers = [pltpu.VMEM(arrays[i].shape, arrays[i].dtype) for i in far_in]
    buffers += [pltpu.VMEM(outs[i][0], outs[i][1]) for i in far_out]

    def wrapped(*refs):
        ins, results, rest = list(refs[:n_in]), list(refs[n_in : n_in + n_out]), refs[n_in + n_out :]
        own, held = rest[: len(scratch)], rest[len(scratch) : len(scratch) + n_far]
        sems = rest[-1]
        waits, later, sent = [], [], []
        sem = (sems.at[k] for k in range(n_sems))
        for k, i in enumerate(far_in):
            copies = column_copies(ins[i], held[k], operands[i].blocks, sem)
            if operands[i].late:
                big = len(copies) == 1 and math.prod(held[k].shape) > 10**6
                later += [(BLOCKS if big else b, copy) for b, copy in enumerate(copies)]
                ins[i] = Late(copies, held[k])
            else:
                copies[0].start()
                waits.append(copies[0])
                ins[i] = held[k]
        for _, copy in sorted(later, key=lambda item: item[0]):
            copy.start()
        for k, i in enumerate(far_out, len(far_in)):
            blocks = outs[i][4] if len(outs[i]) == 5 else 1
            results[i] = Out(column_copies(held[k], results[i], blocks, sem), held[k])
            sent.append(results[i])
        for copy in waits:
            copy.wait()
        for i in forwarded:
            out = Out(column_copies(ins[outs[i][3]], results[i], 1, sem), None)
            out.send()
            sent.append(out)
        kernel(*ins, *[r for i, r in enumerate(results) if i not in forwarded], *own)
        for out in sent:
            out.finish()
        for out in sent:
            for copy in out.copies:
                copy.wait()

    def place_of(far):
        return pl.BlockSpec(memory_space=pltpu.HBM if far else pltpu.VMEM)

    return pl.pallas_call(
        wrapped,
        out_shape=[pltpu.HBM(o[0], o[1]) if len(o) > 2 else jax.ShapeDtypeStruct(o[0], o[1]) for o in outs],
        in_specs=[place_of(isinstance(o, Far)) for o in operands],
        out_specs=[place_of(len(o) > 2) for o in outs],
        scratch_shapes=[pltpu.VMEM(s, d) for s, d in scratch] + buffers + [pltpu.SemaphoreType.DMA((max(n_sems, 1),))],
        compiler_params=pltpu.CompilerParams(vmem_limit_bytes=24 * 1024 * 1024),
        cost_estimate=pl.CostEstimate(flops=flops, bytes_accessed=moved, transcendentals=0),
    )(*arrays)


def swap(value, axes, of):
    count = 1
    for axis in axes:
        count *= lax.axis_size(axis)
    return lax.ppermute(value, axes, [(i, of(i)) for i in range(count)])


BX = ("xh", "co")
CELL = ("y", "z", "xl")


def swap_x(a, b):
    return swap(a, BX, lambda i: i ^ 1), swap(b, BX, lambda i: i ^ 3)


def swap_y(a, b):
    def other(c):
        return (c - 1) % 64 if c % 2 == 0 else (c + 1) % 64

    return swap(a, CELL, lambda c: c ^ 1), swap(b, CELL, other)


def body(
    positions, species, send_x, send_y, neighbours, live_slots, embedding, radial_in, radial_mid, radial_out, mixing,
    read_first, read_hidden, read_last, w_charge, spectral, wave_ids,
):
    count_x = lax.axis_size("xh") * lax.axis_size("co")
    count_y = lax.axis_size("y") * lax.axis_size("z") * lax.axis_size("xl")
    box_x = count_x * WIDTH_X
    box_y = count_y * WIDTH_Y
    scale = 1.0 / math.sqrt(K * ATOMS * count_x * count_y)
    small = ((8, 128), F32)
    square = ((C, 128), F32)
    edge3 = ((3 * C, EDGES), BF16)
    index = ((1, 128), jnp.int32)
    strip_32, strip_48 = ((32, 128), F32), ((48, 128), F32)
    w1, w3, emb = radial_in.swapaxes(1, 2).astype(F32), radial_out.swapaxes(1, 2), embedding.T.astype(F32)

    with_box = functools.partial

    rows, ix, strip = call(strip_x_kernel, [small, index, small], Far(positions), Far(species[None]), Far(send_x))
    xa, xb = swap_x(strip, strip)
    nb, live, emb, *near_nets, mix_near, wave, send_near = call(
        fetch_kernel,
        [((NB, 128), jnp.int32), ((NB, 128), F32), ((8, C), F32), (w1.shape, F32), (radial_mid.shape, BF16), (radial_out.shape, BF16), (mixing.shape, BF16), ((8, K), F32), (send_y.shape, jnp.int32)],
        Far(neighbours), Far(live_slots), emb, w1, Far(radial_mid), Far(w3), Far(mixing), Far(wave_ids), Far(send_y), flops=10**8, moved=10**6,
    )
    xa, xb, nb, live, emb, near_nets, mix_near, wave, send_near = lax.optimization_barrier(
        (xa, xb, nb, live, emb, near_nets, mix_near, wave, send_near)
    )
    part, iy, strip = call(strip_y_kernel, [small, index, small], rows, xa, xb, send_near)
    ya, yb = swap_y(strip, strip)
    nets = (Far(w1), Far(radial_mid), Far(w3))
    ylm_shape, a_shape, cs_shape = ((8, NB, 128), F32), ((9, C, 128), F32), ((ATOMS, 2 * K), F32)
    geo, ylm, f_zero, r_zero, a_zero, h_one, xa, xb = call(
        with_box(first_kernel, box_x, box_y),
        [ylm_shape, ylm_shape, ((C, EDGES), BF16, True), edge3 + (True,), a_shape, square, strip_32, strip_32],
        rows, part, ya, yb, nb, live, ix, emb, *near_nets, mix_near,
    )
    rows_later, _, _ = lax.optimization_barrier((rows, xa, xb))
    xa, xb = swap_x(xa, xb)
    (cs,) = call(with_box(waves_kernel, box_x, box_y), [cs_shape], rows_later, wave, flops=10**8, moved=10**6)
    xa, xb, cs = lax.optimization_barrier((xa, xb, cs))
    fpart, ya, yb = call(feature_strip_kernel, [square, strip_48, strip_48], h_one, xa, xb, iy)
    geo_soon, _, _ = lax.optimization_barrier((geo, ya, yb))
    ya, yb = swap_y(ya, yb)
    (r_one,) = call(radial_kernel, [edge3], geo_soon, *near_nets, flops=5 * 10**8, moved=10**7)
    f_one, a_one, h_two, charge, s_part, h_far, ylm, r_far, cs, geo, a_zero = call(
        second_kernel,
        [
            ((C, EDGES), BF16, True), a_shape + (True,), square + (True,), ((KC, ATOMS), F32, True), ((TILES * KC, 128), F32),
            square + (True, 0), ylm_shape + (True, 5), edge3 + (True, 6), cs_shape + (True, 7), ylm_shape + (True, 10),
            a_shape + (True, 11),
        ],
        h_one, fpart, ya, yb, nb, ylm, r_one, cs, mix_near, w_charge, geo, a_zero,
        scratch=[square, ((NB, 128), jnp.int32), ((NB, 128), jnp.int32)],
    )
    late = lambda array: Far(array, True)
    edge2 = ((2 * C, EDGES), BF16)
    blocked = (True, None, BLOCKS)
    geo_later, _ = lax.optimization_barrier((geo, s_part))
    p_one, p_zero, oh = call(
        slope_kernel, [edge3 + (True,), edge3 + (True,), ((TABLE, EDGES), BF16, True)], Far(geo_later), *nets, Far(nb), flops=10**9, moved=2 * 10**7
    )
    rows_each = s_part.shape[0] // NWIDE
    pieces = lax.all_to_all(s_part, WIDE, 0, 0, tiled=True)
    pieces, p_one, p_zero, oh = lax.optimization_barrier((pieces, p_one, p_zero, oh))
    (mine,) = call(functools.partial(sum_kernel, NWIDE, 8), [((8 * rows_each, 128), F32)], pieces)
    a_later, _ = lax.optimization_barrier((a_zero, mine))
    g_zero, u_zero = call(
        prepare_zero_kernel, [edge2 + blocked, edge3 + blocked],
        Far(a_later), Far(r_zero, True, BLOCKS), Far(p_zero, True, BLOCKS), Far(f_zero, True, BLOCKS), Far(ylm), flops=10**9, moved=2 * 10**7,
    )
    mine = lax.all_to_all(mine, ("z",), 0, 0, tiled=True)
    mine, g_zero, u_zero = lax.optimization_barrier((mine, g_zero, u_zero))
    (spread,) = call(functools.partial(sum_kernel, 8, NWIDE // 2), [((NWIDE // 2 * rows_each, 128), F32, True)], mine)
    a_later, _ = lax.optimization_barrier((a_one, spread))
    w_one, g_one, u_one = call(
        prepare_one_kernel, [edge3 + blocked, edge2 + blocked, edge3 + blocked],
        Far(a_later), Far(r_far, True, BLOCKS), Far(p_one, True, BLOCKS), Far(f_one, True, BLOCKS), Far(ylm), flops=10**9, moved=2 * 10**7,
    )
    s_own = lax.all_to_all(spread, ("xh", "y", "xl"), 0, 0, tiled=True)
    s_own, w_one, g_one, u_one = lax.optimization_barrier((s_own, w_one, g_one, u_one))
    s_other = swap(s_own, ("co",), lambda i: i ^ 1)
    energy, gpos, gown, gpart, ya, yb, t_one = call(
        with_box(ewald_kernel, box_x, box_y, scale),
        [((1, 128), F32), small, square, square, strip_48, strip_48, ((9, NB, 128), F32)],
        s_own, s_other, Far(spectral), Far(cs), Far(wave_ids), Far(charge), late(h_far), late(h_two), late(a_one),
        Far(w_one, True, BLOCKS), Far(g_one, True, BLOCKS), Far(u_one, True, BLOCKS), late(oh), late(mixing), late(read_first[None]), late(read_last[None]), late(read_hidden),
        late(w_charge),
        scratch=[((3 * C, 128), F32), ((8, C, 128), F32), ((C, EDGES), BF16), ((2 * ATOMS, K), BF16)],
    )
    ya, yb = swap_y(ya, yb)
    gown, xa, xb = call(return_features_kernel, [square, strip_32, strip_32], gown, gpart, ya, yb, iy)
    xa, xb = swap_x(xa, xb)
    own, part, gy = call(
        last_kernel,
        [small, small, small],
        gown, xa, xb, ix, mixing, a_zero, g_zero, u_zero, t_one, geo, oh, gpos,
        scratch=[((3 * C, 128), F32), ((8, C, 128), F32), ((9, NB, 128), F32), ((16, EDGES), F32)],
    )
    ya, yb = swap_y(gy, gy)
    own, part = call(return_y_kernel, [small, small], own, part, ya, yb, iy)
    xa, xb = swap_x(part, part)
    (forces,) = call(final_kernel, [((3, ATOMS), F32)], own, xa, xb, ix)
    return energy[0], forces


def solution(mesh):
    fine = Mesh(mesh.devices.reshape(2, 2, 4, 8, 2), AXES)
    rows, columns = P(AXES), P(None, AXES)
    placed = (columns, rows) + (columns,) * 4 + (P(),) * 11
    return jax.shard_map(body, mesh=fine, in_specs=placed, out_specs=(rows, columns), check_vma=False)
```
